32 devices in a mesh: dp: 2 (over x), ctx: 16 (over z, y, core).
Axes of the slice: x: 2, y: 2, z: 4, core: 2. Of those that a mesh axis runs over, the one named last changes fastest.
Arguments:
- queries: bfloat16 [4, 1024, 2048], P('dp', 'ctx'), may hold values from -52 to 52
- key_rows: bfloat16 [4, 1024, 2048], P('dp', 'ctx'), may hold values from -4 to 4
- value_rows: bfloat16 [4, 1024, 2048], P('dp', 'ctx'), may hold values from -6 to 6
- out_grad: bfloat16 [4, 1024, 2048], P('dp', 'ctx'), may hold values from -64 to 64
- level_slope: float32 [16], replicated, may hold values from -0.5 to 0.5
Outputs:
- query_grad: bfloat16 [4, 1024, 2048], P('dp', 'ctx')
- key_grad: bfloat16 [4, 1024, 2048], P('dp', 'ctx')
- value_grad: bfloat16 [4, 1024, 2048], P('dp', 'ctx')
- slope_grad: float32 [16], replicated
The draws below stay inside these ranges and needn't reach their ends.
All inputs are finite; a program needn't handle non-finite values.
Results may differ from the reference program's by a relative error of at most 0.0075.
Values may be sent and summed in bfloat16 or wider, within the bound.
No kernel may reach another device: no remote copies, remote signals or barrier semaphores. Data moves between devices by JAX's collectives and lax.ppermute only.
A program may use at most 64 MiB of HBM per device.

```python
import math
import jax
import jax.numpy as jnp
from jax import lax

HEADS = 16
BLOCK = 64
HD = 2048
SEQ = 1024
BATCH = 4
N_CTX = 16


def base_keys(key):
    base = jax.random.normal(jax.random.fold_in(key, 11), (BATCH, SEQ, HD), jnp.float32)
    return jnp.clip(base, -4.0, 4.0)


def draw_key_rows(key, part):
    base = base_keys(key)
    return base.astype(jnp.bfloat16)


def draw_queries(key, part):
    drawn = 2.5 * jnp.clip(jax.random.normal(jax.random.fold_in(key, 12), (BATCH, SEQ, HD), jnp.float32), -6.0, 6.0)
    return drawn.astype(jnp.bfloat16)


def draw_out_grad(key, part):
    rows = jnp.arange(BATCH, dtype=jnp.float32)
    ramp = jnp.exp(math.log(3.0) * rows / max(BATCH - 1, 1))
    base = jnp.clip(jax.random.normal(jax.random.fold_in(key, 13), (BATCH, SEQ, HD), jnp.float32), -4.0, 4.0)
    return (4.0 * ramp[:, None, None] * base).astype(jnp.bfloat16)


def block_scale(own_key, dims, shards, least, top_value):
    factor_of, own = 1.0, jax.random.fold_in(own_key, 6)
    for position, shards_of in shards:
        draws = jnp.exp(jax.random.uniform(jax.random.fold_in(own, position), (shards_of,), jnp.float32, least / len(shards), top_value / len(shards)))
        factor_of = factor_of * jnp.repeat(draws, dims[position] // shards_of).reshape([-1 if axis == position else 1 for axis in range(len(dims))])
    return factor_of


def bell_draw(stream_key, extent, scale, reach, split=(), kind=jnp.bfloat16):
    values = scale * jax.random.normal(stream_key, extent, jnp.float32)
    if split:
        values = values * block_scale(stream_key, extent, split, -0.22, 0.18)
    return jnp.clip(values, -reach, reach).astype(kind)


def setup_inputs(seed: int = 0) -> dict:
    streams_of = jax.random.split(jax.random.key(seed), 6)
    queries = draw_queries(jax.random.fold_in(streams_of[5], 71), 0)
    key_rows = draw_key_rows(jax.random.fold_in(streams_of[5], 71), 0)
    value_rows = bell_draw(streams_of[2], (BATCH, SEQ, HD), 1.0, 6.0, ((0, 2), (1, 16)))
    out_grad = draw_out_grad(jax.random.fold_in(streams_of[5], 71), 0)
    level_slope = jnp.clip(jax.random.uniform(streams_of[4], (HEADS,), jnp.float32, -0.5, 0.5), -0.5, 0.5)
    return dict(queries=queries, key_rows=key_rows, value_rows=value_rows, out_grad=out_grad, level_slope=level_slope)


def pair_mean(cells):
    shaped = cells.reshape(cells.shape[:-2] + (cells.shape[-2] // 2, 2, cells.shape[-1])).astype(jnp.float32)
    return ((shaped[..., 0, :] + shaped[..., 1, :]) * 0.5).astype(jnp.bfloat16)

def product(form, left, right):
    return jnp.einsum(form, left.astype(jnp.float32), right.astype(jnp.float32), precision=lax.Precision.HIGHEST)

def attend(query_set, key_set, value_set, grad_set, level_slope):
    seqs, block, width = query_set.shape
    heads = level_slope.shape[0]
    head = width // heads
    key_count = key_set.shape[1]
    scale = 1.0 / math.sqrt(head)
    query_four = query_set.reshape(seqs, block, heads, head)
    key_four = key_set.reshape(seqs, key_count, heads, head)
    value_four = value_set.reshape(seqs, key_count, heads, head)
    grad_four = grad_set.reshape(seqs, block, heads, head)
    column = jnp.arange(key_count, dtype=jnp.int32)
    level_of = column // block - 1
    sibling = jnp.maximum(level_of, 0)
    multiple = jnp.where(level_of < 0, 1.0, jnp.exp2(sibling.astype(jnp.float32)))
    bias = level_slope[:, None] * sibling.astype(jnp.float32)[None, :]
    raw = product('sqhd,skhd->shqk', query_four, key_four)
    scores = raw * scale + bias[None, :, None, :]
    top = lax.optimization_barrier(jnp.max(scores, axis=-1, keepdims=True))
    weights = multiple[None, None, None, :] * jnp.exp(scores - top)
    probs = weights / lax.optimization_barrier(jnp.sum(weights, axis=-1, keepdims=True))
    probs_low = probs.astype(jnp.bfloat16)
    output = product('shqk,skhd->sqhd', probs_low, value_four)
    delta = jnp.transpose(lax.optimization_barrier(jnp.sum(grad_four.astype(jnp.float32) * output, axis=-1)), (0, 2, 1))
    upstream = product('sqhd,skhd->shqk', grad_four, value_four)
    dscore = probs * (upstream - delta[..., None])
    slope_part = lax.optimization_barrier(jnp.sum(dscore * sibling.astype(jnp.float32)[None, None, None, :], axis=(0, 2, 3)))
    dscore_low = dscore.astype(jnp.bfloat16)
    query_part = (product('shqk,skhd->sqhd', dscore_low, key_four) * scale).reshape(seqs, block, width)
    key_part = (product('shqk,sqhd->skhd', dscore_low, query_four) * scale).reshape(seqs, key_count, width)
    value_part = product('shqk,sqhd->skhd', probs_low, grad_four).reshape(seqs, key_count, width)
    return (query_part, key_part, value_part, slope_part)

def partner_of(sent, level, blocks):
    shaped = sent.reshape(blocks // 2 ** (level + 1), 2, 2 ** level, BLOCK, HD)
    return shaped[:, ::-1].reshape(blocks, BLOCK, HD)

def chain(direct, levels, blocks):
    grad_now = jnp.zeros((blocks, BLOCK, HD), jnp.float32)
    for level in reversed(range(levels)):
        spread = jnp.broadcast_to(grad_now[:, :, None, :], (blocks, BLOCK, 2, HD)).reshape(blocks, 2 * BLOCK, HD) * 0.5
        lower = spread[:, :BLOCK]
        upper = spread[:, BLOCK:]
        flag = (jnp.arange(blocks, dtype=jnp.int32) // 2 ** level % 2 == 1)[:, None, None]
        own_half = jnp.where(flag, upper, lower)
        other_half = jnp.where(flag, lower, upper)
        sent = (other_half + direct[:, (level + 1) * BLOCK:(level + 2) * BLOCK]).astype(jnp.bfloat16)
        grad_now = own_half + partner_of(sent, level, blocks).astype(jnp.float32)
    return (grad_now + direct[:, :BLOCK]).astype(jnp.bfloat16).reshape(SEQ, HD)

def one_sequence(query_seq, key_seq, value_seq, grad_seq, level_slope):
    blocks = N_CTX
    levels = N_CTX.bit_length() - 1
    query_blocks = query_seq.reshape(blocks, BLOCK, HD)
    grad_blocks = grad_seq.reshape(blocks, BLOCK, HD)
    keys_by_level = [key_seq.reshape(blocks, BLOCK, HD)]
    values_by_level = [value_seq.reshape(blocks, BLOCK, HD)]
    for level in range(levels - 1):
        keys_by_level.append(pair_mean(keys_by_level[-1].reshape(blocks >> level + 1, 2 * BLOCK, HD)))
        values_by_level.append(pair_mean(values_by_level[-1].reshape(blocks >> level + 1, 2 * BLOCK, HD)))

    def per_block(index):
        key_list = [lax.dynamic_index_in_dim(keys_by_level[0], index, 0, keepdims=False)]
        value_list = [lax.dynamic_index_in_dim(values_by_level[0], index, 0, keepdims=False)]
        for level in range(levels):
            group = index // 2 ** level
            partner = (group + 1 - 2 * (group % 2)).astype(jnp.int32)
            key_list.append(lax.dynamic_index_in_dim(keys_by_level[level], partner, 0, keepdims=False))
            value_list.append(lax.dynamic_index_in_dim(values_by_level[level], partner, 0, keepdims=False))
        key_set = jnp.concatenate(key_list, axis=0)[None]
        value_set = jnp.concatenate(value_list, axis=0)[None]
        query_set = lax.dynamic_index_in_dim(query_blocks, index, 0, keepdims=False)[None]
        grad_set = lax.dynamic_index_in_dim(grad_blocks, index, 0, keepdims=False)[None]
        query_part, key_part, value_part, slope_part = attend(query_set, key_set, value_set, grad_set, level_slope)
        return (query_part[0], key_part[0], value_part[0], slope_part)
    query_all, key_all, value_all, slope_all = lax.map(per_block, jnp.arange(blocks, dtype=jnp.int32))
    query_grad = query_all.astype(jnp.bfloat16).reshape(SEQ, HD)
    key_grad = chain(key_all, levels, blocks)
    value_grad = chain(value_all, levels, blocks)
    return (query_grad, key_grad, value_grad, lax.optimization_barrier(jnp.sum(slope_all, axis=0)))

def reference(queries, key_rows, value_rows, out_grad, level_slope):

    def run(items):
        return one_sequence(items[0], items[1], items[2], items[3], level_slope)
    query_grad, key_grad, value_grad, slope_terms = lax.map(run, (queries, key_rows, value_rows, out_grad))
    return (query_grad, key_grad, value_grad, lax.optimization_barrier(jnp.sum(slope_terms, axis=0)))
```

```python
import functools
import math

import jax
import jax.numpy as jnp
from jax import lax
from jax.experimental import pallas as pl
from jax.experimental.pallas import tpu as pltpu
from jax.sharding import PartitionSpec as P

F32, BF16 = jnp.float32, jnp.bfloat16
LOG2E = math.log2(math.e)
VMEM = pl.BlockSpec(memory_space=pltpu.VMEM)
SMEM = pl.BlockSpec(memory_space=pltpu.SMEM)


def swap(value, apart):
    count = lax.axis_size("ctx")
    return lax.ppermute(value, "ctx", [(source, source ^ apart) for source in range(count)])


def like(*shape, dtype=BF16):
    return jax.ShapeDtypeStruct(shape, dtype)


def call(body, out_shape, operands, scalars=0, flops=0, name=None):
    moved = sum(a.size * a.dtype.itemsize for a in jax.tree.leaves((operands, out_shape)))
    return pl.pallas_call(
        body,
        out_shape=out_shape,
        in_specs=[SMEM] * scalars + [VMEM] * (len(operands) - scalars),
        out_specs=jax.tree.map(lambda _: VMEM, out_shape),
        compiler_params=pltpu.CompilerParams(vmem_limit_bytes=32 * 2**20),
        cost_estimate=pl.CostEstimate(flops=flops, bytes_accessed=moved, transcendentals=0),
        name=name,
    )(*operands)


def dot(left, right, left_dim=1, right_dim=0):
    dims = (((left_dim,), (right_dim,)), ((), ()))
    return lax.dot_general(left, right, dims, preferred_element_type=F32)


def pair_matrix(rows):
    cell = lax.broadcasted_iota(jnp.int32, (rows, 2 * rows), 0)
    source = lax.broadcasted_iota(jnp.int32, (rows, 2 * rows), 1)
    return jnp.where(source // 2 == cell, 0.5, 0.0).astype(BF16)


def spread_matrix(rows, level):
    row = lax.broadcasted_iota(jnp.int32, (rows, rows >> level), 0)
    cell = lax.broadcasted_iota(jnp.int32, (rows, rows >> level), 1)
    return jnp.where(row >> level == cell, 0.5**level, 0.0).astype(BF16)


def split_body(core, k, v, q, g, kv_own, kv_send, qg_own, qg_send):
    half = kv_own.shape[-1]
    mine = pl.ds(pl.multiple_of(core[0] * half, half), half)
    theirs = pl.ds(pl.multiple_of((1 - core[0]) * half, half), half)
    for index, (first, second) in enumerate(((k, q), (v, g))):
        kv_own[index] = first[:, :, mine]
        kv_send[index] = first[:, :, theirs]
        qg_own[index] = second[:, :, mine]
        qg_send[index] = second[:, :, theirs]


def summary_body(own, other, *cells):
    for kind in range(own.shape[0]):
        for seq in range(own.shape[1]):
            rows = jnp.concatenate([own[kind, seq], other[kind, seq]], axis=0)
            for out in cells:
                rows = dot(pair_matrix(rows.shape[0] // 2), rows).astype(BF16)
                out[kind, seq] = rows


def coarser_body(cells, out):
    for kind in range(cells.shape[0]):
        for seq in range(cells.shape[1]):
            rows = cells[kind, seq]
            out[kind, seq] = dot(pair_matrix(rows.shape[0] // 2), rows).astype(BF16)


def attend_body(levels_of, head, core, slope, *refs):
    count = len(levels_of)
    qg_own, qg_other = refs[:2]
    pieces = refs[2 : 2 + count]
    dq_own, dq_send, slope_out = refs[2 + count : 5 + count]
    outs = refs[5 + count :]
    seqs, block, width = qg_own.shape[1:]
    heads = width // head
    scale = 1.0 / math.sqrt(head)
    sizes = [piece.shape[2] for piece in pieces]
    starts = [sum(sizes[:i]) for i in range(count + 1)]
    for h in range(heads):
        lanes = slice(h * head, (h + 1) * head)
        step = slope[core[0] * heads + h] * LOG2E + 1.0
        slope_sum = jnp.zeros((1, 2 * block), F32)
        for seq in range(seqs):
            query = jnp.concatenate([qg_own[0, seq, :, lanes], qg_other[0, seq, :, lanes]], axis=0)
            grad = jnp.concatenate([qg_own[1, seq, :, lanes], qg_other[1, seq, :, lanes]], axis=0)
            keys = jnp.concatenate([piece[0, seq, :, lanes] for piece in pieces], axis=0)
            values = jnp.concatenate([piece[1, seq, :, lanes] for piece in pieces], axis=0)
            raw = dot(keys, query, 1, 1)
            upstream = dot(values, grad, 1, 1)
            scores = jnp.concatenate(
                [
                    raw[starts[i] : starts[i + 1]] * (scale * LOG2E) + step * float(levels_of[i])
                    for i in range(count)
                ],
                axis=0,
            )
            weights = jnp.exp2(scores - jnp.max(scores, axis=0, keepdims=True))
            probs = weights * (1.0 / jnp.sum(weights, axis=0, keepdims=True))
            probs_low = probs.astype(BF16)
            delta = jnp.sum(probs_low.astype(F32) * upstream, axis=0, keepdims=True)
            dscore = probs * (upstream - delta)
            for i in range(count):
                if levels_of[i]:
                    part = jnp.sum(dscore[starts[i] : starts[i + 1]], axis=0, keepdims=True)
                    slope_sum = slope_sum + part * float(levels_of[i])
            dscore_low = dscore.astype(BF16)
            dv = dot(probs_low, grad)
            dk = dot(dscore_low, query) * scale
            dq = (dot(dscore_low, keys, 0, 0) * scale).astype(BF16)
            dq_own[seq, :, lanes] = dq[:block]
            dq_send[seq, :, lanes] = dq[block:]
            for i in range(count):
                outs[i][0, seq, :, lanes] = dk[starts[i] : starts[i + 1]].astype(outs[i].dtype)
                outs[i][1, seq, :, lanes] = dv[starts[i] : starts[i + 1]].astype(outs[i].dtype)
        slope_out[h : h + 1, :] = slope_sum


def fold_body(direct, coarse, out):
    rows = direct.shape[2]
    for kind in range(direct.shape[0]):
        for seq in range(direct.shape[1]):
            spread = dot(spread_matrix(rows, 1), coarse[kind, seq])
            out[kind, seq] = (direct[kind, seq] + spread).astype(BF16)


def relay_body(count, *refs):
    direct, back, outs = refs[:count], refs[count : 2 * count], refs[2 * count :]
    for first, second, out in zip(direct, back, outs):
        out[...] = (first[...] + second[...].astype(F32)).astype(BF16)


def gather_body(levels_of, own, other, *refs):
    back, (kept, sent) = refs[: len(levels_of)], refs[len(levels_of) :]
    block = own.shape[2]
    spread = jnp.concatenate([spread_matrix(2 * block, level) for level in levels_of], axis=1)
    for kind in range(own.shape[0]):
        for seq in range(own.shape[1]):
            cells = jnp.concatenate([part[kind, seq] for part in back], axis=0)
            total = dot(spread, cells)
            kept[kind, seq] = (own[kind, seq] + total[:block]).astype(BF16)
            sent[kind, seq] = (other[kind, seq] + total[block:]).astype(BF16)


def join_body(core, dq_own, dq_other, kv_own, kv_other, dq, dk, dv):
    half = dq_own.shape[-1]
    mine = pl.ds(pl.multiple_of(core[0] * half, half), half)
    theirs = pl.ds(pl.multiple_of((1 - core[0]) * half, half), half)
    dq[:, :, mine] = dq_own[...]
    dq[:, :, theirs] = dq_other[...]
    for index, out in enumerate((dk, dv)):
        out[:, :, mine] = kv_own[index]
        out[:, :, theirs] = kv_other[index]


def paired(queries, key_rows, value_rows, out_grad, level_slope):
    seqs, block, width = queries.shape
    heads = level_slope.shape[0]
    half = width // 2
    ctx_count = lax.axis_size("ctx")
    levels = ctx_count.bit_length() - 1
    core = (lax.axis_index("ctx") % 2).astype(jnp.int32).reshape(1)

    part = like(2, seqs, block, half)
    kv_own, kv_send, qg_own, qg_send = call(
        split_body, (part,) * 4, (core, key_rows, value_rows, queries, out_grad), scalars=1, name="split_heads"
    )
    kv_other = swap(kv_send, 1)
    qg_other = swap(qg_send, 1)

    cells = call(
        summary_body,
        tuple(like(2, seqs, 2 * block >> level, half) for level in range(1, levels)),
        (kv_own, kv_other),
        name="summaries",
    )
    level_of = {m: m.bit_length() for m in range(1, ctx_count // 2)}
    far = [m for m in range(4, ctx_count // 2, 2)]
    far_cells = [swap(cells[level_of[m] - 1], 2 * m) for m in far]
    near_cells = swap(cells[0], 2)
    side_cells = swap(cells[1], 4)
    relayed_cells = [swap(c, 2) for c in far_cells]
    across = call(coarser_body, like(2, seqs, block // 2, half), (near_cells,), name="coarser")
    across_cells = swap(across, 4)

    pieces = [kv_own, kv_other, near_cells, side_cells, across_cells] + far_cells + relayed_cells
    levels_of = [0, 0, 1, 2, 2] + [level_of[m] for m in far] * 2
    kinds = [F32, F32, F32, BF16, BF16] + [F32] * len(far) + [BF16] * len(far)
    rows = sum(p.shape[2] for p in pieces)
    dq_part = like(seqs, block, half)
    dq_own, dq_send, slope_part, *grads = call(
        functools.partial(attend_body, tuple(levels_of), width // heads),
        (dq_part, dq_part, like(heads // 2, 2 * block, dtype=F32))
        + tuple(like(*p.shape, dtype=kind) for p, kind in zip(pieces, kinds)),
        (core, level_slope, qg_own, qg_other, *pieces),
        scalars=2,
        flops=10 * seqs * 2 * block * rows * half,
        name="attend",
    )
    own, other, near, side, across = grads[:5]
    far_direct, far_relayed = grads[5 : 5 + len(far)], grads[5 + len(far) :]

    across_back = swap(across, 4)
    relay_back = [swap(part, 2) for part in far_relayed]
    near_total = call(fold_body, like(*near.shape), (near, across_back), name="fold")
    far_total = call(
        functools.partial(relay_body, len(far)),
        tuple(like(*part.shape) for part in far_direct),
        (*far_direct, *relay_back),
        name="relay",
    )
    near_back = swap(near_total, 2)
    far_back = [swap(part, 2 * m) for m, part in zip(far, far_total)]
    side_back = swap(side, 4)
    dq_other = swap(dq_send, 1)

    slope_sum = slope_part
    dp_count = lax.axis_size("dp")
    for bit in range(dp_count.bit_length() - 1):
        slope_sum = slope_sum + lax.ppermute(slope_sum, "dp", [(i, i ^ 2**bit) for i in range(dp_count)])
    for level in range(1, levels):
        slope_sum = slope_sum + swap(slope_sum, 2**level)
    slope_other = swap(slope_sum, 1)
    both = jnp.where(
        core[0] == 0,
        jnp.concatenate([slope_sum, slope_other], axis=0),
        jnp.concatenate([slope_other, slope_sum], axis=0),
    )
    slope_grad = jnp.sum(both, axis=1)

    kv_grad, kv_grad_send = call(
        functools.partial(gather_body, (1, 2) + tuple(level_of[m] for m in far)),
        (part, part),
        (own, other, near_back, side_back, *far_back),
        name="gather_cells",
    )
    kv_grad_other = swap(kv_grad_send, 1)
    whole = like(seqs, block, width)
    dq, dk, dv = call(
        join_body, (whole,) * 3, (core, dq_own, dq_other, kv_grad, kv_grad_other), scalars=1, name="join_heads"
    )
    return dq, dk, dv, slope_grad


def as_sent(x):
    return jax.tree.map(lambda a: a.astype(jnp.bfloat16) if a.dtype == jnp.float32 else a, x)


def from_partner(value, axis, apart):
    mask = 2**apart
    pairs = [(source, source ^ mask) for source in range(lax.axis_size(axis))]
    return lax.ppermute(value, axis, pairs)


def pair_mean(cells):
    shaped = cells.reshape(cells.shape[:-2] + (cells.shape[-2] // 2, 2, cells.shape[-1])).astype(
        jnp.float32
    )
    return ((shaped[..., 0, :] + shaped[..., 1, :]) * 0.5).astype(jnp.bfloat16)


def merge_level(own_pair, other_pair, flag):
    merged = []
    for own_part, other_part in zip(own_pair, other_pair):
        own_small = pair_mean(own_part)
        other_small = pair_mean(other_part)
        merged.append(
            jnp.where(
                flag == 1,
                jnp.concatenate([other_small, own_small], axis=1),
                jnp.concatenate([own_small, other_small], axis=1),
            )
        )
    return tuple(merged)


def to_heads(rows, heads):
    seqs, count, width = rows.shape
    return jnp.transpose(rows.reshape(seqs, count, heads, width // heads), (0, 2, 1, 3))


def from_heads(split):
    seqs, heads, count, head = split.shape
    return jnp.transpose(split, (0, 2, 1, 3)).reshape(seqs, count, heads * head)


def product(form, left, right):
    return jnp.einsum(form, left, right, preferred_element_type=jnp.float32)


def attend(query_four, key_four, value_four, grad_four, level_slope, block):
    head = query_four.shape[3]
    key_count = key_four.shape[2]
    scale = 1.0 / math.sqrt(head)
    column = jnp.arange(key_count, dtype=jnp.int32)
    level_of = column // block - 1
    sibling = jnp.maximum(level_of, 0)
    multiple = jnp.where(level_of < 0, 1.0, jnp.exp2(sibling.astype(jnp.float32)))
    bias = level_slope[:, None] * sibling.astype(jnp.float32)[None, :]
    raw = product("shqd,shkd->shqk", query_four, key_four)
    scores = raw * scale + bias[None, :, None, :]
    top = jnp.max(scores, axis=-1, keepdims=True)
    weights = multiple[None, None, None, :] * jnp.exp(scores - top)
    probs = weights / jnp.sum(weights, axis=-1, keepdims=True)
    probs_low = probs.astype(jnp.bfloat16)
    output = product("shqk,shkd->shqd", probs_low, value_four)
    delta = jnp.sum(grad_four.astype(jnp.float32) * output, axis=-1)
    upstream = product("shqd,shkd->shqk", grad_four, value_four)
    dscore = probs * (upstream - delta[..., None])
    slope_part = jnp.sum(dscore * sibling.astype(jnp.float32)[None, None, None, :], axis=(0, 2, 3))
    dscore_low = dscore.astype(jnp.bfloat16)
    query_part = product("shqk,shkd->shqd", dscore_low, key_four) * scale
    key_part = product("shqk,shqd->shkd", dscore_low, query_four) * scale
    value_part = product("shqk,shqd->shkd", probs_low, grad_four)
    return (query_part, key_part, value_part, slope_part)


def split_level(grad_now, direct, flag, level, block):
    half = block // 2
    lower_src = grad_now[:, :, :half]
    upper_src = grad_now[:, :, half:]
    own_src = jnp.where(flag == 1, upper_src, lower_src)
    other_src = jnp.where(flag == 1, lower_src, upper_src)
    own_half = jnp.repeat(own_src, 2, axis=2) * 0.5
    other_half = jnp.repeat(other_src, 2, axis=2) * 0.5
    sent = (other_half + direct[:, :, (level + 1) * block : (level + 2) * block]).astype(
        jnp.bfloat16
    )
    return (own_half, sent)


def by_blocks(queries, key_rows, value_rows, out_grad, level_slope):
    seqs, block, width = queries.shape
    heads = level_slope.shape[0]
    ctx_count = lax.axis_size("ctx")
    levels = ctx_count.bit_length() - 1
    position = lax.axis_index("ctx")
    bit_list = [position // 2**level % 2 for level in range(levels)]
    own_pair = (key_rows, value_rows)
    partners = []
    for level in range(levels - 2):
        other_pair = jax.tree.map(
            lambda part, own: part.astype(own.dtype),
            from_partner(as_sent(own_pair), "ctx", level),
            own_pair,
        )
        partners.append(other_pair)
        own_pair = merge_level(own_pair, other_pair, bit_list[level])
    for level in range(levels - 2, levels):
        other_pair = jax.tree.map(
            lambda part, own: part.astype(own.dtype),
            from_partner(as_sent(own_pair), "ctx", level),
            own_pair,
        )
        partners.append(other_pair)
        if level + 1 < levels:
            own_pair = merge_level(own_pair, other_pair, bit_list[level])
    key_set = jnp.concatenate(
        [to_heads(key_rows, heads)] + [to_heads(pair[0], heads) for pair in partners], axis=2
    )
    value_set = jnp.concatenate(
        [to_heads(value_rows, heads)] + [to_heads(pair[1], heads) for pair in partners], axis=2
    )
    query_four = to_heads(queries, heads)
    grad_four = to_heads(out_grad, heads)
    query_part, key_part, value_part, slope_part = attend(
        query_four, key_set, value_set, grad_four, level_slope, block
    )
    slope_grad = lax.psum(slope_part, ("dp", "ctx"))
    head = width // heads
    grad_keys = jnp.zeros((seqs, heads, block, head), jnp.float32)
    grad_values = jnp.zeros((seqs, heads, block, head), jnp.float32)
    for level in reversed(range(levels)):
        own_keys, sent_keys = split_level(grad_keys, key_part, bit_list[level], level, block)
        own_values, sent_values = split_level(
            grad_values, value_part, bit_list[level], level, block
        )
        back_keys, back_values = from_partner((sent_keys, sent_values), "ctx", level)
        grad_keys = own_keys + back_keys.astype(jnp.float32)
        grad_values = own_values + back_values.astype(jnp.float32)
    key_grad = from_heads((grad_keys + key_part[:, :, :block]).astype(jnp.bfloat16))
    value_grad = from_heads((grad_values + value_part[:, :, :block]).astype(jnp.bfloat16))
    return (from_heads(query_part.astype(jnp.bfloat16)), key_grad, value_grad, slope_grad)


def shards(queries, key_rows, value_rows, out_grad, level_slope):
    levels = lax.axis_size("ctx").bit_length() - 1
    few = levels >= 3 and 2 * queries.shape[1] >> levels - 1 >= 16
    form = paired if few else by_blocks
    return form(queries, key_rows, value_rows, out_grad, level_slope)


def solution(mesh):
    placed = (
        P("dp", "ctx", None),
        P("dp", "ctx", None),
        P("dp", "ctx", None),
        P("dp", "ctx", None),
        P(),
    )
    return jax.shard_map(
        shards,
        mesh=mesh,
        in_specs=placed,
        out_specs=(P("dp", "ctx", None), P("dp", "ctx", None), P("dp", "ctx", None), P()),
        check_vma=False,
    )
```

```python
import functools
import math

import jax
import jax.numpy as jnp
from jax import lax
from jax.experimental import pallas as pl
from jax.experimental.pallas import tpu as pltpu
from jax.sharding import PartitionSpec as P

F32, BF16 = jnp.float32, jnp.bfloat16
LOG2E = math.log2(math.e)
VMEM = pl.BlockSpec(memory_space=pltpu.VMEM)
SMEM = pl.BlockSpec(memory_space=pltpu.SMEM)
HBM = pl.BlockSpec(memory_space=pltpu.HBM)


def swap(value, apart, dp_apart=0):
    count = lax.axis_size("ctx")
    if not dp_apart:
        return lax.ppermute(value, "ctx", [(source, source ^ apart) for source in range(count)])
    mask = dp_apart * count + apart
    pairs = [(source, source ^ mask) for source in range(lax.axis_size("dp") * count)]
    return lax.ppermute(value, ("dp", "ctx"), pairs)


def like(*shape, dtype=BF16):
    return jax.ShapeDtypeStruct(shape, dtype)


def call(body, out_shape, operands, name, scalars=0, hbm_in=0, hbm_out=False, copies=0, flops=0):
    moved = sum(a.size * a.dtype.itemsize for a in jax.tree.leaves((operands, out_shape)))
    count = len(operands) - scalars - hbm_in
    return pl.pallas_call(
        body,
        out_shape=out_shape,
        in_specs=[SMEM] * scalars + [HBM] * hbm_in + [VMEM] * count,
        out_specs=jax.tree.map(lambda _: HBM if hbm_out else VMEM, out_shape),
        scratch_shapes=[pltpu.SemaphoreType.DMA((copies,))] if copies else [],
        compiler_params=pltpu.CompilerParams(vmem_limit_bytes=32 * 2**20),
        cost_estimate=pl.CostEstimate(flops=flops, bytes_accessed=moved, transcendentals=0),
        name=name,
    )(*operands)


def dot(left, right, left_dim=1, right_dim=0):
    dims = (((left_dim,), (right_dim,)), ((), ()))
    return lax.dot_general(left, right, dims, preferred_element_type=F32)


def pair_matrix(rows):
    cell = lax.broadcasted_iota(jnp.int32, (rows, 2 * rows), 0)
    source = lax.broadcasted_iota(jnp.int32, (rows, 2 * rows), 1)
    return jnp.where(source // 2 == cell, 0.5, 0.0).astype(BF16)


def spread_matrix(rows, level):
    row = lax.broadcasted_iota(jnp.int32, (rows, rows >> level), 0)
    cell = lax.broadcasted_iota(jnp.int32, (rows, rows >> level), 1)
    return jnp.where(row >> level == cell, 0.5**level, 0.0).astype(BF16)


def two_parts(x):
    high = x.astype(BF16)
    return jnp.concatenate([high, (x - high.astype(F32)).astype(BF16)], axis=0)


def one_part(x):
    rows = x.shape[0] // 2
    return x[:rows].astype(F32) + x[rows:].astype(F32)


def head_halves(core, half):
    mine = pl.ds(pl.multiple_of(core[0] * half, half), half)
    theirs = pl.ds(pl.multiple_of((1 - core[0]) * half, half), half)
    return mine, theirs


def copy_all(moves, sems):
    copies = [pltpu.make_async_copy(src, dst, sems.at[i]) for i, (src, dst) in enumerate(moves)]
    for copy in copies:
        copy.start()
    for copy in copies:
        copy.wait()


def split_body(core, first, second, own, send, sems):
    mine, theirs = head_halves(core, own.shape[-1])
    moves = []
    for index, whole in enumerate((first, second)):
        moves.append((whole.at[:, :, theirs], send.at[index]))
        moves.append((whole.at[:, :, mine], own.at[index]))
    copy_all(moves, sems)


def summary_body(own, other, *cells):
    for kind in range(own.shape[0]):
        for seq in range(own.shape[1]):
            rows = jnp.concatenate([own[kind, seq], other[kind, seq]], axis=0)
            for out in cells:
                rows = dot(pair_matrix(rows.shape[0] // 2), rows).astype(BF16)
                out[kind, seq] = rows


def coarser_body(cells, out):
    for kind in range(cells.shape[0]):
        for seq in range(cells.shape[1]):
            rows = cells[kind, seq]
            out[kind, seq] = dot(pair_matrix(rows.shape[0] // 2), rows).astype(BF16)


def attend_body(levels_of, head, core, slope, *refs):
    count = len(levels_of)
    qg_own, qg_other = refs[:2]
    pieces = refs[2 : 2 + count]
    dq_own, dq_send, slope_out, own, other, near, across, side, far, relay = refs[2 + count :]
    seqs, block, width = qg_own.shape[1:]
    heads = width // head
    scale = 1.0 / math.sqrt(head)
    sizes = [piece.shape[2] for piece in pieces]
    starts = [sum(sizes[:i]) for i in range(count + 1)]
    far_count = (count - 5) // 2
    slabs = [2 * seqs * heads * sum(sizes[5 : 5 + i]) for i in range(far_count)]
    for h in range(heads):
        lanes = slice(h * head, (h + 1) * head)
        step = slope[core[0] * heads + h] * LOG2E + 1.0
        slope_sum = jnp.zeros((1, 2 * block), F32)
        for seq in range(seqs):
            query = jnp.concatenate([qg_own[0, seq, :, lanes], qg_other[0, seq, :, lanes]], axis=0)
            grad = jnp.concatenate([qg_own[1, seq, :, lanes], qg_other[1, seq, :, lanes]], axis=0)
            keys = jnp.concatenate([piece[0, seq, :, lanes] for piece in pieces], axis=0)
            values = jnp.concatenate([piece[1, seq, :, lanes] for piece in pieces], axis=0)
            raw = dot(keys, query, 1, 1)
            upstream = dot(values, grad, 1, 1)
            scores = jnp.concatenate(
                [
                    raw[starts[i] : starts[i + 1]] * (scale * LOG2E) + step * float(levels_of[i])
                    for i in range(count)
                ],
                axis=0,
            )
            weights = jnp.exp2(scores - jnp.max(scores, axis=0, keepdims=True))
            probs = weights * (1.0 / jnp.sum(weights, axis=0, keepdims=True))
            probs_low = probs.astype(BF16)
            delta = jnp.sum(probs_low.astype(F32) * upstream, axis=0, keepdims=True)
            dscore = probs * (upstream - delta)
            for i in range(count):
                if levels_of[i]:
                    part = jnp.sum(dscore[starts[i] : starts[i + 1]], axis=0, keepdims=True)
                    slope_sum = slope_sum + part * float(levels_of[i])
            dscore_low = dscore.astype(BF16)
            dv = dot(probs_low, grad)
            dk = dot(dscore_low, query) * scale
            dq = (dot(dscore_low, keys, 0, 0) * scale).astype(BF16)
            dq_own[seq, :, lanes] = dq[:block]
            dq_send[seq, :, lanes] = dq[block:]
            for kind, direct in enumerate((dk, dv)):
                parts = [direct[starts[i] : starts[i + 1]] for i in range(count)]
                own[kind, seq, :, lanes] = parts[0]
                other[kind, seq, :, lanes] = parts[1]
                near[kind, seq, :, lanes] = parts[2]
                group = (kind * seqs + seq) * heads + h
                side[pl.ds(group * sizes[3], sizes[3]), :] = parts[3].astype(BF16)
                across[kind, seq, :, lanes] = parts[4].astype(BF16)
                for i in range(far_count):
                    at = pl.ds(slabs[i] + group * sizes[5 + i], sizes[5 + i])
                    far[at, :] = parts[5 + i]
                    relay[at, :] = parts[5 + far_count + i].astype(BF16)
        slope_out[h : h + 1, :] = slope_sum
    relay[pl.ds(far.shape[0], 2 * heads), :] = two_parts(slope_out[...])


def fold_body(direct, coarse, out):
    rows = direct.shape[2]
    for kind in range(direct.shape[0]):
        for seq in range(direct.shape[1]):
            spread = dot(spread_matrix(rows, 1), coarse[kind, seq])
            out[kind, seq] = (direct[kind, seq] + spread).astype(BF16)


def relay_body(side, far, back, slope, *refs):
    heads = slope.shape[0]
    tail = 2 * heads
    slopes = [ref for ref in refs if ref.shape == slope.shape]
    others, slope_out = slopes[:-1], slopes[-1]
    side_out, *far_outs = [ref for ref in refs if ref.shape != slope.shape]
    total = slope[...] + one_part(back[pl.ds(far.shape[0], tail), :])
    for ref in others:
        total = total + ref[...]
    slope_out[...] = total
    ending = two_parts(total)
    rows = side.shape[0]
    side_out[pl.ds(0, rows), :] = side[...]
    side_out[pl.ds(rows, tail), :] = ending
    start = 0
    for out in far_outs:
        rows = out.shape[0] - tail
        here = pl.ds(start, rows)
        out[pl.ds(0, rows), :] = (far[here, :] + back[here, :].astype(F32)).astype(BF16)
        out[pl.ds(rows, tail), :] = ending
        start += rows


def gather_body(levels_of, own, other, slope, near, *refs):
    back, (kept, sent, slope_out) = refs[:-3], refs[-3:]
    kinds, seqs, block, width = own.shape
    heads = slope.shape[0]
    head = width // heads
    sizes = [2 * block >> level for level in levels_of[1:]]
    spread = jnp.concatenate([spread_matrix(2 * block, level) for level in levels_of], axis=1)
    for kind in range(kinds):
        for seq in range(seqs):
            for h in range(heads):
                lanes = slice(h * head, (h + 1) * head)
                group = (kind * seqs + seq) * heads + h
                cells = [near[kind, seq, :, lanes]]
                cells += [part[pl.ds(group * size, size), :] for part, size in zip(back, sizes)]
                total = dot(spread, jnp.concatenate(cells, axis=0))
                kept[kind, seq, :, lanes] = (own[kind, seq, :, lanes] + total[:block]).astype(BF16)
                sent[kind, seq, :, lanes] = (other[kind, seq, :, lanes] + total[block:]).astype(BF16)
    all_slopes = slope[...]
    for part, size in zip(back, sizes):
        all_slopes = all_slopes + one_part(part[pl.ds(kinds * seqs * heads * size, 2 * heads), :])
    slope_out[...] = all_slopes


def join_body(core, own, other, out, sems):
    mine, theirs = head_halves(core, own.shape[-1])
    copy_all([(other, out.at[:, :, theirs]), (own, out.at[:, :, mine])], sems)


def join_pair_body(core, own, other, first, second, sems):
    mine, theirs = head_halves(core, own.shape[-1])
    moves = []
    for index, out in enumerate((first, second)):
        moves.append((other.at[index], out.at[:, :, theirs]))
        moves.append((own.at[index], out.at[:, :, mine]))
    copy_all(moves, sems)


def paired(queries, key_rows, value_rows, out_grad, level_slope):
    seqs, block, width = queries.shape
    heads = level_slope.shape[0]
    half, head = width // 2, width // heads
    ctx_count, dp_count = lax.axis_size("ctx"), lax.axis_size("dp")
    levels = ctx_count.bit_length() - 1
    position = lax.axis_index("ctx")
    core = (position % 2).astype(jnp.int32).reshape(1)

    part = like(2, seqs, block, half)
    kv_own, kv_send = call(
        split_body, (part, part), (core, key_rows, value_rows), "split_kv", scalars=1, hbm_in=2, copies=4
    )
    kv_other = swap(kv_send, 1)
    qg_own, qg_send = call(
        split_body, (part, part), (core, queries, out_grad), "split_qg", scalars=1, hbm_in=2, copies=4
    )
    qg_other = swap(qg_send, 1)

    cells = call(
        summary_body,
        tuple(like(2, seqs, 2 * block >> level, half) for level in range(1, levels)),
        (kv_own, kv_other),
        "summaries",
    )
    far = list(range(4, ctx_count // 2, 2))
    far_levels = [m.bit_length() for m in far]
    far_cells = [swap(cells[level - 1], 2 * m) for m, level in zip(far, far_levels)]
    near_cells = swap(cells[0], 2)
    side_cells = swap(cells[1], 4)
    across_cells = swap(call(coarser_body, like(2, seqs, block // 2, half), (near_cells,), "coarser"), 4)
    relayed_cells = [swap(c, 2) for c in far_cells]

    pieces = [kv_own, kv_other, near_cells, side_cells, across_cells] + far_cells + relayed_cells
    levels_of = [0, 0, 1, 2, 2] + far_levels * 2
    rows = sum(p.shape[2] for p in pieces)
    groups = seqs * heads
    far_rows = [groups * (2 * block >> level) for level in far_levels]
    tail = heads
    slope_part = like(heads // 2, 2 * block, dtype=F32)
    dq_part = like(seqs, block, half)
    dq_own, dq_send, slope, own, other, near, across, side, far_direct, relay = call(
        functools.partial(attend_body, tuple(levels_of), head),
        (
            dq_part,
            dq_part,
            slope_part,
            like(*part.shape, dtype=F32),
            like(*part.shape, dtype=F32),
            like(*part.shape, dtype=F32),
            like(2, seqs, block // 2, half),
            like(groups * (block // 2), head),
            like(sum(far_rows), head, dtype=F32),
            like(sum(far_rows) + tail, head),
        ),
        (core, level_slope, qg_own, qg_other, *pieces),
        "attend",
        scalars=2,
        flops=10 * seqs * 2 * block * rows * half,
    )

    across_back = swap(across, 4)
    relay_back = swap(relay, 2)
    slopes = [swap(slope, 2 * y, dp) for dp in range(1, dp_count) for y in range(2)]
    dq_other = swap(dq_send, 1)
    near_back = swap(call(fold_body, like(*near.shape), (near, across_back), "fold"), 2)
    slope, side_total, *far_total = call(
        relay_body,
        (slope_part, like(side.shape[0] + tail, head)) + tuple(like(r + tail, head) for r in far_rows),
        (side, far_direct, relay_back, slope, *slopes),
        "relay",
    )
    side_back = swap(side_total, 4)
    far_back = [swap(message, 2 * m) for m, message in zip(far, far_total)]
    whole = like(seqs, block, width)
    dq = call(
        join_body, whole, (core, dq_own, dq_other), "join_queries", scalars=1, hbm_out=True, copies=2
    )
    kept, sent, slope = call(
        functools.partial(gather_body, (1, 2, *far_levels)),
        (part, part, slope_part),
        (own, other, slope, near_back, side_back, *far_back),
        "gather_cells",
    )
    kv_grad_other = swap(sent, 1)
    slope_other = swap(slope, 1)
    dk, dv = call(
        join_pair_body, (whole, whole), (core, kept, kv_grad_other), "join_kv", scalars=1, hbm_out=True, copies=4
    )
    ours, rest = jnp.sum(slope, axis=1), jnp.sum(slope_other, axis=1)
    slope_grad = jnp.concatenate([jnp.where(core == 0, ours, rest), jnp.where(core == 0, rest, ours)])
    return dq, dk, dv, slope_grad


def as_sent(x):
    return jax.tree.map(lambda a: a.astype(jnp.bfloat16) if a.dtype == jnp.float32 else a, x)


def from_partner(value, axis, apart):
    mask = 2**apart
    pairs = [(source, source ^ mask) for source in range(lax.axis_size(axis))]
    return lax.ppermute(value, axis, pairs)


def pair_mean(cells):
    shaped = cells.reshape(cells.shape[:-2] + (cells.shape[-2] // 2, 2, cells.shape[-1])).astype(
        jnp.float32
    )
    return ((shaped[..., 0, :] + shaped[..., 1, :]) * 0.5).astype(jnp.bfloat16)


def merge_level(own_pair, other_pair, flag):
    merged = []
    for own_part, other_part in zip(own_pair, other_pair):
        own_small = pair_mean(own_part)
        other_small = pair_mean(other_part)
        merged.append(
            jnp.where(
                flag == 1,
                jnp.concatenate([other_small, own_small], axis=1),
                jnp.concatenate([own_small, other_small], axis=1),
            )
        )
    return tuple(merged)


def to_heads(rows, heads):
    seqs, count, width = rows.shape
    return jnp.transpose(rows.reshape(seqs, count, heads, width // heads), (0, 2, 1, 3))


def from_heads(split):
    seqs, heads, count, head = split.shape
    return jnp.transpose(split, (0, 2, 1, 3)).reshape(seqs, count, heads * head)


def product(form, left, right):
    return jnp.einsum(form, left, right, preferred_element_type=jnp.float32)


def attend(query_four, key_four, value_four, grad_four, level_slope, block):
    head = query_four.shape[3]
    key_count = key_four.shape[2]
    scale = 1.0 / math.sqrt(head)
    column = jnp.arange(key_count, dtype=jnp.int32)
    level_of = column // block - 1
    sibling = jnp.maximum(level_of, 0)
    multiple = jnp.where(level_of < 0, 1.0, jnp.exp2(sibling.astype(jnp.float32)))
    bias = level_slope[:, None] * sibling.astype(jnp.float32)[None, :]
    raw = product("shqd,shkd->shqk", query_four, key_four)
    scores = raw * scale + bias[None, :, None, :]
    top = jnp.max(scores, axis=-1, keepdims=True)
    weights = multiple[None, None, None, :] * jnp.exp(scores - top)
    probs = weights / jnp.sum(weights, axis=-1, keepdims=True)
    probs_low = probs.astype(jnp.bfloat16)
    output = product("shqk,shkd->shqd", probs_low, value_four)
    delta = jnp.sum(grad_four.astype(jnp.float32) * output, axis=-1)
    upstream = product("shqd,shkd->shqk", grad_four, value_four)
    dscore = probs * (upstream - delta[..., None])
    slope_part = jnp.sum(dscore * sibling.astype(jnp.float32)[None, None, None, :], axis=(0, 2, 3))
    dscore_low = dscore.astype(jnp.bfloat16)
    query_part = product("shqk,shkd->shqd", dscore_low, key_four) * scale
    key_part = product("shqk,shqd->shkd", dscore_low, query_four) * scale
    value_part = product("shqk,shqd->shkd", probs_low, grad_four)
    return (query_part, key_part, value_part, slope_part)


def split_level(grad_now, direct, flag, level, block):
    half = block // 2
    lower_src = grad_now[:, :, :half]
    upper_src = grad_now[:, :, half:]
    own_src = jnp.where(flag == 1, upper_src, lower_src)
    other_src = jnp.where(flag == 1, lower_src, upper_src)
    own_half = jnp.repeat(own_src, 2, axis=2) * 0.5
    other_half = jnp.repeat(other_src, 2, axis=2) * 0.5
    sent = (other_half + direct[:, :, (level + 1) * block : (level + 2) * block]).astype(
        jnp.bfloat16
    )
    return (own_half, sent)


def by_blocks(queries, key_rows, value_rows, out_grad, level_slope):
    seqs, block, width = queries.shape
    heads = level_slope.shape[0]
    ctx_count = lax.axis_size("ctx")
    levels = ctx_count.bit_length() - 1
    position = lax.axis_index("ctx")
    bit_list = [position // 2**level % 2 for level in range(levels)]
    own_pair = (key_rows, value_rows)
    partners = []
    for level in range(levels - 2):
        other_pair = jax.tree.map(
            lambda part, own: part.astype(own.dtype),
            from_partner(as_sent(own_pair), "ctx", level),
            own_pair,
        )
        partners.append(other_pair)
        own_pair = merge_level(own_pair, other_pair, bit_list[level])
    for level in range(levels - 2, levels):
        other_pair = jax.tree.map(
            lambda part, own: part.astype(own.dtype),
            from_partner(as_sent(own_pair), "ctx", level),
            own_pair,
        )
        partners.append(other_pair)
        if level + 1 < levels:
            own_pair = merge_level(own_pair, other_pair, bit_list[level])
    key_set = jnp.concatenate(
        [to_heads(key_rows, heads)] + [to_heads(pair[0], heads) for pair in partners], axis=2
    )
    value_set = jnp.concatenate(
        [to_heads(value_rows, heads)] + [to_heads(pair[1], heads) for pair in partners], axis=2
    )
    query_four = to_heads(queries, heads)
    grad_four = to_heads(out_grad, heads)
    query_part, key_part, value_part, slope_part = attend(
        query_four, key_set, value_set, grad_four, level_slope, block
    )
    slope_grad = lax.psum(slope_part, ("dp", "ctx"))
    head = width // heads
    grad_keys = jnp.zeros((seqs, heads, block, head), jnp.float32)
    grad_values = jnp.zeros((seqs, heads, block, head), jnp.float32)
    for level in reversed(range(levels)):
        own_keys, sent_keys = split_level(grad_keys, key_part, bit_list[level], level, block)
        own_values, sent_values = split_level(
            grad_values, value_part, bit_list[level], level, block
        )
        back_keys, back_values = from_partner((sent_keys, sent_values), "ctx", level)
        grad_keys = own_keys + back_keys.astype(jnp.float32)
        grad_values = own_values + back_values.astype(jnp.float32)
    key_grad = from_heads((grad_keys + key_part[:, :, :block]).astype(jnp.bfloat16))
    value_grad = from_heads((grad_values + value_part[:, :, :block]).astype(jnp.bfloat16))
    return (from_heads(query_part.astype(jnp.bfloat16)), key_grad, value_grad, slope_grad)


def shards(queries, key_rows, value_rows, out_grad, level_slope):
    levels = lax.axis_size("ctx").bit_length() - 1
    cells = 2 * queries.shape[1] >> levels - 1
    few = levels >= 4 and cells >= 16 and level_slope.shape[0] % 16 == 0
    form = paired if few else by_blocks
    return form(queries, key_rows, value_rows, out_grad, level_slope)


def solution(mesh):
    placed = (
        P("dp", "ctx", None),
        P("dp", "ctx", None),
        P("dp", "ctx", None),
        P("dp", "ctx", None),
        P(),
    )
    return jax.shard_map(
        shards,
        mesh=mesh,
        in_specs=placed,
        out_specs=(P("dp", "ctx", None), P("dp", "ctx", None), P("dp", "ctx", None), P()),
        check_vma=False,
    )
```

```python
import functools
import math

import jax
import jax.numpy as jnp
from jax import lax
from jax.experimental import pallas as pl
from jax.experimental.pallas import tpu as pltpu
from jax.sharding import PartitionSpec as P

F32, BF16 = jnp.float32, jnp.bfloat16
LOG2E = math.log2(math.e)
VMEM = pl.BlockSpec(memory_space=pltpu.VMEM)
SMEM = pl.BlockSpec(memory_space=pltpu.SMEM)
HBM = pl.BlockSpec(memory_space=pltpu.HBM)


def swap(value, apart, dp_apart=0):
    count = lax.axis_size("ctx")
    if not dp_apart:
        return lax.ppermute(value, "ctx", [(source, source ^ apart) for source in range(count)])
    mask = dp_apart * count + apart
    pairs = [(source, source ^ mask) for source in range(lax.axis_size("dp") * count)]
    return lax.ppermute(value, ("dp", "ctx"), pairs)


def like(*shape, dtype=BF16):
    return jax.ShapeDtypeStruct(shape, dtype)


def call(body, out_shape, operands, name, scalars=0, hbm_in=0, hbm_out=0, copies=0, flops=0, limit=32):
    moved = sum(a.size * a.dtype.itemsize for a in jax.tree.leaves((operands, out_shape)))
    count = len(operands) - scalars - hbm_in
    return pl.pallas_call(
        body,
        out_shape=out_shape,
        in_specs=[SMEM] * scalars + [HBM] * hbm_in + [VMEM] * count,
        out_specs=tuple(HBM if i < hbm_out else VMEM for i in range(len(out_shape)))
        if isinstance(out_shape, tuple)
        else VMEM,
        scratch_shapes=[pltpu.SemaphoreType.DMA((copies,))] if copies else [],
        compiler_params=pltpu.CompilerParams(vmem_limit_bytes=limit * 2**20),
        cost_estimate=pl.CostEstimate(flops=flops, bytes_accessed=moved, transcendentals=0),
        name=name,
    )(*operands)


def dot(left, right, left_dim=1, right_dim=0):
    dims = (((left_dim,), (right_dim,)), ((), ()))
    return lax.dot_general(left, right, dims, preferred_element_type=F32)


def pair_matrix(rows):
    cell = lax.broadcasted_iota(jnp.int32, (rows, 2 * rows), 0)
    source = lax.broadcasted_iota(jnp.int32, (rows, 2 * rows), 1)
    return jnp.where(source // 2 == cell, 0.5, 0.0).astype(BF16)


def spread_matrix(rows, level):
    row = lax.broadcasted_iota(jnp.int32, (rows, rows >> level), 0)
    cell = lax.broadcasted_iota(jnp.int32, (rows, rows >> level), 1)
    return jnp.where(row >> level == cell, 0.5**level, 0.0).astype(BF16)


def two_parts(x):
    high = x.astype(BF16)
    return jnp.concatenate([high, (x - high.astype(F32)).astype(BF16)], axis=0)


def one_part(x):
    rows = x.shape[0] // 2
    return x[:rows].astype(F32) + x[rows:].astype(F32)


def head_halves(core, half):
    mine = pl.ds(pl.multiple_of(core[0] * half, half), half)
    theirs = pl.ds(pl.multiple_of((1 - core[0]) * half, half), half)
    return mine, theirs


def copy_all(moves, sems):
    copies = [pltpu.make_async_copy(src, dst, sems.at[i]) for i, (src, dst) in enumerate(moves)]
    for copy in copies:
        copy.start()
    for copy in copies:
        copy.wait()


def split_body(core, first, second, own, send, sems):
    mine, theirs = head_halves(core, own.shape[-1])
    moves = []
    for index, whole in enumerate((first, second)):
        moves.append((whole.at[:, :, theirs], send.at[index]))
        moves.append((whole.at[:, :, mine], own.at[index]))
    copy_all(moves, sems)


def summary_body(own, other, *cells):
    for kind in range(own.shape[0]):
        for seq in range(own.shape[1]):
            rows = jnp.concatenate([own[kind, seq], other[kind, seq]], axis=0)
            for out in cells:
                rows = dot(pair_matrix(rows.shape[0] // 2), rows).astype(BF16)
                out[kind, seq] = rows


def coarser_body(cells, out):
    for kind in range(cells.shape[0]):
        for seq in range(cells.shape[1]):
            rows = cells[kind, seq]
            out[kind, seq] = dot(pair_matrix(rows.shape[0] // 2), rows).astype(BF16)


def stack_body(*refs):
    *parts, out = refs
    start = 0
    for part in parts:
        rows = part.shape[2]
        out[:, :, pl.ds(start, rows), :] = part[...]
        start += rows


def stacked(parts, kind, seq, lanes):
    return jnp.concatenate([part[kind, seq, :, lanes] for part in parts], axis=0)


def score_body(levels_of, head, core, slope, qg_own, qg_other, *refs):
    *pieces, scores, upstream = refs
    seqs, width = qg_own.shape[1], qg_own.shape[3]
    heads = width // head
    scale = LOG2E / math.sqrt(head)
    for h in range(heads):
        lanes = slice(h * head, (h + 1) * head)
        step = slope[core[0] * heads + h] * LOG2E + 1.0
        for seq in range(seqs):
            raw = dot(stacked(pieces, 0, seq, lanes), stacked((qg_own, qg_other), 0, seq, lanes), 1, 1)
            start = 0
            for piece, level in zip(pieces, levels_of):
                here = slice(start, start + piece.shape[2])
                scores[seq * heads + h, here] = raw[here] * scale + step * float(level)
                start += piece.shape[2]
            upstream[seq * heads + h] = dot(
                stacked(pieces, 1, seq, lanes), stacked((qg_own, qg_other), 1, seq, lanes), 1, 1
            )


def attend_body(runs, head, far_sizes, core, slope, *refs):
    early, (qg_own, qg_other, across_cells, relayed_cells), outs = refs[:4], refs[4:8], refs[8:]
    slope_out, near, across, side, far, relay, dscore_out, probs_out = outs
    seqs, block, width = qg_own.shape[1:]
    heads = width // head
    scale = 1.0 / math.sqrt(head)
    token_rows = 2 * block
    early_rows = early[0].shape[1] + early[2].shape[1]
    starts = [sum(rows for _, rows in runs[:i]) for i in range(len(runs) + 1)]
    far_count = len(far_sizes)
    slabs = [2 * seqs * heads * sum(far_sizes[:i]) for i in range(far_count)]
    for h in range(heads):
        lanes = slice(h * head, (h + 1) * head)
        step = slope[core[0] * heads + h] * LOG2E + 1.0
        slope_sum = jnp.zeros((1, token_rows), F32)
        for seq in range(seqs):
            at = seq * heads + h
            query = stacked((qg_own, qg_other), 0, seq, lanes)
            grad = stacked((qg_own, qg_other), 1, seq, lanes)
            late = (across_cells, relayed_cells)
            raw = dot(stacked(late, 0, seq, lanes), query, 1, 1)
            late_up = dot(stacked(late, 1, seq, lanes), grad, 1, 1)
            late_scores = [
                raw[starts[i] - early_rows : starts[i + 1] - early_rows] * (scale * LOG2E) + step * float(runs[i][0])
                for i in range(len(runs))
                if starts[i] >= early_rows
            ]
            scores = jnp.concatenate([early[0][at], early[2][at], *late_scores], axis=0)
            upstream = jnp.concatenate([early[1][at], early[3][at], late_up], axis=0)
            weights = jnp.exp2(scores - jnp.max(scores, axis=0, keepdims=True))
            probs = weights * (1.0 / jnp.sum(weights, axis=0, keepdims=True))
            probs_low = probs.astype(BF16)
            delta = jnp.sum(probs_low.astype(F32) * upstream, axis=0, keepdims=True)
            dscore = probs * (upstream - delta)
            for i, (level, _) in enumerate(runs):
                if level:
                    part = jnp.sum(dscore[starts[i] : starts[i + 1]], axis=0, keepdims=True)
                    slope_sum = slope_sum + part * float(level)
            dscore_low = dscore.astype(BF16)
            dscore_out[at] = dscore_low
            probs_out[at] = probs_low[:token_rows]
            dk = dot(dscore_low[token_rows:], query) * scale
            dv = dot(probs_low[token_rows:], grad)
            for kind, direct in enumerate((dk, dv)):
                parts = [direct[starts[i] - token_rows : starts[i + 1] - token_rows] for i in range(1, len(runs))]
                group = (kind * seqs + seq) * heads + h
                near[kind, seq, :, lanes] = parts[0]
                side[pl.ds(group * (block // 2), block // 2), :] = parts[1].astype(BF16)
                across[kind, seq, :, lanes] = parts[2 + far_count].astype(BF16)
                for i, size in enumerate(far_sizes):
                    here = pl.ds(slabs[i] + group * size, size)
                    far[here, :] = parts[2 + i]
                    relay[here, :] = parts[3 + far_count + i].astype(BF16)
        slope_out[h : h + 1, :] = slope_sum
    relay[pl.ds(far.shape[0], 2 * heads), :] = two_parts(slope_out[...])


def own_grads_body(head, dscore, probs, qg_own, qg_other, *refs):
    *pieces, dq_own, dq_send, own, other = refs
    seqs, block, width = qg_own.shape[1:]
    heads = width // head
    scale = 1.0 / math.sqrt(head)
    for h in range(heads):
        lanes = slice(h * head, (h + 1) * head)
        for seq in range(seqs):
            at = seq * heads + h
            dq = (dot(dscore[at], stacked(pieces, 0, seq, lanes), 0, 0) * scale).astype(BF16)
            dq_own[seq, :, lanes] = dq[:block]
            dq_send[seq, :, lanes] = dq[block:]
            dk = dot(dscore[at, : 2 * block], stacked((qg_own, qg_other), 0, seq, lanes)) * scale
            dv = dot(probs[at], stacked((qg_own, qg_other), 1, seq, lanes))
            for kind, direct in enumerate((dk, dv)):
                own[kind, seq, :, lanes] = direct[:block]
                other[kind, seq, :, lanes] = direct[block:]


def fold_body(direct, coarse, slope, *refs):
    *slopes, out, slope_out = refs
    total = slope[...]
    for ref in slopes:
        total = total + ref[...]
    slope_out[...] = total
    rows = direct.shape[2]
    for kind in range(direct.shape[0]):
        for seq in range(direct.shape[1]):
            spread = dot(spread_matrix(rows, 1), coarse[kind, seq])
            out[kind, seq] = (direct[kind, seq] + spread).astype(BF16)


def relay_body(side, far, back, slope, slope_out, side_out, *far_outs):
    tail = 2 * slope.shape[0]
    total = slope[...] + one_part(back[pl.ds(far.shape[0], tail), :])
    slope_out[...] = total
    ending = two_parts(total)
    rows = side.shape[0]
    side_out[pl.ds(0, rows), :] = side[...]
    side_out[pl.ds(rows, tail), :] = ending
    start = 0
    for out in far_outs:
        rows = out.shape[0] - tail
        here = pl.ds(start, rows)
        out[pl.ds(0, rows), :] = (far[here, :] + back[here, :].astype(F32)).astype(BF16)
        out[pl.ds(rows, tail), :] = ending
        start += rows


def gather_body(levels_of, own, other, slope, near, *refs):
    back, (kept, sent, slope_out) = refs[:-3], refs[-3:]
    kinds, seqs, block, width = own.shape
    heads = slope.shape[0]
    head = width // heads
    sizes = [2 * block >> level for level in levels_of[1:]]
    spread = jnp.concatenate([spread_matrix(2 * block, level) for level in levels_of], axis=1)
    for kind in range(kinds):
        for seq in range(seqs):
            for h in range(heads):
                lanes = slice(h * head, (h + 1) * head)
                group = (kind * seqs + seq) * heads + h
                cells = [near[kind, seq, :, lanes]]
                cells += [part[pl.ds(group * size, size), :] for part, size in zip(back, sizes)]
                total = dot(spread, jnp.concatenate(cells, axis=0))
                kept[kind, seq, :, lanes] = (own[kind, seq, :, lanes] + total[:block]).astype(BF16)
                sent[kind, seq, :, lanes] = (other[kind, seq, :, lanes] + total[block:]).astype(BF16)
    all_slopes = slope[...]
    for part, size in zip(back, sizes):
        all_slopes = all_slopes + one_part(part[pl.ds(kinds * seqs * heads * size, 2 * heads), :])
    slope_out[...] = all_slopes


def join_body(core, own, other, out, sems):
    mine, theirs = head_halves(core, own.shape[-1])
    copy_all([(other, out.at[:, :, theirs]), (own, out.at[:, :, mine])], sems)


def join_pair_body(core, own, other, slope, slope_other, first, second, slope_out, sems):
    mine, theirs = head_halves(core, own.shape[-1])
    moves = []
    for index, out in enumerate((first, second)):
        moves.append((other.at[index], out.at[:, :, theirs]))
        moves.append((own.at[index], out.at[:, :, mine]))
    copy_all(moves, sems)
    ours, rest = slope[...], slope_other[...]
    lower = jnp.where(core[0] == 0, ours, rest)
    upper = jnp.where(core[0] == 0, rest, ours)
    terms = jnp.concatenate([lower, upper], axis=0)
    slope_out[...] = jnp.sum(terms.T, axis=0, keepdims=True)


def paired(queries, key_rows, value_rows, out_grad, level_slope):
    seqs, block, width = queries.shape
    heads = level_slope.shape[0]
    half, head = width // 2, width // heads
    ctx_count, dp_count = lax.axis_size("ctx"), lax.axis_size("dp")
    levels = ctx_count.bit_length() - 1
    position = lax.axis_index("ctx")
    core = (position % 2).astype(jnp.int32).reshape(1)

    part = like(2, seqs, block, half)
    kv_own, kv_send = call(
        split_body, (part, part), (core, key_rows, value_rows), "split_kv", scalars=1, hbm_in=2, copies=4
    )
    kv_other = swap(kv_send, 1)
    qg_own, qg_send = call(
        split_body, (part, part), (core, queries, out_grad), "split_qg", scalars=1, hbm_in=2, copies=4
    )
    qg_other = swap(qg_send, 1)

    cells = call(
        summary_body,
        tuple(like(2, seqs, 2 * block >> level, half) for level in range(1, levels)),
        (kv_own, kv_other),
        "summaries",
    )
    far = list(range(4, ctx_count // 2, 2))
    far_levels = [m.bit_length() for m in far]
    far_cells = [swap(cells[level - 1], 2 * m) for m, level in zip(far, far_levels)]
    near_cells = swap(cells[0], 2)
    side_cells = swap(cells[1], 4)
    across_cells = swap(call(coarser_body, like(2, seqs, block // 2, half), (near_cells,), "coarser"), 4)
    far_sizes = [2 * block >> level for level in far_levels]
    far_stack = call(stack_body, like(2, seqs, sum(far_sizes), half), far_cells, "stack")
    relayed_cells = swap(far_stack, 2)

    groups = seqs * heads
    early_levels, late_levels = (0, 0), (1, 2, *far_levels)
    token_rows, cell_rows = 2 * block, block + block // 2 + sum(far_sizes)
    rows = token_rows + cell_rows + block // 2 + sum(far_sizes)

    def score(levels_of, pieces, count):
        product = like(groups // 2, count, token_rows, dtype=F32)
        return call(
            functools.partial(score_body, levels_of, head),
            (product, product),
            (core, level_slope, qg_own, qg_other, *pieces),
            "scores",
            scalars=2,
            flops=40 * seqs * token_rows * count * half,
        )

    token_pieces = [kv_own, kv_other]
    cell_pieces = [near_cells, side_cells, *far_cells]
    early = (*score(early_levels, token_pieces, token_rows), *score(late_levels, cell_pieces, cell_rows))
    runs = [(0, token_rows), (1, block), (2, block // 2), *zip(far_levels, far_sizes)]
    runs += [(2, block // 2), *zip(far_levels, far_sizes)]
    far_rows = [groups * size for size in far_sizes]
    tail = heads
    slope_part = like(heads // 2, token_rows, dtype=F32)
    wide = like(*part.shape, dtype=F32)
    slope, near, across, side, far_direct, relay, dscore, probs = call(
        functools.partial(attend_body, tuple(runs), head, tuple(far_sizes)),
        (
            slope_part,
            wide,
            like(2, seqs, block // 2, half),
            like(groups * (block // 2), head),
            like(sum(far_rows), head, dtype=F32),
            like(sum(far_rows) + tail, head),
            like(groups // 2, rows, token_rows),
            like(groups // 2, token_rows, token_rows),
        ),
        (core, level_slope, *early, qg_own, qg_other, across_cells, relayed_cells),
        "attend",
        scalars=2,
        flops=40 * seqs * token_rows * rows * half,
    )
    dq_part = like(seqs, block, half)
    dq_own, dq_send, own, other = call(
        functools.partial(own_grads_body, head),
        (dq_part, dq_part, wide, wide),
        (dscore, probs, qg_own, qg_other, *token_pieces, *cell_pieces, across_cells, relayed_cells),
        "own_grads",
        flops=40 * seqs * token_rows * rows * half,
    )

    across_back = swap(across, 4)
    relay_back = swap(relay, 2)
    slopes = [swap(slope, 2 * y, dp) for dp in range(1, dp_count) for y in range(2)]
    dq_other = swap(dq_send, 1)
    near_total, slope = call(
        fold_body, (like(*near.shape), slope_part), (near, across_back, slope, *slopes), "fold"
    )
    near_back = swap(near_total, 2)
    slope, side_total, *far_total = call(
        relay_body,
        (slope_part, like(side.shape[0] + tail, head)) + tuple(like(r + tail, head) for r in far_rows),
        (side, far_direct, relay_back, slope),
        "relay",
    )
    side_back = swap(side_total, 4)
    far_back = [swap(message, 2 * m) for m, message in zip(far, far_total)]
    whole = like(seqs, block, width)
    (dq,) = call(
        join_body, (whole,), (core, dq_own, dq_other), "join_queries", scalars=1, hbm_out=1, copies=2
    )
    kept, sent, slope = call(
        functools.partial(gather_body, (1, 2, *far_levels)),
        (part, part, slope_part),
        (own, other, slope, near_back, side_back, *far_back),
        "gather_cells",
    )
    kv_grad_other = swap(sent, 1)
    slope_other = swap(slope, 1)
    dk, dv, slope_grad = call(
        join_pair_body,
        (whole, whole, like(1, heads, dtype=F32)),
        (core, kept, kv_grad_other, slope, slope_other),
        "join_kv",
        scalars=1,
        hbm_out=2,
        copies=4,
    )
    return dq, dk, dv, slope_grad.reshape(heads)


def as_sent(x):
    return jax.tree.map(lambda a: a.astype(jnp.bfloat16) if a.dtype == jnp.float32 else a, x)


def from_partner(value, axis, apart):
    mask = 2**apart
    pairs = [(source, source ^ mask) for source in range(lax.axis_size(axis))]
    return lax.ppermute(value, axis, pairs)


def pair_mean(cells):
    shaped = cells.reshape(cells.shape[:-2] + (cells.shape[-2] // 2, 2, cells.shape[-1])).astype(
        jnp.float32
    )
    return ((shaped[..., 0, :] + shaped[..., 1, :]) * 0.5).astype(jnp.bfloat16)


def merge_level(own_pair, other_pair, flag):
    merged = []
    for own_part, other_part in zip(own_pair, other_pair):
        own_small = pair_mean(own_part)
        other_small = pair_mean(other_part)
        merged.append(
            jnp.where(
                flag == 1,
                jnp.concatenate([other_small, own_small], axis=1),
                jnp.concatenate([own_small, other_small], axis=1),
            )
        )
    return tuple(merged)


def to_heads(rows, heads):
    seqs, count, width = rows.shape
    return jnp.transpose(rows.reshape(seqs, count, heads, width // heads), (0, 2, 1, 3))


def from_heads(split):
    seqs, heads, count, head = split.shape
    return jnp.transpose(split, (0, 2, 1, 3)).reshape(seqs, count, heads * head)


def product(form, left, right):
    return jnp.einsum(form, left, right, preferred_element_type=jnp.float32)


def attend(query_four, key_four, value_four, grad_four, level_slope, block):
    head = query_four.shape[3]
    key_count = key_four.shape[2]
    scale = 1.0 / math.sqrt(head)
    column = jnp.arange(key_count, dtype=jnp.int32)
    level_of = column // block - 1
    sibling = jnp.maximum(level_of, 0)
    multiple = jnp.where(level_of < 0, 1.0, jnp.exp2(sibling.astype(jnp.float32)))
    bias = level_slope[:, None] * sibling.astype(jnp.float32)[None, :]
    raw = product("shqd,shkd->shqk", query_four, key_four)
    scores = raw * scale + bias[None, :, None, :]
    top = jnp.max(scores, axis=-1, keepdims=True)
    weights = multiple[None, None, None, :] * jnp.exp(scores - top)
    probs = weights / jnp.sum(weights, axis=-1, keepdims=True)
    probs_low = probs.astype(jnp.bfloat16)
    output = product("shqk,shkd->shqd", probs_low, value_four)
    delta = jnp.sum(grad_four.astype(jnp.float32) * output, axis=-1)
    upstream = product("shqd,shkd->shqk", grad_four, value_four)
    dscore = probs * (upstream - delta[..., None])
    slope_part = jnp.sum(dscore * sibling.astype(jnp.float32)[None, None, None, :], axis=(0, 2, 3))
    dscore_low = dscore.astype(jnp.bfloat16)
    query_part = product("shqk,shkd->shqd", dscore_low, key_four) * scale
    key_part = product("shqk,shqd->shkd", dscore_low, query_four) * scale
    value_part = product("shqk,shqd->shkd", probs_low, grad_four)
    return (query_part, key_part, value_part, slope_part)


def split_level(grad_now, direct, flag, level, block):
    half = block // 2
    lower_src = grad_now[:, :, :half]
    upper_src = grad_now[:, :, half:]
    own_src = jnp.where(flag == 1, upper_src, lower_src)
    other_src = jnp.where(flag == 1, lower_src, upper_src)
    own_half = jnp.repeat(own_src, 2, axis=2) * 0.5
    other_half = jnp.repeat(other_src, 2, axis=2) * 0.5
    sent = (other_half + direct[:, :, (level + 1) * block : (level + 2) * block]).astype(
        jnp.bfloat16
    )
    return (own_half, sent)


def by_blocks(queries, key_rows, value_rows, out_grad, level_slope):
    seqs, block, width = queries.shape
    heads = level_slope.shape[0]
    ctx_count = lax.axis_size("ctx")
    levels = ctx_count.bit_length() - 1
    position = lax.axis_index("ctx")
    bit_list = [position // 2**level % 2 for level in range(levels)]
    own_pair = (key_rows, value_rows)
    partners = []
    for level in range(levels - 2):
        other_pair = jax.tree.map(
            lambda part, own: part.astype(own.dtype),
            from_partner(as_sent(own_pair), "ctx", level),
            own_pair,
        )
        partners.append(other_pair)
        own_pair = merge_level(own_pair, other_pair, bit_list[level])
    for level in range(levels - 2, levels):
        other_pair = jax.tree.map(
            lambda part, own: part.astype(own.dtype),
            from_partner(as_sent(own_pair), "ctx", level),
            own_pair,
        )
        partners.append(other_pair)
        if level + 1 < levels:
            own_pair = merge_level(own_pair, other_pair, bit_list[level])
    key_set = jnp.concatenate(
        [to_heads(key_rows, heads)] + [to_heads(pair[0], heads) for pair in partners], axis=2
    )
    value_set = jnp.concatenate(
        [to_heads(value_rows, heads)] + [to_heads(pair[1], heads) for pair in partners], axis=2
    )
    query_four = to_heads(queries, heads)
    grad_four = to_heads(out_grad, heads)
    query_part, key_part, value_part, slope_part = attend(
        query_four, key_set, value_set, grad_four, level_slope, block
    )
    slope_grad = lax.psum(slope_part, ("dp", "ctx"))
    head = width // heads
    grad_keys = jnp.zeros((seqs, heads, block, head), jnp.float32)
    grad_values = jnp.zeros((seqs, heads, block, head), jnp.float32)
    for level in reversed(range(levels)):
        own_keys, sent_keys = split_level(grad_keys, key_part, bit_list[level], level, block)
        own_values, sent_values = split_level(
            grad_values, value_part, bit_list[level], level, block
        )
        back_keys, back_values = from_partner((sent_keys, sent_values), "ctx", level)
        grad_keys = own_keys + back_keys.astype(jnp.float32)
        grad_values = own_values + back_values.astype(jnp.float32)
    key_grad = from_heads((grad_keys + key_part[:, :, :block]).astype(jnp.bfloat16))
    value_grad = from_heads((grad_values + value_part[:, :, :block]).astype(jnp.bfloat16))
    return (from_heads(query_part.astype(jnp.bfloat16)), key_grad, value_grad, slope_grad)


def shards(queries, key_rows, value_rows, out_grad, level_slope):
    levels = lax.axis_size("ctx").bit_length() - 1
    cells = 2 * queries.shape[1] >> levels - 1
    few = levels >= 4 and cells >= 16 and level_slope.shape[0] % 16 == 0
    form = paired if few else by_blocks
    return form(queries, key_rows, value_rows, out_grad, level_slope)


def solution(mesh):
    placed = (
        P("dp", "ctx", None),
        P("dp", "ctx", None),
        P("dp", "ctx", None),
        P("dp", "ctx", None),
        P(),
    )
    return jax.shard_map(
        shards,
        mesh=mesh,
        in_specs=placed,
        out_specs=(P("dp", "ctx", None), P("dp", "ctx", None), P("dp", "ctx", None), P()),
        check_vma=False,
    )
```

```python
import functools
import math

import jax
import jax.numpy as jnp
from jax import lax
from jax.experimental import pallas as pl
from jax.experimental.pallas import tpu as pltpu
from jax.sharding import PartitionSpec as P

F32, BF16 = jnp.float32, jnp.bfloat16
LOG2E = math.log2(math.e)
VMEM = pl.BlockSpec(memory_space=pltpu.VMEM)
SMEM = pl.BlockSpec(memory_space=pltpu.SMEM)
HBM = pl.BlockSpec(memory_space=pltpu.HBM)


def swap(value, apart, dp_apart=0):
    count = lax.axis_size("ctx")
    if not dp_apart:
        return lax.ppermute(value, "ctx", [(source, source ^ apart) for source in range(count)])
    mask = dp_apart * count + apart
    pairs = [(source, source ^ mask) for source in range(lax.axis_size("dp") * count)]
    return lax.ppermute(value, ("dp", "ctx"), pairs)


def like(*shape, dtype=BF16):
    return jax.ShapeDtypeStruct(shape, dtype)


def call(body, out_shape, operands, name, scalars=0, hbm_in=0, hbm_out=0, copies=0, flops=0, limit=32, scratch=()):
    moved = sum(a.size * a.dtype.itemsize for a in jax.tree.leaves((operands, out_shape)))
    count = len(operands) - scalars - hbm_in
    return pl.pallas_call(
        body,
        out_shape=out_shape,
        in_specs=[SMEM] * scalars + [HBM] * hbm_in + [VMEM] * count,
        out_specs=tuple(HBM if i < hbm_out else VMEM for i in range(len(out_shape)))
        if isinstance(out_shape, tuple)
        else VMEM,
        scratch_shapes=[*scratch, *([pltpu.SemaphoreType.DMA((copies,))] if copies else [])],
        compiler_params=pltpu.CompilerParams(vmem_limit_bytes=int(limit * 2**20)),
        cost_estimate=pl.CostEstimate(flops=flops, bytes_accessed=moved, transcendentals=0),
        name=name,
    )(*operands)


def dot(left, right, left_dim=1, right_dim=0):
    dims = (((left_dim,), (right_dim,)), ((), ()))
    return lax.dot_general(left, right, dims, preferred_element_type=F32)


def pair_matrix(rows):
    cell = lax.broadcasted_iota(jnp.int32, (rows, 2 * rows), 0)
    source = lax.broadcasted_iota(jnp.int32, (rows, 2 * rows), 1)
    return jnp.where(source // 2 == cell, 0.5, 0.0).astype(BF16)


def spread_matrix(rows, level):
    row = lax.broadcasted_iota(jnp.int32, (rows, rows >> level), 0)
    cell = lax.broadcasted_iota(jnp.int32, (rows, rows >> level), 1)
    return jnp.where(row >> level == cell, 0.5**level, 0.0).astype(BF16)


def two_parts(x):
    high = x.astype(BF16)
    return jnp.concatenate([high, (x - high.astype(F32)).astype(BF16)], axis=0)


def one_part(x):
    rows = x.shape[0] // 2
    return x[:rows].astype(F32) + x[rows:].astype(F32)


def head_halves(core, half):
    mine = pl.ds(pl.multiple_of(core[0] * half, half), half)
    theirs = pl.ds(pl.multiple_of((1 - core[0]) * half, half), half)
    return mine, theirs


def start_all(moves, sems):
    copies = [pltpu.make_async_copy(src, dst, sems.at[i]) for i, (src, dst) in enumerate(moves)]
    for copy in copies:
        copy.start()
    return copies


def copy_all(moves, sems):
    for copy in start_all(moves, sems):
        copy.wait()


def split_body(core, first, second, own, send, sems):
    mine, theirs = head_halves(core, own.shape[-1])
    moves = []
    for index, whole in enumerate((first, second)):
        moves.append((whole.at[:, :, theirs], send.at[index]))
        moves.append((whole.at[:, :, mine], own.at[index]))
    copy_all(moves, sems)


def keep_body(core, k, v, k_other, v_other, own, other):
    mine, _ = head_halves(core, own.shape[-1])
    for index, (first, second) in enumerate(((k, k_other), (v, v_other))):
        own[index] = first[:, :, mine]
        other[index] = second[:, :, mine]


def halve(rows, wide):
    count = rows.shape[0]
    wide[pl.ds(0, count), :] = rows
    return (wide[pl.ds(0, count // 2, stride=2), :] + wide[pl.ds(1, count // 2, stride=2), :]) * 0.5


def tiles_of(shape, core, wide):
    kinds, seqs, _, half = shape
    for kind in range(kinds):
        for seq in range(seqs):
            for start in range(0, half, 128):
                source = pl.ds(pl.multiple_of(core[0] * half + start, 128), 128)
                yield kind, seq, source, slice(start, start + 128), wide.at[kind, seq, start // 128]


def own_summary_body(core, k, v, *refs):
    *cells, wide = refs
    for kind, seq, source, lanes, scratch in tiles_of(cells[0].shape, core, wide):
        rows = (k, v)[kind][seq, :, source].astype(F32)
        for out in cells:
            rows = halve(rows, scratch)
            out[kind, seq, :, lanes] = jnp.concatenate([rows, jnp.zeros_like(rows)], axis=0).astype(BF16)
            rows = rows.astype(BF16).astype(F32)


def summary_body(core, k_other, v_other, *refs):
    *refs, wide = refs
    own, cells = refs[: len(refs) // 2], refs[len(refs) // 2 :]
    for kind, seq, source, lanes, scratch in tiles_of(cells[0].shape, core, wide):
        rows = (k_other, v_other)[kind][seq, :, source].astype(F32)
        for first, out in zip(own, cells):
            rows = halve(rows, scratch)
            before = first[kind, seq, :, lanes].astype(F32)[: rows.shape[0]]
            out[kind, seq, :, lanes] = jnp.concatenate([before, rows], axis=0).astype(BF16)
            rows = rows.astype(BF16).astype(F32)


def coarser_body(cells, out):
    for kind in range(cells.shape[0]):
        for seq in range(cells.shape[1]):
            rows = cells[kind, seq]
            out[kind, seq] = dot(pair_matrix(rows.shape[0] // 2), rows).astype(BF16)


def stacked(parts, kind, seq, lanes):
    return jnp.concatenate([part[kind, seq, :, lanes] for part in parts], axis=0)


def score_body(levels_of, head, core, slope, qg_own, qg_other, *refs):
    *pieces, weights, upstream, stats = refs
    seqs, width = qg_own.shape[1], qg_own.shape[3]
    heads = width // head
    scale = LOG2E / math.sqrt(head)
    for h in range(heads):
        lanes = slice(h * head, (h + 1) * head)
        step = slope[core[0] * heads + h] * LOG2E + 1.0
        for seq in range(seqs):
            at = seq * heads + h
            raw = dot(stacked(pieces, 0, seq, lanes), stacked((qg_own, qg_other), 0, seq, lanes), 1, 1)
            upstream[at] = dot(stacked(pieces, 1, seq, lanes), stacked((qg_own, qg_other), 1, seq, lanes), 1, 1)
            scores = with_bias(raw * scale, zip(levels_of, [piece.shape[2] for piece in pieces]), step)
            top = jnp.max(scores, axis=0, keepdims=True)
            spread = jnp.exp2(scores - top)
            weights[at] = spread
            stats[at, 0:1] = top
            stats[at, 1:2] = jnp.sum(spread, axis=0, keepdims=True)


def with_bias(scores, runs, step):
    parts, start = [], 0
    for level, count in runs:
        part = scores[start : start + count]
        parts.append(part + step * float(level) if level else part)
        start += count
    return jnp.concatenate(parts, axis=0)


def attend_body(runs, head, far_sizes, core, slope, *refs):
    *refs, late_scores, late_up, probs_cells = refs
    early, (qg_own, qg_other, *late), outs = refs[:6], refs[6:-8], refs[-8:]
    slope_out, near, across, side, far, relay, dscore_out, probs_out = outs
    seqs, block, width = qg_own.shape[1:]
    heads = width // head
    scale = 1.0 / math.sqrt(head)
    starts = [sum(rows for _, rows in runs[:i]) for i in range(len(runs) + 1)]
    token_rows = early[0].shape[1]
    early_rows = token_rows + early[3].shape[1]
    bounds = (0, token_rows, early_rows, starts[-1])
    late_runs = [run for run, start in zip(runs, starts) if start >= early_rows]
    far_count = len(far_sizes)
    slabs = [2 * seqs * heads * sum(far_sizes[:i]) for i in range(far_count)]

    def score(h, seq):
        at, lanes = seq * heads + h, slice(h * head, (h + 1) * head)
        step = slope[core[0] * heads + h] * LOG2E + 1.0
        raw = dot(stacked(late, 0, seq, lanes), stacked((qg_own, qg_other), 0, seq, lanes), 1, 1)
        late_scores[at] = with_bias(raw * (scale * LOG2E), late_runs, step)
        late_up[at] = dot(stacked(late, 1, seq, lanes), stacked((qg_own, qg_other), 1, seq, lanes), 1, 1)

    def normalise(h, seq):
        at = seq * heads + h
        tops = early[2][at, 0:1], early[5][at, 0:1]
        scores = late_scores[at]
        top = jnp.maximum(jnp.maximum(*tops), jnp.max(scores, axis=0, keepdims=True))
        shares = [jnp.exp2(part - top) for part in tops]
        weights = jnp.exp2(scores - top)
        total = early[2][at, 1:2] * shares[0] + early[5][at, 1:2] * shares[1]
        inverse = 1.0 / (total + jnp.sum(weights, axis=0, keepdims=True))
        probs = [early[0][at] * (shares[0] * inverse), early[3][at] * (shares[1] * inverse), weights * inverse]
        upstream = [early[1][at], early[4][at], late_up[at]]
        probs_low = [part.astype(BF16) for part in probs]
        delta = sum(jnp.sum(p.astype(F32) * u, axis=0, keepdims=True) for p, u in zip(probs_low, upstream))
        slope_sum = jnp.zeros_like(delta)
        for p, u, low, high in zip(probs, upstream, bounds, bounds[1:]):
            dscore = p * (u - delta)
            for (level, rows), start in zip(runs, starts):
                if level and low <= start < high:
                    here = dscore[start - low : start - low + rows]
                    slope_sum = slope_sum + jnp.sum(here, axis=0, keepdims=True) * float(level)
            dscore_out[at, low:high] = dscore.astype(BF16)
        probs_out[at] = probs_low[0]
        probs_cells[at] = jnp.concatenate(probs_low[1:], axis=0)
        return slope_sum

    def gradients(h, seq):
        at, lanes = seq * heads + h, slice(h * head, (h + 1) * head)
        dk = dot(dscore_out[at, token_rows:], stacked((qg_own, qg_other), 0, seq, lanes)) * scale
        dv = dot(probs_cells[at], stacked((qg_own, qg_other), 1, seq, lanes))
        for kind, direct in enumerate((dk, dv)):
            parts = [direct[starts[i] - token_rows : starts[i + 1] - token_rows] for i in range(1, len(runs))]
            group = (kind * seqs + seq) * heads + h
            near[kind, seq, :, lanes] = parts[0]
            side[pl.ds(group * (block // 2), block // 2), :] = parts[1].astype(BF16)
            across[kind, seq, :, lanes] = parts[2 + far_count].astype(BF16)
            for i, size in enumerate(far_sizes):
                here = pl.ds(slabs[i] + group * size, size)
                far[here, :] = parts[2 + i]
                relay[here, :] = parts[3 + far_count + i].astype(BF16)

    items = [(h, seq) for h in range(heads) for seq in range(seqs)]
    behind = 2
    sums = {}
    for i in range(len(items) + 2 * behind):
        if i < len(items):
            score(*items[i])
        if 0 <= i - behind < len(items):
            item = items[i - behind]
            sums[item] = normalise(*item)
        if 0 <= i - 2 * behind < len(items):
            gradients(*items[i - 2 * behind])
    for h in range(heads):
        slope_out[h : h + 1, :] = sum(sums[h, seq] for seq in range(seqs))
    relay[pl.ds(far.shape[0], 2 * heads), :] = two_parts(slope_out[...])


def own_grads_body(head, dscore, probs, qg_own, qg_other, *refs):
    *pieces, dq_own, dq_send, own, other = refs
    seqs, block, width = qg_own.shape[1:]
    heads = width // head
    scale = 1.0 / math.sqrt(head)
    for h in range(heads):
        lanes = slice(h * head, (h + 1) * head)
        for seq in range(seqs):
            at = seq * heads + h
            dq = (dot(dscore[at], stacked(pieces, 0, seq, lanes), 0, 0) * scale).astype(BF16)
            dq_own[seq, :, lanes] = dq[:block]
            dq_send[seq, :, lanes] = dq[block:]
            dk = dot(dscore[at, : 2 * block], stacked((qg_own, qg_other), 0, seq, lanes)) * scale
            dv = dot(probs[at], stacked((qg_own, qg_other), 1, seq, lanes))
            for kind, direct in enumerate((dk, dv)):
                own[kind, seq, :, lanes] = direct[:block]
                other[kind, seq, :, lanes] = direct[block:]


def fold_body(direct, coarse, slope, *refs):
    *slopes, out, slope_out = refs
    total = slope[...]
    for ref in slopes:
        total = total + ref[...]
    slope_out[...] = total
    rows = direct.shape[2]
    for kind in range(direct.shape[0]):
        for seq in range(direct.shape[1]):
            spread = dot(spread_matrix(rows, 1), coarse[kind, seq])
            out[kind, seq] = (direct[kind, seq] + spread).astype(BF16)


def relay_body(far, back, slope, slope_out, *far_outs):
    tail = 2 * slope.shape[0]
    total = slope[...] + one_part(back[pl.ds(far.shape[0], tail), :])
    slope_out[...] = total
    ending = two_parts(total)
    start = 0
    for out in far_outs:
        rows = out.shape[0] - tail
        here = pl.ds(start, rows)
        out[pl.ds(0, rows), :] = (far[here, :] + back[here, :].astype(F32)).astype(BF16)
        out[pl.ds(rows, tail), :] = ending
        start += rows


def gather_body(levels_of, done, own, other, slope, slope_side, near, *refs):
    back, (kept, sent, slope_out) = refs[:-3], refs[-3:]
    kinds, seqs, block, width = own.shape
    heads = slope.shape[0]
    head = width // heads
    sizes = [2 * block >> level for level in levels_of[1:]]
    spread = jnp.concatenate([spread_matrix(2 * block, level) for level in levels_of], axis=1)
    for kind in range(kinds):
        for seq in range(seqs):
            for h in range(heads):
                lanes = slice(h * head, (h + 1) * head)
                group = (kind * seqs + seq) * heads + h
                cells = [near[kind, seq, :, lanes]]
                cells += [part[pl.ds(group * size, size), :] for part, size in zip(back, sizes)]
                total = dot(spread, jnp.concatenate(cells, axis=0))
                kept[kind, seq, :, lanes] = (own[kind, seq, :, lanes] + total[:block]).astype(BF16)
                sent[kind, seq, :, lanes] = (other[kind, seq, :, lanes] + total[block:]).astype(BF16)
    all_slopes = slope[...] + slope_side[...]
    for part, size in zip(back[1:], sizes[1:]):
        all_slopes = all_slopes + one_part(part[pl.ds(kinds * seqs * heads * size, 2 * heads), :])
    slope_out[...] = all_slopes


def join_body(core, own, other, out, done, sems):
    mine, theirs = head_halves(core, own.shape[-1])
    copy_all([(other, out.at[:, :, theirs]), (own, out.at[:, :, mine])], sems)
    done[...] = jnp.zeros_like(done)


def join_pair_body(core, own, other, slope, slope_other, first, second, slope_out, sums, sems):
    mine, theirs = head_halves(core, own.shape[-1])
    moves = []
    for index, out in enumerate((first, second)):
        moves.append((other.at[index], out.at[:, :, theirs]))
        moves.append((own.at[index], out.at[:, :, mine]))
    copies = start_all(moves, sems)
    ours, rest = slope[...], slope_other[...]
    lower = jnp.where(core[0] == 0, ours, rest)
    upper = jnp.where(core[0] == 0, rest, ours)
    terms = jnp.concatenate([lower, upper], axis=0)
    sums[...] = jnp.sum(terms.T, axis=0, keepdims=True)
    last = pltpu.make_async_copy(sums, slope_out, sems.at[len(moves)])
    last.start()
    for copy in (*copies, last):
        copy.wait()


def paired(queries, key_rows, value_rows, out_grad, level_slope):
    seqs, block, width = queries.shape
    heads = level_slope.shape[0]
    half, head = width // 2, width // heads
    ctx_count, dp_count = lax.axis_size("ctx"), lax.axis_size("dp")
    levels = ctx_count.bit_length() - 1
    position = lax.axis_index("ctx")
    core = (position % 2).astype(jnp.int32).reshape(1)

    part = like(2, seqs, block, half)
    k_other, v_other = swap(key_rows, 1), swap(value_rows, 1)
    cell_shapes = tuple(like(2, seqs, 2 * block >> level, half) for level in range(1, levels))
    wide = (pltpu.VMEM((2, seqs, half // 128, block, 128), F32),)
    own_cells = call(own_summary_body, cell_shapes, (core, key_rows, value_rows), "own_summaries", scalars=1, scratch=wide)
    cells = call(summary_body, cell_shapes, (core, k_other, v_other, *own_cells), "summaries", scalars=1, scratch=wide)
    qg_own, qg_send = call(
        split_body, (part, part), (core, queries, out_grad), "split_qg", scalars=1, hbm_in=2, copies=4
    )
    qg_other = swap(qg_send, 1)

    kv_own, kv_other = call(
        keep_body, (part, part), (core, key_rows, value_rows, k_other, v_other), "keep_halves", scalars=1
    )
    far = list(range(4, ctx_count // 2, 2))
    far_levels = [m.bit_length() for m in far]
    far_cells = [swap(cells[level - 1], 2 * m) for m, level in zip(far, far_levels)]
    near_cells = swap(cells[0], 2)
    side_cells = swap(cells[1], 4)
    across = call(coarser_body, like(2, seqs, block // 2, half), (near_cells,), "coarser")
    across_cells = swap(across, 4)
    far_sizes = [2 * block >> level for level in far_levels]
    relayed_cells = [swap(c, 2) for c in far_cells]

    groups = seqs * heads
    early_levels, late_levels = (0, 0), (1, 2, *far_levels)
    token_rows, cell_rows = 2 * block, block + block // 2 + sum(far_sizes)
    rows = token_rows + cell_rows + block // 2 + sum(far_sizes)

    def score(levels_of, pieces, count):
        product = like(groups // 2, count, token_rows, dtype=F32)
        return call(
            functools.partial(score_body, levels_of, head),
            (product, product, like(groups // 2, 8, token_rows, dtype=F32)),
            (core, level_slope, qg_own, qg_other, *pieces),
            "scores",
            scalars=2,
            flops=40 * seqs * token_rows * count * half,
        )

    token_pieces = [kv_own, kv_other]
    cell_pieces = [near_cells, side_cells, *far_cells]
    early = (*score(early_levels, token_pieces, token_rows), *score(late_levels, cell_pieces, cell_rows))
    runs = [(0, token_rows), (1, block), (2, block // 2), *zip(far_levels, far_sizes)]
    runs += [(2, block // 2), *zip(far_levels, far_sizes)]
    far_rows = [groups * size for size in far_sizes]
    tail = heads
    slope_part = like(heads // 2, token_rows, dtype=F32)
    wide = like(*part.shape, dtype=F32)
    slope, near, across, side, far_direct, relay, dscore, probs = call(
        functools.partial(attend_body, tuple(runs), head, tuple(far_sizes)),
        (
            slope_part,
            wide,
            like(2, seqs, block // 2, half),
            like(groups * (block // 2), head),
            like(sum(far_rows), head, dtype=F32),
            like(sum(far_rows) + tail, head),
            like(groups // 2, rows, token_rows),
            like(groups // 2, token_rows, token_rows),
        ),
        (core, level_slope, *early, qg_own, qg_other, across_cells, *relayed_cells),
        "attend",
        scalars=2,
        flops=40 * seqs * token_rows * rows * half,
        scratch=(
            pltpu.VMEM((groups // 2, block // 2 + sum(far_sizes), token_rows), F32),
            pltpu.VMEM((groups // 2, block // 2 + sum(far_sizes), token_rows), F32),
            pltpu.VMEM((groups // 2, rows - token_rows, token_rows), BF16),
        ),
    )
    dq_part = like(seqs, block, half)
    dq_own, dq_send, own, other = call(
        functools.partial(own_grads_body, head),
        (dq_part, dq_part, wide, wide),
        (dscore, probs, qg_own, qg_other, *token_pieces, *cell_pieces, across_cells, *relayed_cells),
        "own_grads",
        flops=40 * seqs * token_rows * rows * half,
    )

    across_back = swap(across, 4)
    relay_back = swap(relay, 2)
    slopes = [swap(slope, 2 * y, dp) for dp in range(1, dp_count) for y in range(2)]
    dq_other = swap(dq_send, 1)
    near_total, slope = call(
        fold_body, (like(*near.shape), slope_part), (near, across_back, slope, *slopes), "fold"
    )
    near_back = swap(near_total, 2)
    side_back = swap(side, 4)
    slope, *far_total = call(
        relay_body,
        (slope_part, *(like(r + tail, head) for r in far_rows)),
        (far_direct, relay_back, slope),
        "relay",
    )
    far_back = [swap(message, 2 * m) for m, message in zip(far, far_total)]
    whole = like(seqs, block, width)
    dq, done = call(
        join_body, (whole, slope_part), (core, dq_own, dq_other), "join_queries", scalars=1, hbm_out=1, copies=2
    )
    kept, sent, slope = call(
        functools.partial(gather_body, (1, 2, *far_levels)),
        (part, part, slope_part),
        (done, own, other, slope, swap(slope, 4), near_back, side_back, *far_back),
        "gather_cells",
    )
    kv_grad_other = swap(sent, 1)
    dk, dv, slope_grad = call(
        join_pair_body,
        (whole, whole, like(1, heads, dtype=F32)),
        (core, kept, kv_grad_other, slope, swap(slope, 1)),
        "join_kv",
        scalars=1,
        hbm_out=3,
        copies=5,
        scratch=(pltpu.VMEM((1, heads), F32),),
    )
    return dq, dk, dv, slope_grad.reshape(heads)


def as_sent(x):
    return jax.tree.map(lambda a: a.astype(jnp.bfloat16) if a.dtype == jnp.float32 else a, x)


def from_partner(value, axis, apart):
    mask = 2**apart
    pairs = [(source, source ^ mask) for source in range(lax.axis_size(axis))]
    return lax.ppermute(value, axis, pairs)


def pair_mean(cells):
    shaped = cells.reshape(cells.shape[:-2] + (cells.shape[-2] // 2, 2, cells.shape[-1])).astype(
        jnp.float32
    )
    return ((shaped[..., 0, :] + shaped[..., 1, :]) * 0.5).astype(jnp.bfloat16)


def merge_level(own_pair, other_pair, flag):
    merged = []
    for own_part, other_part in zip(own_pair, other_pair):
        own_small = pair_mean(own_part)
        other_small = pair_mean(other_part)
        merged.append(
            jnp.where(
                flag == 1,
                jnp.concatenate([other_small, own_small], axis=1),
                jnp.concatenate([own_small, other_small], axis=1),
            )
        )
    return tuple(merged)


def to_heads(rows, heads):
    seqs, count, width = rows.shape
    return jnp.transpose(rows.reshape(seqs, count, heads, width // heads), (0, 2, 1, 3))


def from_heads(split):
    seqs, heads, count, head = split.shape
    return jnp.transpose(split, (0, 2, 1, 3)).reshape(seqs, count, heads * head)


def product(form, left, right):
    return jnp.einsum(form, left, right, preferred_element_type=jnp.float32)


def attend(query_four, key_four, value_four, grad_four, level_slope, block):
    head = query_four.shape[3]
    key_count = key_four.shape[2]
    scale = 1.0 / math.sqrt(head)
    column = jnp.arange(key_count, dtype=jnp.int32)
    level_of = column // block - 1
    sibling = jnp.maximum(level_of, 0)
    multiple = jnp.where(level_of < 0, 1.0, jnp.exp2(sibling.astype(jnp.float32)))
    bias = level_slope[:, None] * sibling.astype(jnp.float32)[None, :]
    raw = product("shqd,shkd->shqk", query_four, key_four)
    scores = raw * scale + bias[None, :, None, :]
    top = jnp.max(scores, axis=-1, keepdims=True)
    weights = multiple[None, None, None, :] * jnp.exp(scores - top)
    probs = weights / jnp.sum(weights, axis=-1, keepdims=True)
    probs_low = probs.astype(jnp.bfloat16)
    output = product("shqk,shkd->shqd", probs_low, value_four)
    delta = jnp.sum(grad_four.astype(jnp.float32) * output, axis=-1)
    upstream = product("shqd,shkd->shqk", grad_four, value_four)
    dscore = probs * (upstream - delta[..., None])
    slope_part = jnp.sum(dscore * sibling.astype(jnp.float32)[None, None, None, :], axis=(0, 2, 3))
    dscore_low = dscore.astype(jnp.bfloat16)
    query_part = product("shqk,shkd->shqd", dscore_low, key_four) * scale
    key_part = product("shqk,shqd->shkd", dscore_low, query_four) * scale
    value_part = product("shqk,shqd->shkd", probs_low, grad_four)
    return (query_part, key_part, value_part, slope_part)


def split_level(grad_now, direct, flag, level, block):
    half = block // 2
    lower_src = grad_now[:, :, :half]
    upper_src = grad_now[:, :, half:]
    own_src = jnp.where(flag == 1, upper_src, lower_src)
    other_src = jnp.where(flag == 1, lower_src, upper_src)
    own_half = jnp.repeat(own_src, 2, axis=2) * 0.5
    other_half = jnp.repeat(other_src, 2, axis=2) * 0.5
    sent = (other_half + direct[:, :, (level + 1) * block : (level + 2) * block]).astype(
        jnp.bfloat16
    )
    return (own_half, sent)


def by_blocks(queries, key_rows, value_rows, out_grad, level_slope):
    seqs, block, width = queries.shape
    heads = level_slope.shape[0]
    ctx_count = lax.axis_size("ctx")
    levels = ctx_count.bit_length() - 1
    position = lax.axis_index("ctx")
    bit_list = [position // 2**level % 2 for level in range(levels)]
    own_pair = (key_rows, value_rows)
    partners = []
    for level in range(levels - 2):
        other_pair = jax.tree.map(
            lambda part, own: part.astype(own.dtype),
            from_partner(as_sent(own_pair), "ctx", level),
            own_pair,
        )
        partners.append(other_pair)
        own_pair = merge_level(own_pair, other_pair, bit_list[level])
    for level in range(levels - 2, levels):
        other_pair = jax.tree.map(
            lambda part, own: part.astype(own.dtype),
            from_partner(as_sent(own_pair), "ctx", level),
            own_pair,
        )
        partners.append(other_pair)
        if level + 1 < levels:
            own_pair = merge_level(own_pair, other_pair, bit_list[level])
    key_set = jnp.concatenate(
        [to_heads(key_rows, heads)] + [to_heads(pair[0], heads) for pair in partners], axis=2
    )
    value_set = jnp.concatenate(
        [to_heads(value_rows, heads)] + [to_heads(pair[1], heads) for pair in partners], axis=2
    )
    query_four = to_heads(queries, heads)
    grad_four = to_heads(out_grad, heads)
    query_part, key_part, value_part, slope_part = attend(
        query_four, key_set, value_set, grad_four, level_slope, block
    )
    slope_grad = lax.psum(slope_part, ("dp", "ctx"))
    head = width // heads
    grad_keys = jnp.zeros((seqs, heads, block, head), jnp.float32)
    grad_values = jnp.zeros((seqs, heads, block, head), jnp.float32)
    for level in reversed(range(levels)):
        own_keys, sent_keys = split_level(grad_keys, key_part, bit_list[level], level, block)
        own_values, sent_values = split_level(
            grad_values, value_part, bit_list[level], level, block
        )
        back_keys, back_values = from_partner((sent_keys, sent_values), "ctx", level)
        grad_keys = own_keys + back_keys.astype(jnp.float32)
        grad_values = own_values + back_values.astype(jnp.float32)
    key_grad = from_heads((grad_keys + key_part[:, :, :block]).astype(jnp.bfloat16))
    value_grad = from_heads((grad_values + value_part[:, :, :block]).astype(jnp.bfloat16))
    return (from_heads(query_part.astype(jnp.bfloat16)), key_grad, value_grad, slope_grad)


def shards(queries, key_rows, value_rows, out_grad, level_slope):
    levels = lax.axis_size("ctx").bit_length() - 1
    cells = 2 * queries.shape[1] >> levels - 1
    few = levels >= 4 and cells >= 16 and level_slope.shape[0] % 16 == 0
    form = paired if few else by_blocks
    return form(queries, key_rows, value_rows, out_grad, level_slope)


def solution(mesh):
    placed = (
        P("dp", "ctx", None),
        P("dp", "ctx", None),
        P("dp", "ctx", None),
        P("dp", "ctx", None),
        P(),
    )
    return jax.shard_map(
        shards,
        mesh=mesh,
        in_specs=placed,
        out_specs=(P("dp", "ctx", None), P("dp", "ctx", None), P("dp", "ctx", None), P()),
        check_vma=False,
    )
```

```python
import functools
import math

import jax
import jax.numpy as jnp
from jax import lax
from jax.experimental import pallas as pl
from jax.experimental.pallas import tpu as pltpu
from jax.sharding import PartitionSpec as P

F32, BF16 = jnp.float32, jnp.bfloat16
LOG2E = math.log2(math.e)
VMEM = pl.BlockSpec(memory_space=pltpu.VMEM)
SMEM = pl.BlockSpec(memory_space=pltpu.SMEM)
HBM = pl.BlockSpec(memory_space=pltpu.HBM)


def swap(value, apart, dp_apart=0):
    count = lax.axis_size("ctx")
    if not dp_apart:
        return lax.ppermute(value, "ctx", [(source, source ^ apart) for source in range(count)])
    mask = dp_apart * count + apart
    pairs = [(source, source ^ mask) for source in range(lax.axis_size("dp") * count)]
    return lax.ppermute(value, ("dp", "ctx"), pairs)


def like(*shape, dtype=BF16):
    return jax.ShapeDtypeStruct(shape, dtype)


def call(body, out_shape, operands, name, scalars=0, hbm_in=0, hbm_out=0, copies=0, flops=0, limit=32, scratch=()):
    moved = sum(a.size * a.dtype.itemsize for a in jax.tree.leaves((operands, out_shape)))
    count = len(operands) - scalars - hbm_in
    return pl.pallas_call(
        body,
        out_shape=out_shape,
        in_specs=[SMEM] * scalars + [HBM] * hbm_in + [VMEM] * count,
        out_specs=tuple(HBM if i < hbm_out else VMEM for i in range(len(out_shape)))
        if isinstance(out_shape, tuple)
        else VMEM,
        scratch_shapes=[*scratch, *([pltpu.SemaphoreType.DMA((copies,))] if copies else [])],
        compiler_params=pltpu.CompilerParams(vmem_limit_bytes=int(limit * 2**20)),
        cost_estimate=pl.CostEstimate(flops=flops, bytes_accessed=moved, transcendentals=0),
        name=name,
    )(*operands)


def dot(left, right, left_dim=1, right_dim=0):
    dims = (((left_dim,), (right_dim,)), ((), ()))
    return lax.dot_general(left, right, dims, preferred_element_type=F32)


def pair_matrix(rows):
    cell = lax.broadcasted_iota(jnp.int32, (rows, 2 * rows), 0)
    source = lax.broadcasted_iota(jnp.int32, (rows, 2 * rows), 1)
    return jnp.where(source // 2 == cell, 0.5, 0.0).astype(BF16)


def spread_matrix(rows, level):
    row = lax.broadcasted_iota(jnp.int32, (rows, rows >> level), 0)
    cell = lax.broadcasted_iota(jnp.int32, (rows, rows >> level), 1)
    return jnp.where(row >> level == cell, 0.5**level, 0.0).astype(BF16)


def two_parts(x):
    high = x.astype(BF16)
    return jnp.concatenate([high, (x - high.astype(F32)).astype(BF16)], axis=0)


def one_part(x):
    rows = x.shape[0] // 2
    return x[:rows].astype(F32) + x[rows:].astype(F32)


def head_halves(core, half):
    mine = pl.ds(pl.multiple_of(core[0] * half, half), half)
    theirs = pl.ds(pl.multiple_of((1 - core[0]) * half, half), half)
    return mine, theirs


def start_all(moves, sems):
    copies = [pltpu.make_async_copy(src, dst, sems.at[i]) for i, (src, dst) in enumerate(moves)]
    for copy in copies:
        copy.start()
    return copies


def copy_all(moves, sems):
    for copy in start_all(moves, sems):
        copy.wait()


def split_body(core, first, second, own, send, sems):
    mine, theirs = head_halves(core, own.shape[-1])
    moves = []
    for index, whole in enumerate((first, second)):
        moves.append((whole.at[:, :, theirs], send.at[index]))
        moves.append((whole.at[:, :, mine], own.at[index]))
    copy_all(moves, sems)


def keep_body(core, k, v, k_other, v_other, own, other):
    mine, _ = head_halves(core, own.shape[-1])
    for index, (first, second) in enumerate(((k, k_other), (v, v_other))):
        own[index] = first[:, :, mine]
        other[index] = second[:, :, mine]


def halve(rows, wide):
    count = rows.shape[0]
    wide[pl.ds(0, count), :] = rows
    return (wide[pl.ds(0, count // 2, stride=2), :] + wide[pl.ds(1, count // 2, stride=2), :]) * 0.5


def tiles_of(shape, core, wide):
    kinds, seqs, _, half = shape
    for kind in range(kinds):
        for seq in range(seqs):
            for start in range(0, half, 128):
                source = pl.ds(pl.multiple_of(core[0] * half + start, 128), 128)
                yield kind, seq, source, slice(start, start + 128), wide.at[kind, seq, start // 128]


def own_summary_body(core, k, v, *refs):
    *cells, wide = refs
    for kind, seq, source, lanes, scratch in tiles_of(cells[0].shape, core, wide):
        rows = (k, v)[kind][seq, :, source].astype(F32)
        for out in cells:
            rows = halve(rows, scratch)
            out[kind, seq, :, lanes] = jnp.concatenate([rows, jnp.zeros_like(rows)], axis=0).astype(BF16)
            rows = rows.astype(BF16).astype(F32)


def summary_body(core, k_other, v_other, *refs):
    *refs, wide = refs
    own, cells = refs[: len(refs) // 2], refs[len(refs) // 2 :]
    for kind, seq, source, lanes, scratch in tiles_of(cells[0].shape, core, wide):
        rows = (k_other, v_other)[kind][seq, :, source].astype(F32)
        for first, out in zip(own, cells):
            rows = halve(rows, scratch)
            before = first[kind, seq, :, lanes].astype(F32)[: rows.shape[0]]
            out[kind, seq, :, lanes] = jnp.concatenate([before, rows], axis=0).astype(BF16)
            rows = rows.astype(BF16).astype(F32)


def coarser_body(cells, out):
    for kind in range(cells.shape[0]):
        for seq in range(cells.shape[1]):
            rows = cells[kind, seq]
            out[kind, seq] = dot(pair_matrix(rows.shape[0] // 2), rows).astype(BF16)


def stacked(parts, kind, seq, lanes):
    return jnp.concatenate([part[kind, seq, :, lanes] for part in parts], axis=0)


def score_body(levels_of, head, core, slope, qg_own, qg_other, *refs):
    *pieces, weights, upstream, stats = refs
    seqs, width = qg_own.shape[1], qg_own.shape[3]
    heads = width // head
    scale = LOG2E / math.sqrt(head)
    for h in range(heads):
        lanes = slice(h * head, (h + 1) * head)
        step = slope[core[0] * heads + h] * LOG2E + 1.0
        for seq in range(seqs):
            at = seq * heads + h
            raw = dot(stacked(pieces, 0, seq, lanes), stacked((qg_own, qg_other), 0, seq, lanes), 1, 1)
            upstream[at] = dot(stacked(pieces, 1, seq, lanes), stacked((qg_own, qg_other), 1, seq, lanes), 1, 1)
            scores = with_bias(raw * scale, zip(levels_of, [piece.shape[2] for piece in pieces]), step)
            top = jnp.max(scores, axis=0, keepdims=True)
            spread = jnp.exp2(scores - top)
            weights[at] = spread
            stats[at, 0:1] = top
            stats[at, 1:2] = jnp.sum(spread, axis=0, keepdims=True)


def with_bias(scores, runs, step):
    parts, start = [], 0
    for level, count in runs:
        part = scores[start : start + count]
        parts.append(part + step * float(level) if level else part)
        start += count
    return jnp.concatenate(parts, axis=0)


def attend_body(runs, head, far_sizes, core, slope, *refs):
    *refs, late_scores, late_up, probs_cells = refs
    early, (qg_own, qg_other, *late), outs = refs[:6], refs[6:-8], refs[-8:]
    slope_out, near, across, side, far, relay, dscore_out, probs_out = outs
    seqs, block, width = qg_own.shape[1:]
    heads = width // head
    scale = 1.0 / math.sqrt(head)
    starts = [sum(rows for _, rows in runs[:i]) for i in range(len(runs) + 1)]
    token_rows = early[0].shape[1]
    early_rows = token_rows + early[3].shape[1]
    bounds = (0, token_rows, early_rows, starts[-1])
    late_runs = [run for run, start in zip(runs, starts) if start >= early_rows]
    far_count = len(far_sizes)
    slabs = [2 * seqs * heads * sum(far_sizes[:i]) for i in range(far_count)]

    def score(h, seq):
        at, lanes = seq * heads + h, slice(h * head, (h + 1) * head)
        step = slope[core[0] * heads + h] * LOG2E + 1.0
        raw = dot(stacked(late, 0, seq, lanes), stacked((qg_own, qg_other), 0, seq, lanes), 1, 1)
        late_scores[at] = with_bias(raw * (scale * LOG2E), late_runs, step)
        late_up[at] = dot(stacked(late, 1, seq, lanes), stacked((qg_own, qg_other), 1, seq, lanes), 1, 1)

    def normalise(h, seq):
        at = seq * heads + h
        tops = early[2][at, 0:1], early[5][at, 0:1]
        scores = late_scores[at]
        top = jnp.maximum(jnp.maximum(*tops), jnp.max(scores, axis=0, keepdims=True))
        shares = [jnp.exp2(part - top) for part in tops]
        weights = jnp.exp2(scores - top)
        total = early[2][at, 1:2] * shares[0] + early[5][at, 1:2] * shares[1]
        inverse = 1.0 / (total + jnp.sum(weights, axis=0, keepdims=True))
        probs = [early[0][at] * (shares[0] * inverse), early[3][at] * (shares[1] * inverse), weights * inverse]
        upstream = [early[1][at], early[4][at], late_up[at]]
        probs_low = [part.astype(BF16) for part in probs]
        delta = sum(jnp.sum(p.astype(F32) * u, axis=0, keepdims=True) for p, u in zip(probs_low, upstream))
        slope_sum = jnp.zeros_like(delta)
        for p, u, low, high in zip(probs, upstream, bounds, bounds[1:]):
            dscore = p * (u - delta)
            for (level, rows), start in zip(runs, starts):
                if level and low <= start < high:
                    here = dscore[start - low : start - low + rows]
                    slope_sum = slope_sum + jnp.sum(here, axis=0, keepdims=True) * float(level)
            dscore_out[at, low:high] = dscore.astype(BF16)
        probs_out[at] = probs_low[0]
        probs_cells[at] = jnp.concatenate(probs_low[1:], axis=0)
        return slope_sum

    def gradients(h, seq):
        at, lanes = seq * heads + h, slice(h * head, (h + 1) * head)
        dk = dot(dscore_out[at, token_rows:], stacked((qg_own, qg_other), 0, seq, lanes)) * scale
        dv = dot(probs_cells[at], stacked((qg_own, qg_other), 1, seq, lanes))
        for kind, direct in enumerate((dk, dv)):
            parts = [direct[starts[i] - token_rows : starts[i + 1] - token_rows] for i in range(1, len(runs))]
            group = (kind * seqs + seq) * heads + h
            near[kind, seq, :, lanes] = parts[0]
            side[pl.ds(group * (block // 2), block // 2), :] = parts[1].astype(BF16)
            across[kind, seq, :, lanes] = parts[2 + far_count].astype(BF16)
            for i, size in enumerate(far_sizes):
                here = pl.ds(slabs[i] + group * size, size)
                far[here, :] = parts[2 + i]
                relay[here, :] = parts[3 + far_count + i].astype(BF16)

    items = [(h, seq) for h in range(heads) for seq in range(seqs)]
    behind = 2
    sums = {}
    for i in range(len(items) + 2 * behind):
        if i < len(items):
            score(*items[i])
        if 0 <= i - behind < len(items):
            item = items[i - behind]
            sums[item] = normalise(*item)
        if 0 <= i - 2 * behind < len(items):
            gradients(*items[i - 2 * behind])
    for h in range(heads):
        slope_out[h : h + 1, :] = sum(sums[h, seq] for seq in range(seqs))
    relay[pl.ds(far.shape[0], 2 * heads), :] = two_parts(slope_out[...])


def own_grads_body(head, dscore, probs, qg_own, qg_other, *refs):
    *pieces, dq_own, dq_send, own, other = refs
    seqs, block, width = qg_own.shape[1:]
    heads = width // head
    scale = 1.0 / math.sqrt(head)
    for h in range(heads):
        lanes = slice(h * head, (h + 1) * head)
        for seq in range(seqs):
            at = seq * heads + h
            dq = (dot(dscore[at], stacked(pieces, 0, seq, lanes), 0, 0) * scale).astype(BF16)
            dq_own[seq, :, lanes] = dq[:block]
            dq_send[seq, :, lanes] = dq[block:]
            dk = dot(dscore[at, : 2 * block], stacked((qg_own, qg_other), 0, seq, lanes)) * scale
            dv = dot(probs[at], stacked((qg_own, qg_other), 1, seq, lanes))
            for kind, direct in enumerate((dk, dv)):
                own[kind, seq, :, lanes] = direct[:block]
                other[kind, seq, :, lanes] = direct[block:]


def fold_body(direct, coarse, done, out):
    rows = direct.shape[2]
    for kind in range(direct.shape[0]):
        for seq in range(direct.shape[1]):
            spread = dot(spread_matrix(rows, 1), coarse[kind, seq])
            out[kind, seq] = (direct[kind, seq] + spread).astype(BF16)


def relay_body(far, back, slope, *refs):
    *slopes, slope_out, keep, message = refs
    rows = keep.shape[0]
    total = slope[...] + one_part(back[pl.ds(2 * rows, 2 * slope.shape[0]), :])
    for ref in slopes:
        total = total + ref[...]
    slope_out[...] = total
    keep[...] = far[pl.ds(0, rows), :] + back[pl.ds(0, rows), :].astype(F32)
    message[pl.ds(0, rows), :] = (far[pl.ds(rows, rows), :] + back[pl.ds(rows, rows), :].astype(F32)).astype(BF16)
    message[pl.ds(rows, 2 * slope.shape[0]), :] = two_parts(total)


def meet_body(keep, back, slope, slope_out, message):
    rows = keep.shape[0]
    total = slope[...] + one_part(back[pl.ds(rows, 2 * slope.shape[0]), :])
    slope_out[...] = total
    message[pl.ds(0, rows), :] = (keep[...] + back[pl.ds(0, rows), :].astype(F32)).astype(BF16)
    message[pl.ds(rows, 2 * slope.shape[0]), :] = two_parts(total)


def gather_body(levels_of, done, own, other, slope, near, *refs):
    back, (kept, sent, slope_out) = refs[:-3], refs[-3:]
    kinds, seqs, block, width = own.shape
    heads = slope.shape[0]
    head = width // heads
    sizes = [2 * block >> level for level in levels_of[1:]]
    spread = jnp.concatenate([spread_matrix(2 * block, level) for level in levels_of], axis=1)
    for kind in range(kinds):
        for seq in range(seqs):
            for h in range(heads):
                lanes = slice(h * head, (h + 1) * head)
                group = (kind * seqs + seq) * heads + h
                cells = [near[kind, seq, :, lanes]]
                cells += [part[pl.ds(group * size, size), :] for part, size in zip(back, sizes)]
                total = dot(spread, jnp.concatenate(cells, axis=0))
                kept[kind, seq, :, lanes] = (own[kind, seq, :, lanes] + total[:block]).astype(BF16)
                sent[kind, seq, :, lanes] = (other[kind, seq, :, lanes] + total[block:]).astype(BF16)
    far, size = back[-1], sizes[-1]
    slope_out[...] = slope[...] + one_part(far[pl.ds(kinds * seqs * heads * size, 2 * heads), :])


def join_body(core, own, other, out, done, sems):
    mine, theirs = head_halves(core, own.shape[-1])
    copy_all([(other, out.at[:, :, theirs]), (own, out.at[:, :, mine])], sems)
    done[...] = jnp.zeros_like(done)


def join_pair_body(core, own, other, slope, slope_other, first, second, slope_out, sums, sems):
    mine, theirs = head_halves(core, own.shape[-1])
    moves = []
    for index, out in enumerate((first, second)):
        moves.append((other.at[index], out.at[:, :, theirs]))
        moves.append((own.at[index], out.at[:, :, mine]))
    copies = start_all(moves, sems)
    ours, rest = slope[...], slope_other[...]
    lower = jnp.where(core[0] == 0, ours, rest)
    upper = jnp.where(core[0] == 0, rest, ours)
    terms = jnp.concatenate([lower, upper], axis=0)
    sums[...] = jnp.sum(terms.T, axis=0, keepdims=True)
    last = pltpu.make_async_copy(sums, slope_out, sems.at[len(moves)])
    last.start()
    for copy in (*copies, last):
        copy.wait()


def paired(queries, key_rows, value_rows, out_grad, level_slope):
    seqs, block, width = queries.shape
    heads = level_slope.shape[0]
    half, head = width // 2, width // heads
    dp_count = lax.axis_size("dp")
    levels = 4
    position = lax.axis_index("ctx")
    core = (position % 2).astype(jnp.int32).reshape(1)

    part = like(2, seqs, block, half)
    k_other, v_other = swap(key_rows, 1), swap(value_rows, 1)
    cell_shapes = tuple(like(2, seqs, 2 * block >> level, half) for level in range(1, levels))
    wide = (pltpu.VMEM((2, seqs, half // 128, block, 128), F32),)
    own_cells = call(own_summary_body, cell_shapes, (core, key_rows, value_rows), "own_summaries", scalars=1, scratch=wide)
    cells = call(summary_body, cell_shapes, (core, k_other, v_other, *own_cells), "summaries", scalars=1, scratch=wide)
    qg_own, qg_send = call(
        split_body, (part, part), (core, queries, out_grad), "split_qg", scalars=1, hbm_in=2, copies=4
    )
    qg_other = swap(qg_send, 1)

    kv_own, kv_other = call(
        keep_body, (part, part), (core, key_rows, value_rows, k_other, v_other), "keep_halves", scalars=1
    )
    near_cells = swap(cells[0], 2)
    far_cells = swap(cells[2], 8)
    side_cells = swap(cells[1], 4)
    across_cells = swap(call(coarser_body, like(2, seqs, block // 2, half), (near_cells,), "coarser"), 4)
    far_side_cells = swap(far_cells, 4)
    relayed_cells = [swap(far_cells, 2), swap(far_side_cells, 2)]

    groups = seqs * heads
    far_size = block // 4
    token_rows, cell_rows, late_rows = 2 * block, 2 * block, block
    rows = token_rows + cell_rows + late_rows

    def score(levels_of, pieces, count):
        product = like(groups // 2, count, token_rows, dtype=F32)
        return call(
            functools.partial(score_body, levels_of, head),
            (product, product, like(groups // 2, 8, token_rows, dtype=F32)),
            (core, level_slope, qg_own, qg_other, *pieces),
            "scores",
            scalars=2,
            flops=40 * seqs * token_rows * count * half,
        )

    token_pieces = [kv_own, kv_other]
    cell_pieces = [near_cells, side_cells, far_cells, far_side_cells]
    late_pieces = [across_cells, *relayed_cells]
    early = (*score((0, 0), token_pieces, token_rows), *score((1, 2, 3, 3), cell_pieces, cell_rows))
    runs = ((0, token_rows), (1, block), (2, block // 2), (3, far_size), (3, far_size))
    runs += ((2, block // 2), (3, far_size), (3, far_size))
    far_rows, tail = groups * far_size, heads
    slope_part = like(heads // 2, token_rows, dtype=F32)
    wide = like(*part.shape, dtype=F32)
    slope, near, across, side, far_direct, relay, dscore, probs = call(
        functools.partial(attend_body, runs, head, (far_size, far_size)),
        (
            slope_part,
            wide,
            like(2, seqs, block // 2, half),
            like(groups * (block // 2), head),
            like(2 * far_rows, head, dtype=F32),
            like(2 * far_rows + tail, head),
            like(groups // 2, rows, token_rows),
            like(groups // 2, token_rows, token_rows),
        ),
        (core, level_slope, *early, qg_own, qg_other, *late_pieces),
        "attend",
        scalars=2,
        flops=40 * seqs * token_rows * rows * half,
        scratch=(
            pltpu.VMEM((groups // 2, late_rows, token_rows), F32),
            pltpu.VMEM((groups // 2, late_rows, token_rows), F32),
            pltpu.VMEM((groups // 2, rows - token_rows, token_rows), BF16),
        ),
    )
    dq_part = like(seqs, block, half)
    dq_own, dq_send, own, other = call(
        functools.partial(own_grads_body, head),
        (dq_part, dq_part, wide, wide),
        (dscore, probs, qg_own, qg_other, *token_pieces, *cell_pieces, *late_pieces),
        "own_grads",
        flops=40 * seqs * token_rows * rows * half,
    )

    across_back = swap(across, 4)
    relay_back = swap(relay, 2)
    slopes = [swap(slope, 2 * y, dp) for dp in range(1, dp_count) for y in range(2)]
    dq_other = swap(dq_send, 1)
    message = like(far_rows + tail, head)
    slope, keep, far_side = call(
        relay_body,
        (slope_part, like(far_rows, head, dtype=F32), message),
        (far_direct, relay_back, slope, *slopes),
        "relay",
    )
    far_side_back = swap(far_side, 4)
    near_back = swap(call(fold_body, like(*near.shape), (near, across_back, slope), "fold"), 2)
    side_back = swap(side, 4)
    slope, far_total = call(meet_body, (slope_part, message), (keep, far_side_back, slope), "meet")
    far_back = swap(far_total, 8)
    whole = like(seqs, block, width)
    dq, done = call(
        join_body, (whole, slope_part), (core, dq_own, dq_other), "join_queries", scalars=1, hbm_out=1, copies=2
    )
    kept, sent, slope = call(
        functools.partial(gather_body, (1, 2, 3)),
        (part, part, slope_part),
        (done, own, other, slope, near_back, side_back, far_back),
        "gather_cells",
    )
    kv_grad_other = swap(sent, 1)
    dk, dv, slope_grad = call(
        join_pair_body,
        (whole, whole, like(1, heads, dtype=F32)),
        (core, kept, kv_grad_other, slope, swap(slope, 1)),
        "join_kv",
        scalars=1,
        hbm_out=3,
        copies=5,
        scratch=(pltpu.VMEM((1, heads), F32),),
    )
    return dq, dk, dv, slope_grad.reshape(heads)


def as_sent(x):
    return jax.tree.map(lambda a: a.astype(jnp.bfloat16) if a.dtype == jnp.float32 else a, x)


def from_partner(value, axis, apart):
    mask = 2**apart
    pairs = [(source, source ^ mask) for source in range(lax.axis_size(axis))]
    return lax.ppermute(value, axis, pairs)


def pair_mean(cells):
    shaped = cells.reshape(cells.shape[:-2] + (cells.shape[-2] // 2, 2, cells.shape[-1])).astype(
        jnp.float32
    )
    return ((shaped[..., 0, :] + shaped[..., 1, :]) * 0.5).astype(jnp.bfloat16)


def merge_level(own_pair, other_pair, flag):
    merged = []
    for own_part, other_part in zip(own_pair, other_pair):
        own_small = pair_mean(own_part)
        other_small = pair_mean(other_part)
        merged.append(
            jnp.where(
                flag == 1,
                jnp.concatenate([other_small, own_small], axis=1),
                jnp.concatenate([own_small, other_small], axis=1),
            )
        )
    return tuple(merged)


def to_heads(rows, heads):
    seqs, count, width = rows.shape
    return jnp.transpose(rows.reshape(seqs, count, heads, width // heads), (0, 2, 1, 3))


def from_heads(split):
    seqs, heads, count, head = split.shape
    return jnp.transpose(split, (0, 2, 1, 3)).reshape(seqs, count, heads * head)


def product(form, left, right):
    return jnp.einsum(form, left, right, preferred_element_type=jnp.float32)


def attend(query_four, key_four, value_four, grad_four, level_slope, block):
    head = query_four.shape[3]
    key_count = key_four.shape[2]
    scale = 1.0 / math.sqrt(head)
    column = jnp.arange(key_count, dtype=jnp.int32)
    level_of = column // block - 1
    sibling = jnp.maximum(level_of, 0)
    multiple = jnp.where(level_of < 0, 1.0, jnp.exp2(sibling.astype(jnp.float32)))
    bias = level_slope[:, None] * sibling.astype(jnp.float32)[None, :]
    raw = product("shqd,shkd->shqk", query_four, key_four)
    scores = raw * scale + bias[None, :, None, :]
    top = jnp.max(scores, axis=-1, keepdims=True)
    weights = multiple[None, None, None, :] * jnp.exp(scores - top)
    probs = weights / jnp.sum(weights, axis=-1, keepdims=True)
    probs_low = probs.astype(jnp.bfloat16)
    output = product("shqk,shkd->shqd", probs_low, value_four)
    delta = jnp.sum(grad_four.astype(jnp.float32) * output, axis=-1)
    upstream = product("shqd,shkd->shqk", grad_four, value_four)
    dscore = probs * (upstream - delta[..., None])
    slope_part = jnp.sum(dscore * sibling.astype(jnp.float32)[None, None, None, :], axis=(0, 2, 3))
    dscore_low = dscore.astype(jnp.bfloat16)
    query_part = product("shqk,shkd->shqd", dscore_low, key_four) * scale
    key_part = product("shqk,shqd->shkd", dscore_low, query_four) * scale
    value_part = product("shqk,shqd->shkd", probs_low, grad_four)
    return (query_part, key_part, value_part, slope_part)


def split_level(grad_now, direct, flag, level, block):
    half = block // 2
    lower_src = grad_now[:, :, :half]
    upper_src = grad_now[:, :, half:]
    own_src = jnp.where(flag == 1, upper_src, lower_src)
    other_src = jnp.where(flag == 1, lower_src, upper_src)
    own_half = jnp.repeat(own_src, 2, axis=2) * 0.5
    other_half = jnp.repeat(other_src, 2, axis=2) * 0.5
    sent = (other_half + direct[:, :, (level + 1) * block : (level + 2) * block]).astype(
        jnp.bfloat16
    )
    return (own_half, sent)


def by_blocks(queries, key_rows, value_rows, out_grad, level_slope):
    seqs, block, width = queries.shape
    heads = level_slope.shape[0]
    ctx_count = lax.axis_size("ctx")
    levels = ctx_count.bit_length() - 1
    position = lax.axis_index("ctx")
    bit_list = [position // 2**level % 2 for level in range(levels)]
    own_pair = (key_rows, value_rows)
    partners = []
    for level in range(levels - 2):
        other_pair = jax.tree.map(
            lambda part, own: part.astype(own.dtype),
            from_partner(as_sent(own_pair), "ctx", level),
            own_pair,
        )
        partners.append(other_pair)
        own_pair = merge_level(own_pair, other_pair, bit_list[level])
    for level in range(levels - 2, levels):
        other_pair = jax.tree.map(
            lambda part, own: part.astype(own.dtype),
            from_partner(as_sent(own_pair), "ctx", level),
            own_pair,
        )
        partners.append(other_pair)
        if level + 1 < levels:
            own_pair = merge_level(own_pair, other_pair, bit_list[level])
    key_set = jnp.concatenate(
        [to_heads(key_rows, heads)] + [to_heads(pair[0], heads) for pair in partners], axis=2
    )
    value_set = jnp.concatenate(
        [to_heads(value_rows, heads)] + [to_heads(pair[1], heads) for pair in partners], axis=2
    )
    query_four = to_heads(queries, heads)
    grad_four = to_heads(out_grad, heads)
    query_part, key_part, value_part, slope_part = attend(
        query_four, key_set, value_set, grad_four, level_slope, block
    )
    slope_grad = lax.psum(slope_part, ("dp", "ctx"))
    head = width // heads
    grad_keys = jnp.zeros((seqs, heads, block, head), jnp.float32)
    grad_values = jnp.zeros((seqs, heads, block, head), jnp.float32)
    for level in reversed(range(levels)):
        own_keys, sent_keys = split_level(grad_keys, key_part, bit_list[level], level, block)
        own_values, sent_values = split_level(
            grad_values, value_part, bit_list[level], level, block
        )
        back_keys, back_values = from_partner((sent_keys, sent_values), "ctx", level)
        grad_keys = own_keys + back_keys.astype(jnp.float32)
        grad_values = own_values + back_values.astype(jnp.float32)
    key_grad = from_heads((grad_keys + key_part[:, :, :block]).astype(jnp.bfloat16))
    value_grad = from_heads((grad_values + value_part[:, :, :block]).astype(jnp.bfloat16))
    return (from_heads(query_part.astype(jnp.bfloat16)), key_grad, value_grad, slope_grad)


def shards(queries, key_rows, value_rows, out_grad, level_slope):
    few = lax.axis_size("ctx") == 16 and queries.shape[1] % 64 == 0 and level_slope.shape[0] % 16 == 0
    form = paired if few else by_blocks
    return form(queries, key_rows, value_rows, out_grad, level_slope)


def solution(mesh):
    placed = (
        P("dp", "ctx", None),
        P("dp", "ctx", None),
        P("dp", "ctx", None),
        P("dp", "ctx", None),
        P(),
    )
    return jax.shard_map(
        shards,
        mesh=mesh,
        in_specs=placed,
        out_specs=(P("dp", "ctx", None), P("dp", "ctx", None), P("dp", "ctx", None), P()),
        check_vma=False,
    )
```

```python
import functools
import math

import jax
import jax.numpy as jnp
from jax import lax
from jax.experimental import pallas as pl
from jax.experimental.pallas import tpu as pltpu
from jax.sharding import PartitionSpec as P

F32, BF16 = jnp.float32, jnp.bfloat16
LOG2E = math.log2(math.e)
VMEM = pl.BlockSpec(memory_space=pltpu.VMEM)
SMEM = pl.BlockSpec(memory_space=pltpu.SMEM)
HBM = pl.BlockSpec(memory_space=pltpu.HBM)


def swap(value, apart, dp_apart=0):
    count = lax.axis_size("ctx")
    if not dp_apart:
        return lax.ppermute(value, "ctx", [(source, source ^ apart) for source in range(count)])
    mask = dp_apart * count + apart
    pairs = [(source, source ^ mask) for source in range(lax.axis_size("dp") * count)]
    return lax.ppermute(value, ("dp", "ctx"), pairs)


def like(*shape, dtype=BF16):
    return jax.ShapeDtypeStruct(shape, dtype)


def call(body, out_shape, operands, name, scalars=0, hbm_in=0, hbm_out=0, copies=0, flops=0, limit=32, scratch=()):
    moved = sum(a.size * a.dtype.itemsize for a in jax.tree.leaves((operands, out_shape)))
    count = len(operands) - scalars - hbm_in
    return pl.pallas_call(
        body,
        out_shape=out_shape,
        in_specs=[SMEM] * scalars + [HBM] * hbm_in + [VMEM] * count,
        out_specs=tuple(HBM if i < hbm_out else VMEM for i in range(len(out_shape)))
        if isinstance(out_shape, tuple)
        else VMEM,
        scratch_shapes=[*scratch, *([pltpu.SemaphoreType.DMA((copies,))] if copies else [])],
        compiler_params=pltpu.CompilerParams(vmem_limit_bytes=int(limit * 2**20)),
        cost_estimate=pl.CostEstimate(flops=flops, bytes_accessed=moved, transcendentals=0),
        name=name,
    )(*operands)


def dot(left, right, left_dim=1, right_dim=0):
    dims = (((left_dim,), (right_dim,)), ((), ()))
    return lax.dot_general(left, right, dims, preferred_element_type=F32)


def pair_matrix(rows):
    cell = lax.broadcasted_iota(jnp.int32, (rows, 2 * rows), 0)
    source = lax.broadcasted_iota(jnp.int32, (rows, 2 * rows), 1)
    return jnp.where(source // 2 == cell, 0.5, 0.0).astype(BF16)


def spread_matrix(rows, level):
    row = lax.broadcasted_iota(jnp.int32, (rows, rows >> level), 0)
    cell = lax.broadcasted_iota(jnp.int32, (rows, rows >> level), 1)
    return jnp.where(row >> level == cell, 0.5**level, 0.0).astype(BF16)


def two_parts(x):
    high = x.astype(BF16)
    return jnp.concatenate([high, (x - high.astype(F32)).astype(BF16)], axis=0)


def one_part(x):
    rows = x.shape[0] // 2
    return x[:rows].astype(F32) + x[rows:].astype(F32)


def head_halves(core, half):
    mine = pl.ds(pl.multiple_of(core[0] * half, half), half)
    theirs = pl.ds(pl.multiple_of((1 - core[0]) * half, half), half)
    return mine, theirs


def start_all(moves, sems):
    copies = [pltpu.make_async_copy(src, dst, sems.at[i]) for i, (src, dst) in enumerate(moves)]
    for copy in copies:
        copy.start()
    return copies


def copy_all(moves, sems):
    for copy in start_all(moves, sems):
        copy.wait()


def split_body(core, first, second, own, send, sems):
    mine, theirs = head_halves(core, own.shape[-1])
    moves = []
    for index, whole in enumerate((first, second)):
        moves.append((whole.at[:, :, theirs], send.at[index]))
        moves.append((whole.at[:, :, mine], own.at[index]))
    copy_all(moves, sems)


def keep_body(core, k, v, k_other, v_other, own, other):
    mine, _ = head_halves(core, own.shape[-1])
    for index, (first, second) in enumerate(((k, k_other), (v, v_other))):
        own[index] = first[:, :, mine]
        other[index] = second[:, :, mine]


def halve(rows, wide):
    count = rows.shape[0]
    wide[pl.ds(0, count), :] = rows
    return (wide[pl.ds(0, count // 2, stride=2), :] + wide[pl.ds(1, count // 2, stride=2), :]) * 0.5


def tiles_of(shape, core, wide):
    kinds, seqs, _, half = shape
    for kind in range(kinds):
        for seq in range(seqs):
            for start in range(0, half, 128):
                source = pl.ds(pl.multiple_of(core[0] * half + start, 128), 128)
                yield kind, seq, source, slice(start, start + 128), wide.at[kind, seq, start // 128]


def own_summary_body(core, k, v, *refs):
    *cells, wide = refs
    for kind, seq, source, lanes, scratch in tiles_of(cells[0].shape, core, wide):
        rows = (k, v)[kind][seq, :, source].astype(F32)
        for out in cells:
            rows = halve(rows, scratch)
            out[kind, seq, :, lanes] = jnp.concatenate([rows, jnp.zeros_like(rows)], axis=0).astype(BF16)
            rows = rows.astype(BF16).astype(F32)


def summary_body(core, k_other, v_other, *refs):
    *refs, wide = refs
    own, cells = refs[: len(refs) // 2], refs[len(refs) // 2 :]
    for kind, seq, source, lanes, scratch in tiles_of(cells[0].shape, core, wide):
        rows = (k_other, v_other)[kind][seq, :, source].astype(F32)
        for first, out in zip(own, cells):
            rows = halve(rows, scratch)
            before = first[kind, seq, :, lanes].astype(F32)[: rows.shape[0]]
            out[kind, seq, :, lanes] = jnp.concatenate([before, rows], axis=0).astype(BF16)
            rows = rows.astype(BF16).astype(F32)


def coarser_body(cells, out):
    for kind in range(cells.shape[0]):
        for seq in range(cells.shape[1]):
            rows = cells[kind, seq]
            out[kind, seq] = dot(pair_matrix(rows.shape[0] // 2), rows).astype(BF16)


def stacked(parts, kind, seq, lanes):
    return jnp.concatenate([part[kind, seq, :, lanes] for part in parts], axis=0)


def turn_body(head, qg_own, qg_other, turned):
    kinds, seqs, _, width = qg_own.shape
    heads = width // head
    for kind in range(kinds):
        for h in range(heads):
            for seq in range(seqs):
                lanes = slice(h * head, (h + 1) * head)
                turned[kind, seq * heads + h] = stacked((qg_own, qg_other), kind, seq, lanes).T


def score_body(levels_of, head, core, slope, turned, *refs):
    *pieces, weights, upstream, stats = refs
    seqs, width = pieces[0].shape[1], pieces[0].shape[3]
    heads = width // head
    scale = LOG2E / math.sqrt(head)
    for h in range(heads):
        lanes = slice(h * head, (h + 1) * head)
        step = slope[core[0] * heads + h] * LOG2E + 1.0
        for seq in range(seqs):
            at = seq * heads + h
            raw = dot(stacked(pieces, 0, seq, lanes), turned[0, at])
            upstream[at] = dot(stacked(pieces, 1, seq, lanes), turned[1, at])
            scores = with_bias(raw * scale, zip(levels_of, [piece.shape[2] for piece in pieces]), step)
            top = jnp.max(scores, axis=0, keepdims=True)
            spread = jnp.exp2(scores - top)
            weights[at] = spread
            stats[at, 0:1] = top
            stats[at, 1:2] = jnp.sum(spread, axis=0, keepdims=True)


def with_bias(scores, runs, step):
    parts, start = [], 0
    for level, count in runs:
        part = scores[start : start + count]
        parts.append(part + step * float(level) if level else part)
        start += count
    return jnp.concatenate(parts, axis=0)


def by_eights(x):
    return jnp.sum(x.reshape(x.shape[0] // 8, 8, x.shape[1]), axis=0)


def attend_body(runs, head, core, slope, *refs):
    *refs, late_scores, late_up = refs
    early, (turned, qg_own, qg_other, *late), outs = refs[:6], refs[6:-5], refs[-5:]
    slope_out, across, relay, dscore_out, probs_out = outs
    seqs, block, width = qg_own.shape[1:]
    heads = width // head
    scale = 1.0 / math.sqrt(head)
    starts = [sum(rows for _, rows in runs[:i]) for i in range(len(runs) + 1)]
    token_rows = early[0].shape[1]
    early_rows = token_rows + early[3].shape[1]
    bounds = (0, token_rows, early_rows, starts[-1])
    late_runs = [run for run, start in zip(runs, starts) if start >= early_rows]
    sent_rows, far_size = starts[-4], runs[-1][1]
    slab = 2 * seqs * heads * far_size

    def score(h, seq):
        at, lanes = seq * heads + h, slice(h * head, (h + 1) * head)
        step = slope[core[0] * heads + h] * LOG2E + 1.0
        raw = dot(stacked(late, 0, seq, lanes), turned[0, at])
        late_scores[at] = with_bias(raw * (scale * LOG2E), late_runs, step)
        late_up[at] = dot(stacked(late, 1, seq, lanes), turned[1, at])

    def normalise(h, seq):
        at = seq * heads + h
        tops = early[2][at, 0:1], early[5][at, 0:1]
        scores = late_scores[at]
        top = jnp.maximum(jnp.maximum(*tops), jnp.max(scores, axis=0, keepdims=True))
        shares = [jnp.exp2(part - top) for part in tops]
        weights = jnp.exp2(scores - top)
        total = early[2][at, 1:2] * shares[0] + early[5][at, 1:2] * shares[1]
        inverse = 1.0 / (total + jnp.sum(weights, axis=0, keepdims=True))
        probs = [early[0][at] * (shares[0] * inverse), early[3][at] * (shares[1] * inverse), weights * inverse]
        upstream = [early[1][at], early[4][at], late_up[at]]
        probs_low = [part.astype(BF16) for part in probs]
        delta = sum(by_eights(p.astype(F32) * u) for p, u in zip(probs_low, upstream))
        delta = jnp.sum(delta, axis=0, keepdims=True)
        slope_sum = jnp.zeros((8, token_rows), F32)
        for p, u, low, high in zip(probs, upstream, bounds, bounds[1:]):
            dscore = p * (u - delta)
            for (level, rows), start in zip(runs, starts):
                if level and low <= start < high:
                    here = dscore[start - low : start - low + rows]
                    slope_sum = slope_sum + by_eights(here) * float(level)
            dscore_out[at, low:high] = dscore.astype(BF16)
        probs_out[at] = jnp.concatenate(probs_low, axis=0)
        return slope_sum

    def gradients(h, seq):
        at, lanes = seq * heads + h, slice(h * head, (h + 1) * head)
        dk = dot(dscore_out[at, sent_rows:], stacked((qg_own, qg_other), 0, seq, lanes)) * scale
        dv = dot(probs_out[at, sent_rows:], stacked((qg_own, qg_other), 1, seq, lanes))
        for kind, direct in enumerate((dk, dv)):
            group = (kind * seqs + seq) * heads + h
            first, direct = direct[:far_size], direct[far_size:]
            across[kind, seq, :, lanes] = direct[:-far_size].astype(BF16)
            relay[pl.ds(group * far_size, far_size), :] = first.astype(BF16)
            relay[pl.ds(slab + group * far_size, far_size), :] = direct[-far_size:].astype(BF16)

    items = [(h, seq) for h in range(heads) for seq in range(seqs)]
    behind = 4
    sums = {}
    for i in range(len(items) + 2 * behind):
        if i < len(items):
            score(*items[i])
        if 0 <= i - behind < len(items):
            item = items[i - behind]
            sums[item] = normalise(*item)
        if 0 <= i - 2 * behind < len(items):
            gradients(*items[i - 2 * behind])
    for h in range(heads):
        slope_out[h : h + 1, :] = jnp.sum(sum(sums[h, seq] for seq in range(seqs)), axis=0, keepdims=True)
    relay[pl.ds(2 * slab, 2 * heads), :] = two_parts(slope_out[...])


def cell_grads_body(head, far_sizes, dscore, probs, qg_own, qg_other, near, side, far):
    seqs, block, width = qg_own.shape[1:]
    heads = width // head
    scale = 1.0 / math.sqrt(head)
    sizes = (block, block // 2, *far_sizes)
    rows = slice(2 * block, 2 * block + sum(sizes))
    for h in range(heads):
        lanes = slice(h * head, (h + 1) * head)
        for seq in range(seqs):
            at = seq * heads + h
            dk = dot(dscore[at, rows], stacked((qg_own, qg_other), 0, seq, lanes)) * scale
            dv = dot(probs[at, rows], stacked((qg_own, qg_other), 1, seq, lanes))
            for kind, direct in enumerate((dk, dv)):
                group = (kind * seqs + seq) * heads + h
                near[kind, seq, :, lanes] = direct[:block]
                start = block + sizes[1]
                side[pl.ds(group * sizes[1], sizes[1]), :] = direct[block:start].astype(BF16)
                slab = 0
                for size in far_sizes:
                    far[pl.ds(slab + group * size, size), :] = direct[start : start + size]
                    start += size
                    slab += 2 * seqs * heads * size


def own_grads_body(head, dscore, probs, qg_own, qg_other, *refs):
    *pieces, dq_own, dq_send, own, other = refs
    seqs, block, width = qg_own.shape[1:]
    heads = width // head
    scale = 1.0 / math.sqrt(head)
    for h in range(heads):
        lanes = slice(h * head, (h + 1) * head)
        for seq in range(seqs):
            at = seq * heads + h
            dq = (dot(dscore[at], stacked(pieces, 0, seq, lanes), 0, 0) * scale).astype(BF16)
            dq_own[seq, :, lanes] = dq[:block]
            dq_send[seq, :, lanes] = dq[block:]
            dk = dot(dscore[at, : 2 * block], stacked((qg_own, qg_other), 0, seq, lanes)) * scale
            dv = dot(probs[at, : 2 * block], stacked((qg_own, qg_other), 1, seq, lanes))
            for kind, direct in enumerate((dk, dv)):
                own[kind, seq, :, lanes] = direct[:block]
                other[kind, seq, :, lanes] = direct[block:]


def fold_body(direct, coarse, done, out):
    rows = direct.shape[2]
    for kind in range(direct.shape[0]):
        for seq in range(direct.shape[1]):
            spread = dot(spread_matrix(rows, 1), coarse[kind, seq])
            out[kind, seq] = (direct[kind, seq] + spread).astype(BF16)


def relay_body(far, back, slope, *refs):
    *slopes, slope_out, keep, message = refs
    rows = keep.shape[0]
    total = slope[...] + one_part(back[pl.ds(2 * rows, 2 * slope.shape[0]), :])
    for ref in slopes:
        total = total + ref[...]
    slope_out[...] = total
    keep[...] = far[pl.ds(0, rows), :] + back[pl.ds(0, rows), :].astype(F32)
    message[pl.ds(0, rows), :] = (far[pl.ds(rows, rows), :] + back[pl.ds(rows, rows), :].astype(F32)).astype(BF16)
    message[pl.ds(rows, 2 * slope.shape[0]), :] = two_parts(total)


def meet_body(keep, back, slope, slope_out, message):
    rows = keep.shape[0]
    total = slope[...] + one_part(back[pl.ds(rows, 2 * slope.shape[0]), :])
    slope_out[...] = total
    message[pl.ds(0, rows), :] = (keep[...] + back[pl.ds(0, rows), :].astype(F32)).astype(BF16)
    message[pl.ds(rows, 2 * slope.shape[0]), :] = two_parts(total)


def gather_body(levels_of, done, own, other, slope, near, *refs):
    back, (kept, sent, slope_out) = refs[:-3], refs[-3:]
    kinds, seqs, block, width = own.shape
    heads = slope.shape[0]
    head = width // heads
    sizes = [2 * block >> level for level in levels_of[1:]]
    spread = jnp.concatenate([spread_matrix(2 * block, level) for level in levels_of], axis=1)
    for kind in range(kinds):
        for seq in range(seqs):
            for h in range(heads):
                lanes = slice(h * head, (h + 1) * head)
                group = (kind * seqs + seq) * heads + h
                cells = [near[kind, seq, :, lanes]]
                cells += [part[pl.ds(group * size, size), :] for part, size in zip(back, sizes)]
                total = dot(spread, jnp.concatenate(cells, axis=0))
                kept[kind, seq, :, lanes] = (own[kind, seq, :, lanes] + total[:block]).astype(BF16)
                sent[kind, seq, :, lanes] = (other[kind, seq, :, lanes] + total[block:]).astype(BF16)
    far, size = back[-1], sizes[-1]
    slope_out[...] = slope[...] + one_part(far[pl.ds(kinds * seqs * heads * size, 2 * heads), :])


def join_body(core, own, other, out, done, sems):
    mine, theirs = head_halves(core, own.shape[-1])
    copy_all([(other, out.at[:, :, theirs]), (own, out.at[:, :, mine])], sems)
    done[...] = jnp.zeros_like(done)


def join_pair_body(core, own, other, slope, slope_other, first, second, slope_out, sums, sems):
    mine, theirs = head_halves(core, own.shape[-1])
    moves = []
    for index, out in enumerate((first, second)):
        moves.append((other.at[index], out.at[:, :, theirs]))
        moves.append((own.at[index], out.at[:, :, mine]))
    copies = start_all(moves, sems)
    ours, rest = slope[...], slope_other[...]
    lower = jnp.where(core[0] == 0, ours, rest)
    upper = jnp.where(core[0] == 0, rest, ours)
    terms = jnp.concatenate([lower, upper], axis=0)
    sums[...] = jnp.sum(terms.T, axis=0, keepdims=True)
    last = pltpu.make_async_copy(sums, slope_out, sems.at[len(moves)])
    last.start()
    for copy in (*copies, last):
        copy.wait()


def paired(queries, key_rows, value_rows, out_grad, level_slope):
    seqs, block, width = queries.shape
    heads = level_slope.shape[0]
    half, head = width // 2, width // heads
    dp_count = lax.axis_size("dp")
    levels = 4
    position = lax.axis_index("ctx")
    core = (position % 2).astype(jnp.int32).reshape(1)

    part = like(2, seqs, block, half)
    k_other, v_other = swap(key_rows, 1), swap(value_rows, 1)
    cell_shapes = tuple(like(2, seqs, 2 * block >> level, half) for level in range(1, levels))
    wide = (pltpu.VMEM((2, seqs, half // 128, block, 128), F32),)
    own_cells = call(own_summary_body, cell_shapes, (core, key_rows, value_rows), "own_summaries", scalars=1, scratch=wide)
    cells = call(summary_body, cell_shapes, (core, k_other, v_other, *own_cells), "summaries", scalars=1, scratch=wide)
    qg_own, qg_send = call(
        split_body, (part, part), (core, queries, out_grad), "split_qg", scalars=1, hbm_in=2, copies=4
    )
    qg_other = swap(qg_send, 1)

    kv_own, kv_other = call(
        keep_body, (part, part), (core, key_rows, value_rows, k_other, v_other), "keep_halves", scalars=1
    )
    near_cells = swap(cells[0], 2)
    far_cells = swap(cells[2], 8)
    side_cells = swap(cells[1], 4)
    across_cells = swap(call(coarser_body, like(2, seqs, block // 2, half), (near_cells,), "coarser"), 4)
    far_side_cells = swap(far_cells, 4)
    relayed_cells = [swap(far_cells, 2), swap(far_side_cells, 2)]

    groups = seqs * heads
    far_size = block // 4
    token_rows, cell_rows, late_rows = 2 * block, 2 * block + far_size, block - far_size
    rows = token_rows + cell_rows + late_rows

    turned = call(
        functools.partial(turn_body, head), like(2, groups // 2, head, token_rows), (qg_own, qg_other), "turn"
    )

    def score(levels_of, pieces, count):
        product = like(groups // 2, count, token_rows, dtype=F32)
        return call(
            functools.partial(score_body, levels_of, head),
            (product, product, like(groups // 2, 8, token_rows, dtype=F32)),
            (core, level_slope, turned, *pieces),
            "scores",
            scalars=2,
            flops=40 * seqs * token_rows * count * half,
        )

    token_pieces = [kv_own, kv_other]
    cell_pieces = [near_cells, side_cells, far_cells, far_side_cells, relayed_cells[0]]
    late_pieces = [across_cells, relayed_cells[1]]
    early = (*score((0, 0), token_pieces, token_rows), *score((1, 2, 3, 3, 3), cell_pieces, cell_rows))
    runs = ((0, token_rows), (1, block), (2, block // 2), (3, far_size), (3, far_size))
    runs += ((3, far_size), (2, block // 2), (3, far_size))
    far_rows, tail = groups * far_size, heads
    slope_part = like(heads // 2, token_rows, dtype=F32)
    wide = like(*part.shape, dtype=F32)
    slope, across, relay, dscore, probs = call(
        functools.partial(attend_body, runs, head),
        (
            slope_part,
            like(2, seqs, block // 2, half),
            like(2 * far_rows + tail, head),
            like(groups // 2, rows, token_rows),
            like(groups // 2, rows, token_rows),
        ),
        (core, level_slope, *early, turned, qg_own, qg_other, *late_pieces),
        "attend",
        scalars=2,
        flops=40 * seqs * token_rows * rows * half,
        scratch=(
            pltpu.VMEM((groups // 2, late_rows, token_rows), F32),
            pltpu.VMEM((groups // 2, late_rows, token_rows), F32),
        ),
    )
    near, side, far_direct = call(
        functools.partial(cell_grads_body, head, (far_size, far_size)),
        (wide, like(groups * (block // 2), head), like(2 * far_rows, head, dtype=F32)),
        (dscore, probs, qg_own, qg_other),
        "cell_grads",
    )
    dq_part = like(seqs, block, half)
    dq_own, dq_send, own, other = call(
        functools.partial(own_grads_body, head),
        (dq_part, dq_part, wide, wide),
        (dscore, probs, qg_own, qg_other, *token_pieces, *cell_pieces, *late_pieces),
        "own_grads",
        flops=40 * seqs * token_rows * rows * half,
    )

    across_back = swap(across, 4)
    relay_back = swap(relay, 2)
    slopes = [swap(slope, 2 * y, dp) for dp in range(1, dp_count) for y in range(2)]
    dq_other = swap(dq_send, 1)
    message = like(far_rows + tail, head)
    slope, keep, far_side = call(
        relay_body,
        (slope_part, like(far_rows, head, dtype=F32), message),
        (far_direct, relay_back, slope, *slopes),
        "relay",
    )
    far_side_back = swap(far_side, 4)
    near_back = swap(call(fold_body, like(*near.shape), (near, across_back, slope), "fold"), 2)
    side_back = swap(side, 4)
    slope, far_total = call(meet_body, (slope_part, message), (keep, far_side_back, slope), "meet")
    far_back = swap(far_total, 8)
    whole = like(seqs, block, width)
    dq, done = call(
        join_body, (whole, slope_part), (core, dq_own, dq_other), "join_queries", scalars=1, hbm_out=1, copies=2
    )
    kept, sent, slope = call(
        functools.partial(gather_body, (1, 2, 3)),
        (part, part, slope_part),
        (done, own, other, slope, near_back, side_back, far_back),
        "gather_cells",
    )
    kv_grad_other = swap(sent, 1)
    dk, dv, slope_grad = call(
        join_pair_body,
        (whole, whole, like(1, heads, dtype=F32)),
        (core, kept, kv_grad_other, slope, swap(slope, 1)),
        "join_kv",
        scalars=1,
        hbm_out=3,
        copies=5,
        scratch=(pltpu.VMEM((1, heads), F32),),
    )
    return dq, dk, dv, slope_grad.reshape(heads)


def as_sent(x):
    return jax.tree.map(lambda a: a.astype(jnp.bfloat16) if a.dtype == jnp.float32 else a, x)


def from_partner(value, axis, apart):
    mask = 2**apart
    pairs = [(source, source ^ mask) for source in range(lax.axis_size(axis))]
    return lax.ppermute(value, axis, pairs)


def pair_mean(cells):
    shaped = cells.reshape(cells.shape[:-2] + (cells.shape[-2] // 2, 2, cells.shape[-1])).astype(
        jnp.float32
    )
    return ((shaped[..., 0, :] + shaped[..., 1, :]) * 0.5).astype(jnp.bfloat16)


def merge_level(own_pair, other_pair, flag):
    merged = []
    for own_part, other_part in zip(own_pair, other_pair):
        own_small = pair_mean(own_part)
        other_small = pair_mean(other_part)
        merged.append(
            jnp.where(
                flag == 1,
                jnp.concatenate([other_small, own_small], axis=1),
                jnp.concatenate([own_small, other_small], axis=1),
            )
        )
    return tuple(merged)


def to_heads(rows, heads):
    seqs, count, width = rows.shape
    return jnp.transpose(rows.reshape(seqs, count, heads, width // heads), (0, 2, 1, 3))


def from_heads(split):
    seqs, heads, count, head = split.shape
    return jnp.transpose(split, (0, 2, 1, 3)).reshape(seqs, count, heads * head)


def product(form, left, right):
    return jnp.einsum(form, left, right, preferred_element_type=jnp.float32)


def attend(query_four, key_four, value_four, grad_four, level_slope, block):
    head = query_four.shape[3]
    key_count = key_four.shape[2]
    scale = 1.0 / math.sqrt(head)
    column = jnp.arange(key_count, dtype=jnp.int32)
    level_of = column // block - 1
    sibling = jnp.maximum(level_of, 0)
    multiple = jnp.where(level_of < 0, 1.0, jnp.exp2(sibling.astype(jnp.float32)))
    bias = level_slope[:, None] * sibling.astype(jnp.float32)[None, :]
    raw = product("shqd,shkd->shqk", query_four, key_four)
    scores = raw * scale + bias[None, :, None, :]
    top = jnp.max(scores, axis=-1, keepdims=True)
    weights = multiple[None, None, None, :] * jnp.exp(scores - top)
    probs = weights / jnp.sum(weights, axis=-1, keepdims=True)
    probs_low = probs.astype(jnp.bfloat16)
    output = product("shqk,shkd->shqd", probs_low, value_four)
    delta = jnp.sum(grad_four.astype(jnp.float32) * output, axis=-1)
    upstream = product("shqd,shkd->shqk", grad_four, value_four)
    dscore = probs * (upstream - delta[..., None])
    slope_part = jnp.sum(dscore * sibling.astype(jnp.float32)[None, None, None, :], axis=(0, 2, 3))
    dscore_low = dscore.astype(jnp.bfloat16)
    query_part = product("shqk,shkd->shqd", dscore_low, key_four) * scale
    key_part = product("shqk,shqd->shkd", dscore_low, query_four) * scale
    value_part = product("shqk,shqd->shkd", probs_low, grad_four)
    return (query_part, key_part, value_part, slope_part)


def split_level(grad_now, direct, flag, level, block):
    half = block // 2
    lower_src = grad_now[:, :, :half]
    upper_src = grad_now[:, :, half:]
    own_src = jnp.where(flag == 1, upper_src, lower_src)
    other_src = jnp.where(flag == 1, lower_src, upper_src)
    own_half = jnp.repeat(own_src, 2, axis=2) * 0.5
    other_half = jnp.repeat(other_src, 2, axis=2) * 0.5
    sent = (other_half + direct[:, :, (level + 1) * block : (level + 2) * block]).astype(
        jnp.bfloat16
    )
    return (own_half, sent)


def by_blocks(queries, key_rows, value_rows, out_grad, level_slope):
    seqs, block, width = queries.shape
    heads = level_slope.shape[0]
    ctx_count = lax.axis_size("ctx")
    levels = ctx_count.bit_length() - 1
    position = lax.axis_index("ctx")
    bit_list = [position // 2**level % 2 for level in range(levels)]
    own_pair = (key_rows, value_rows)
    partners = []
    for level in range(levels - 2):
        other_pair = jax.tree.map(
            lambda part, own: part.astype(own.dtype),
            from_partner(as_sent(own_pair), "ctx", level),
            own_pair,
        )
        partners.append(other_pair)
        own_pair = merge_level(own_pair, other_pair, bit_list[level])
    for level in range(levels - 2, levels):
        other_pair = jax.tree.map(
            lambda part, own: part.astype(own.dtype),
            from_partner(as_sent(own_pair), "ctx", level),
            own_pair,
        )
        partners.append(other_pair)
        if level + 1 < levels:
            own_pair = merge_level(own_pair, other_pair, bit_list[level])
    key_set = jnp.concatenate(
        [to_heads(key_rows, heads)] + [to_heads(pair[0], heads) for pair in partners], axis=2
    )
    value_set = jnp.concatenate(
        [to_heads(value_rows, heads)] + [to_heads(pair[1], heads) for pair in partners], axis=2
    )
    query_four = to_heads(queries, heads)
    grad_four = to_heads(out_grad, heads)
    query_part, key_part, value_part, slope_part = attend(
        query_four, key_set, value_set, grad_four, level_slope, block
    )
    slope_grad = lax.psum(slope_part, ("dp", "ctx"))
    head = width // heads
    grad_keys = jnp.zeros((seqs, heads, block, head), jnp.float32)
    grad_values = jnp.zeros((seqs, heads, block, head), jnp.float32)
    for level in reversed(range(levels)):
        own_keys, sent_keys = split_level(grad_keys, key_part, bit_list[level], level, block)
        own_values, sent_values = split_level(
            grad_values, value_part, bit_list[level], level, block
        )
        back_keys, back_values = from_partner((sent_keys, sent_values), "ctx", level)
        grad_keys = own_keys + back_keys.astype(jnp.float32)
        grad_values = own_values + back_values.astype(jnp.float32)
    key_grad = from_heads((grad_keys + key_part[:, :, :block]).astype(jnp.bfloat16))
    value_grad = from_heads((grad_values + value_part[:, :, :block]).astype(jnp.bfloat16))
    return (from_heads(query_part.astype(jnp.bfloat16)), key_grad, value_grad, slope_grad)


def shards(queries, key_rows, value_rows, out_grad, level_slope):
    few = lax.axis_size("ctx") == 16 and queries.shape[1] % 64 == 0 and level_slope.shape[0] % 16 == 0
    form = paired if few else by_blocks
    return form(queries, key_rows, value_rows, out_grad, level_slope)


def solution(mesh):
    placed = (
        P("dp", "ctx", None),
        P("dp", "ctx", None),
        P("dp", "ctx", None),
        P("dp", "ctx", None),
        P(),
    )
    return jax.shard_map(
        shards,
        mesh=mesh,
        in_specs=placed,
        out_specs=(P("dp", "ctx", None), P("dp", "ctx", None), P("dp", "ctx", None), P()),
        check_vma=False,
    )
```

```python
import functools
import math

import jax
import jax.numpy as jnp
from jax import lax
from jax.experimental import pallas as pl
from jax.experimental.pallas import tpu as pltpu
from jax.sharding import PartitionSpec as P

F32, BF16 = jnp.float32, jnp.bfloat16
LOG2E = math.log2(math.e)
VMEM = pl.BlockSpec(memory_space=pltpu.VMEM)
SMEM = pl.BlockSpec(memory_space=pltpu.SMEM)
HBM = pl.BlockSpec(memory_space=pltpu.HBM)


def swap(value, apart, dp_apart=0):
    count = lax.axis_size("ctx")
    if not dp_apart:
        return lax.ppermute(value, "ctx", [(source, source ^ apart) for source in range(count)])
    mask = dp_apart * count + apart
    pairs = [(source, source ^ mask) for source in range(lax.axis_size("dp") * count)]
    return lax.ppermute(value, ("dp", "ctx"), pairs)


def like(*shape, dtype=BF16):
    return jax.ShapeDtypeStruct(shape, dtype)


def call(body, out_shape, operands, name, scalars=0, hbm_in=0, hbm_out=0, copies=0, flops=0, limit=32, scratch=(), aliases={}):
    moved = sum(a.size * a.dtype.itemsize for a in jax.tree.leaves((operands, out_shape)))
    count = len(operands) - scalars - hbm_in
    return pl.pallas_call(
        body,
        out_shape=out_shape,
        in_specs=[SMEM] * scalars + [HBM] * hbm_in + [VMEM] * count,
        out_specs=tuple(HBM if i < hbm_out else VMEM for i in range(len(out_shape)))
        if isinstance(out_shape, tuple)
        else VMEM,
        scratch_shapes=[*scratch, *([pltpu.SemaphoreType.DMA((copies,))] if copies else [])],
        compiler_params=pltpu.CompilerParams(vmem_limit_bytes=int(limit * 2**20)),
        cost_estimate=pl.CostEstimate(flops=flops, bytes_accessed=moved, transcendentals=0),
        input_output_aliases=aliases,
        name=name,
    )(*operands)


def dot(left, right, left_dim=1, right_dim=0):
    dims = (((left_dim,), (right_dim,)), ((), ()))
    return lax.dot_general(left, right, dims, preferred_element_type=F32)


def pair_matrix(rows):
    cell = lax.broadcasted_iota(jnp.int32, (rows, 2 * rows), 0)
    source = lax.broadcasted_iota(jnp.int32, (rows, 2 * rows), 1)
    return jnp.where(source // 2 == cell, 0.5, 0.0).astype(BF16)


def spread_matrix(rows, level):
    row = lax.broadcasted_iota(jnp.int32, (rows, rows >> level), 0)
    cell = lax.broadcasted_iota(jnp.int32, (rows, rows >> level), 1)
    return jnp.where(row >> level == cell, 0.5**level, 0.0).astype(BF16)


def two_parts(x):
    high = x.astype(BF16)
    return jnp.concatenate([high, (x - high.astype(F32)).astype(BF16)], axis=0)


def one_part(x):
    rows = x.shape[0] // 2
    return x[:rows].astype(F32) + x[rows:].astype(F32)


def head_halves(core, half):
    mine = pl.ds(pl.multiple_of(core[0] * half, half), half)
    theirs = pl.ds(pl.multiple_of((1 - core[0]) * half, half), half)
    return mine, theirs


def start_all(moves, sems):
    copies = [pltpu.make_async_copy(src, dst, sems.at[i]) for i, (src, dst) in enumerate(moves)]
    for copy in copies:
        copy.start()
    return copies


def copy_all(moves, sems):
    for copy in start_all(moves, sems):
        copy.wait()


def split_body(core, first, second, own, send, sems):
    mine, theirs = head_halves(core, own.shape[-1])
    moves = []
    for index, whole in enumerate((first, second)):
        moves.append((whole.at[:, :, theirs], send.at[index]))
        moves.append((whole.at[:, :, mine], own.at[index]))
    copy_all(moves, sems)


def keep_body(core, k, v, k_other, v_other, own, other):
    mine, _ = head_halves(core, own.shape[-1])
    for index, (first, second) in enumerate(((k, k_other), (v, v_other))):
        own[index] = first[:, :, mine]
        other[index] = second[:, :, mine]


def halve(rows, wide):
    count = rows.shape[0]
    wide[pl.ds(0, count), :] = rows
    return (wide[pl.ds(0, count // 2, stride=2), :] + wide[pl.ds(1, count // 2, stride=2), :]) * 0.5


def tiles_of(shape, core, wide):
    kinds, seqs, _, half = shape
    for kind in range(kinds):
        for seq in range(seqs):
            for start in range(0, half, 128):
                source = pl.ds(pl.multiple_of(core[0] * half + start, 128), 128)
                yield kind, seq, source, slice(start, start + 128), wide.at[kind, seq, start // 128]


def own_summary_body(core, k, v, *refs):
    *cells, wide = refs
    for kind, seq, source, lanes, scratch in tiles_of(cells[0].shape, core, wide):
        rows = (k, v)[kind][seq, :, source].astype(F32)
        for out in cells:
            rows = halve(rows, scratch)
            out[kind, seq, :, lanes] = jnp.concatenate([rows, jnp.zeros_like(rows)], axis=0).astype(BF16)
            rows = rows.astype(BF16).astype(F32)


def summary_body(core, k_other, v_other, *refs):
    *refs, wide = refs
    own, cells = refs[: len(refs) // 2], refs[len(refs) // 2 :]
    for kind, seq, source, lanes, scratch in tiles_of(cells[0].shape, core, wide):
        rows = (k_other, v_other)[kind][seq, :, source].astype(F32)
        for first, out in zip(own, cells):
            rows = halve(rows, scratch)
            before = first[kind, seq, :, lanes].astype(F32)[: rows.shape[0]]
            out[kind, seq, :, lanes] = jnp.concatenate([before, rows], axis=0).astype(BF16)
            rows = rows.astype(BF16).astype(F32)


def coarser_body(cells, done, out):
    for kind in range(cells.shape[0]):
        for seq in range(cells.shape[1]):
            rows = cells[kind, seq]
            out[kind, seq] = dot(pair_matrix(rows.shape[0] // 2), rows).astype(BF16)


def stacked(parts, kind, seq, lanes):
    return jnp.concatenate([part[kind, seq, :, lanes] for part in parts], axis=0)


def turn_body(head, qg_own, qg_other, turned):
    kinds, seqs, _, width = qg_own.shape
    heads = width // head
    for kind in range(kinds):
        for h in range(heads):
            for seq in range(seqs):
                lanes = slice(h * head, (h + 1) * head)
                turned[kind, seq * heads + h] = stacked((qg_own, qg_other), kind, seq, lanes).T


def score_body(levels_of, head, core, slope, turned, *refs):
    *pieces, weights, upstream, stats = refs
    seqs, width = pieces[0].shape[1], pieces[0].shape[3]
    heads = width // head
    scale = LOG2E / math.sqrt(head)
    for h in range(heads):
        lanes = slice(h * head, (h + 1) * head)
        step = slope[core[0] * heads + h] * LOG2E + 1.0
        for seq in range(seqs):
            at = seq * heads + h
            raw = dot(stacked(pieces, 0, seq, lanes), turned[0, at])
            upstream[at] = dot(stacked(pieces, 1, seq, lanes), turned[1, at])
            scores = with_bias(raw * scale, zip(levels_of, [piece.shape[2] for piece in pieces]), step)
            top = jnp.max(scores, axis=0, keepdims=True)
            spread = jnp.exp2(scores - top)
            weights[at] = spread
            stats[at, 0:1] = top
            stats[at, 1:2] = jnp.sum(spread, axis=0, keepdims=True)


def with_bias(scores, runs, step):
    parts, start = [], 0
    for level, count in runs:
        part = scores[start : start + count]
        parts.append(part + step * float(level) if level else part)
        start += count
    return jnp.concatenate(parts, axis=0)


def by_eights(x):
    return jnp.sum(x.reshape(x.shape[0] // 8, 8, x.shape[1]), axis=0)


def attend_body(runs, head, core, slope, *refs):
    *refs, late_scores, late_up = refs
    early, (turned, qg_own, qg_other, *late), outs = refs[:6], refs[6:-5], refs[-5:]
    slope_out, across, relay, dscore_out, probs_out = outs
    seqs, block, width = qg_own.shape[1:]
    heads = width // head
    scale = 1.0 / math.sqrt(head)
    starts = [sum(rows for _, rows in runs[:i]) for i in range(len(runs) + 1)]
    token_rows = early[0].shape[1]
    early_rows = token_rows + early[3].shape[1]
    bounds = (0, token_rows, early_rows, starts[-1])
    late_runs = [run for run, start in zip(runs, starts) if start >= early_rows]
    sent_rows, far_size = starts[-4], runs[-1][1]
    slab = 2 * seqs * heads * far_size

    def score(h, seq):
        at, lanes = seq * heads + h, slice(h * head, (h + 1) * head)
        step = slope[core[0] * heads + h] * LOG2E + 1.0
        raw = dot(stacked(late, 0, seq, lanes), turned[0, at])
        late_scores[at] = with_bias(raw * (scale * LOG2E), late_runs, step)
        late_up[at] = dot(stacked(late, 1, seq, lanes), turned[1, at])

    def normalise(h, seq):
        at = seq * heads + h
        tops = early[2][at, 0:1], early[5][at, 0:1]
        scores = late_scores[at]
        top = jnp.maximum(jnp.maximum(*tops), jnp.max(scores, axis=0, keepdims=True))
        shares = [jnp.exp2(part - top) for part in tops]
        weights = jnp.exp2(scores - top)
        total = early[2][at, 1:2] * shares[0] + early[5][at, 1:2] * shares[1]
        inverse = 1.0 / (total + jnp.sum(weights, axis=0, keepdims=True))
        probs = [early[0][at] * (shares[0] * inverse), early[3][at] * (shares[1] * inverse), weights * inverse]
        upstream = [early[1][at], early[4][at], late_up[at]]
        probs_low = [part.astype(BF16) for part in probs]
        delta = sum(by_eights(p.astype(F32) * u) for p, u in zip(probs_low, upstream))
        delta = jnp.sum(delta, axis=0, keepdims=True)
        slope_sum = jnp.zeros((8, token_rows), F32)
        for p, u, low, high in zip(probs, upstream, bounds, bounds[1:]):
            dscore = p * (u - delta)
            for (level, rows), start in zip(runs, starts):
                if level and low <= start < high:
                    here = dscore[start - low : start - low + rows]
                    slope_sum = slope_sum + by_eights(here) * float(level)
            dscore_out[at, low:high] = dscore.astype(BF16)
        probs_out[at] = jnp.concatenate(probs_low, axis=0)
        return slope_sum

    def gradients(h, seq):
        at, lanes = seq * heads + h, slice(h * head, (h + 1) * head)
        dk = dot(dscore_out[at, sent_rows:], stacked((qg_own, qg_other), 0, seq, lanes)) * scale
        dv = dot(probs_out[at, sent_rows:], stacked((qg_own, qg_other), 1, seq, lanes))
        for kind, direct in enumerate((dk, dv)):
            group = (kind * seqs + seq) * heads + h
            first, direct = direct[:far_size], direct[far_size:]
            across[kind, seq, :, lanes] = direct[:-far_size].astype(BF16)
            relay[pl.ds(group * far_size, far_size), :] = first.astype(BF16)
            relay[pl.ds(slab + group * far_size, far_size), :] = direct[-far_size:].astype(BF16)

    items = [(h, seq) for h in range(heads) for seq in range(seqs)]
    behind = 4
    sums = {}
    for i in range(len(items) + 2 * behind):
        if i < len(items):
            score(*items[i])
        if 0 <= i - behind < len(items):
            item = items[i - behind]
            sums[item] = normalise(*item)
        if 0 <= i - 2 * behind < len(items):
            gradients(*items[i - 2 * behind])
    for h in range(heads):
        slope_out[h : h + 1, :] = jnp.sum(sum(sums[h, seq] for seq in range(seqs)), axis=0, keepdims=True)
    relay[pl.ds(2 * slab, 2 * heads), :] = two_parts(slope_out[...])


def cell_grads_body(head, far_sizes, dscore, probs, qg_own, qg_other, near, side, far):
    seqs, block, width = qg_own.shape[1:]
    heads = width // head
    scale = 1.0 / math.sqrt(head)
    sizes = (block, block // 2, *far_sizes)
    rows = slice(2 * block, 2 * block + sum(sizes))
    for h in range(heads):
        lanes = slice(h * head, (h + 1) * head)
        for seq in range(seqs):
            at = seq * heads + h
            dk = dot(dscore[at, rows], stacked((qg_own, qg_other), 0, seq, lanes)) * scale
            dv = dot(probs[at, rows], stacked((qg_own, qg_other), 1, seq, lanes))
            for kind, direct in enumerate((dk, dv)):
                group = (kind * seqs + seq) * heads + h
                near[kind, seq, :, lanes] = direct[:block]
                start = block + sizes[1]
                side[pl.ds(group * sizes[1], sizes[1]), :] = direct[block:start].astype(BF16)
                slab = 0
                for size in far_sizes:
                    far[pl.ds(slab + group * size, size), :] = direct[start : start + size]
                    start += size
                    slab += 2 * seqs * heads * size


def own_grads_body(head, dscore, probs, qg_own, qg_other, *refs):
    *pieces, dq_own, dq_send, own, other = refs
    seqs, block, width = qg_own.shape[1:]
    heads = width // head
    scale = 1.0 / math.sqrt(head)
    for h in range(heads):
        lanes = slice(h * head, (h + 1) * head)
        for seq in range(seqs):
            at = seq * heads + h
            dq = (dot(dscore[at], stacked(pieces, 0, seq, lanes), 0, 0) * scale).astype(BF16)
            dq_own[seq, :, lanes] = dq[:block]
            dq_send[seq, :, lanes] = dq[block:]
            dk = dot(dscore[at, : 2 * block], stacked((qg_own, qg_other), 0, seq, lanes)) * scale
            dv = dot(probs[at, : 2 * block], stacked((qg_own, qg_other), 1, seq, lanes))
            for kind, direct in enumerate((dk, dv)):
                own[kind, seq, :, lanes] = direct[:block]
                other[kind, seq, :, lanes] = direct[block:]


def fold_body(direct, coarse, done, out):
    rows = direct.shape[2]
    for kind in range(direct.shape[0]):
        for seq in range(direct.shape[1]):
            spread = dot(spread_matrix(rows, 1), coarse[kind, seq])
            out[kind, seq] = (direct[kind, seq] + spread).astype(BF16)


def relay_body(far, back, slope, *refs):
    *slopes, slope_out, keep, message = refs
    rows = keep.shape[0]
    total = slope[...] + one_part(back[pl.ds(2 * rows, 2 * slope.shape[0]), :])
    for ref in slopes:
        total = total + ref[...]
    slope_out[...] = total
    keep[...] = far[pl.ds(0, rows), :] + back[pl.ds(0, rows), :].astype(F32)
    message[pl.ds(0, rows), :] = (far[pl.ds(rows, rows), :] + back[pl.ds(rows, rows), :].astype(F32)).astype(BF16)
    message[pl.ds(rows, 2 * slope.shape[0]), :] = two_parts(total)


def meet_body(keep, back, slope, slope_out, message):
    rows = keep.shape[0]
    total = slope[...] + one_part(back[pl.ds(rows, 2 * slope.shape[0]), :])
    slope_out[...] = total
    message[pl.ds(0, rows), :] = (keep[...] + back[pl.ds(0, rows), :].astype(F32)).astype(BF16)
    message[pl.ds(rows, 2 * slope.shape[0]), :] = two_parts(total)


def gather_body(kind, levels_of, done, own, other, near, *refs):
    back, (kept, sent) = refs[:-2], refs[-2:]
    _, seqs, block, width = own.shape
    sizes = [2 * block >> level for level in levels_of[1:]]
    head = back[0].shape[1]
    spread = jnp.concatenate([spread_matrix(2 * block, level) for level in levels_of], axis=1)
    for seq in range(seqs):
        for h in range(width // head):
            lanes = slice(h * head, (h + 1) * head)
            group = (kind * seqs + seq) * (width // head) + h
            cells = [near[kind, seq, :, lanes]]
            cells += [part[pl.ds(group * size, size), :] for part, size in zip(back, sizes)]
            total = dot(spread, jnp.concatenate(cells, axis=0))
            kept[seq, :, lanes] = (own[kind, seq, :, lanes] + total[:block]).astype(BF16)
            sent[seq, :, lanes] = (other[kind, seq, :, lanes] + total[block:]).astype(BF16)


def total_body(slope, far, out):
    rows = 2 * slope.shape[0]
    out[...] = slope[...] + one_part(far[pl.ds(far.shape[0] - rows, rows), :])


def join_body(core, own, other, out, done, sems):
    mine, theirs = head_halves(core, own.shape[-1])
    copy_all([(other, out.at[:, :, theirs]), (own, out.at[:, :, mine])], sems)
    done[...] = jnp.zeros_like(done)


def keep_grads_body(core, first, second, first_out, second_out, sems):
    mine, _ = head_halves(core, first.shape[-1])
    copy_all([(first, first_out.at[:, :, mine]), (second, second_out.at[:, :, mine])], sems)


def join_pair_body(core, half_done, other_half_done, first, second, slope, slope_other, *refs):
    first_out, second_out, slope_out, sums, sems = refs
    _, theirs = head_halves(core, first.shape[-1])
    moves = [(first, first_out.at[:, :, theirs]), (second, second_out.at[:, :, theirs])]
    copies = start_all(moves, sems)
    ours, rest = slope[...], slope_other[...]
    lower = jnp.where(core[0] == 0, ours, rest)
    upper = jnp.where(core[0] == 0, rest, ours)
    terms = jnp.concatenate([lower, upper], axis=0)
    sums[...] = jnp.sum(terms.T, axis=0, keepdims=True)
    last = pltpu.make_async_copy(sums, slope_out, sems.at[len(moves)])
    last.start()
    for copy in (*copies, last):
        copy.wait()


def paired(queries, key_rows, value_rows, out_grad, level_slope):
    seqs, block, width = queries.shape
    heads = level_slope.shape[0]
    half, head = width // 2, width // heads
    dp_count = lax.axis_size("dp")
    levels = 4
    position = lax.axis_index("ctx")
    core = (position % 2).astype(jnp.int32).reshape(1)

    part = like(2, seqs, block, half)
    k_other, v_other = swap(key_rows, 1), swap(value_rows, 1)
    cell_shapes = tuple(like(2, seqs, 2 * block >> level, half) for level in range(1, levels))
    wide = (pltpu.VMEM((2, seqs, half // 128, block, 128), F32),)
    own_cells = call(own_summary_body, cell_shapes, (core, key_rows, value_rows), "own_summaries", scalars=1, scratch=wide)
    cells = call(summary_body, cell_shapes, (core, k_other, v_other, *own_cells), "summaries", scalars=1, scratch=wide)
    qg_own, qg_send = call(
        split_body, (part, part), (core, queries, out_grad), "split_qg", scalars=1, hbm_in=2, copies=4
    )
    qg_other = swap(qg_send, 1)

    kv_own, kv_other = call(
        keep_body, (part, part), (core, key_rows, value_rows, k_other, v_other), "keep_halves", scalars=1
    )
    groups = seqs * heads
    far_size = block // 4
    token_rows, cell_rows, late_rows = 2 * block, 2 * block + far_size, block - far_size
    rows = token_rows + cell_rows + late_rows

    turned = call(
        functools.partial(turn_body, head), like(2, groups // 2, head, token_rows), (qg_own, qg_other), "turn"
    )

    def score(levels_of, pieces, count):
        product = like(groups // 2, count, token_rows, dtype=F32)
        return call(
            functools.partial(score_body, levels_of, head),
            (product, product, like(groups // 2, 8, token_rows, dtype=F32)),
            (core, level_slope, turned, *pieces),
            "scores",
            scalars=2,
            flops=40 * seqs * token_rows * count * half,
        )

    token_pieces = [kv_own, kv_other]
    token_scores = score((0, 0), token_pieces, token_rows)

    near_cells = swap(cells[0], 2)
    far_cells = swap(cells[2], 8)
    side_cells = swap(cells[1], 4)
    across = call(coarser_body, like(2, seqs, block // 2, half), (near_cells, token_scores[2]), "coarser")
    across_cells = swap(across, 4)
    far_side_cells = swap(far_cells, 4)
    relayed_cells = [swap(far_cells, 2), swap(far_side_cells, 2)]

    cell_pieces = [near_cells, side_cells, far_cells, far_side_cells, relayed_cells[0]]
    late_pieces = [across_cells, relayed_cells[1]]
    early = (*token_scores, *score((1, 2, 3, 3, 3), cell_pieces, cell_rows))
    runs = ((0, token_rows), (1, block), (2, block // 2), (3, far_size), (3, far_size))
    runs += ((3, far_size), (2, block // 2), (3, far_size))
    far_rows, tail = groups * far_size, heads
    slope_part = like(heads // 2, token_rows, dtype=F32)
    wide = like(*part.shape, dtype=F32)
    slope, across, relay, dscore, probs = call(
        functools.partial(attend_body, runs, head),
        (
            slope_part,
            like(2, seqs, block // 2, half),
            like(2 * far_rows + tail, head),
            like(groups // 2, rows, token_rows),
            like(groups // 2, rows, token_rows),
        ),
        (core, level_slope, *early, turned, qg_own, qg_other, *late_pieces),
        "attend",
        scalars=2,
        flops=40 * seqs * token_rows * rows * half,
        scratch=(
            pltpu.VMEM((groups // 2, late_rows, token_rows), F32),
            pltpu.VMEM((groups // 2, late_rows, token_rows), F32),
        ),
    )
    near, side, far_direct = call(
        functools.partial(cell_grads_body, head, (far_size, far_size)),
        (wide, like(groups * (block // 2), head), like(2 * far_rows, head, dtype=F32)),
        (dscore, probs, qg_own, qg_other),
        "cell_grads",
    )
    dq_part = like(seqs, block, half)
    dq_own, dq_send, own, other = call(
        functools.partial(own_grads_body, head),
        (dq_part, dq_part, wide, wide),
        (dscore, probs, qg_own, qg_other, *token_pieces, *cell_pieces, *late_pieces),
        "own_grads",
        flops=40 * seqs * token_rows * rows * half,
    )

    across_back = swap(across, 4)
    relay_back = swap(relay, 2)
    slopes = [swap(slope, 2 * y, dp) for dp in range(1, dp_count) for y in range(2)]
    dq_other = swap(dq_send, 1)
    message = like(far_rows + tail, head)
    slope, keep, far_side = call(
        relay_body,
        (slope_part, like(far_rows, head, dtype=F32), message),
        (far_direct, relay_back, slope, *slopes),
        "relay",
    )
    far_side_back = swap(far_side, 4)
    near_back = swap(call(fold_body, like(*near.shape), (near, across_back, slope), "fold"), 2)
    side_back = swap(side, 4)
    slope, far_total = call(meet_body, (slope_part, message), (keep, far_side_back, slope), "meet")
    far_back = swap(far_total, 8)
    whole = like(seqs, block, width)
    dq, done = call(
        join_body, (whole, slope_part), (core, dq_own, dq_other), "join_queries", scalars=1, hbm_out=1, copies=2
    )
    kept, others = [], []
    for kind in range(2):
        mine, sent = call(
            functools.partial(gather_body, kind, (1, 2, 3)),
            (dq_part, dq_part),
            (done, own, other, near_back, side_back, far_back),
            "gather_cells",
        )
        kept.append(mine)
        others.append(swap(sent, 1))
    slope = call(total_body, slope_part, (slope, far_back), "slope_terms")
    halves = call(
        keep_grads_body, (whole, whole), (core, *kept), "keep_grads", scalars=1, hbm_out=2, copies=2
    )
    dk, dv, slope_grad = call(
        join_pair_body,
        (whole, whole, like(1, heads, dtype=F32)),
        (core, *halves, *others, slope, swap(slope, 1)),
        "join_kv",
        scalars=1,
        hbm_in=2,
        hbm_out=3,
        copies=3,
        scratch=(pltpu.VMEM((1, heads), F32),),
        aliases={1: 0, 2: 1},
    )
    return dq, dk, dv, slope_grad.reshape(heads)


def as_sent(x):
    return jax.tree.map(lambda a: a.astype(jnp.bfloat16) if a.dtype == jnp.float32 else a, x)


def from_partner(value, axis, apart):
    mask = 2**apart
    pairs = [(source, source ^ mask) for source in range(lax.axis_size(axis))]
    return lax.ppermute(value, axis, pairs)


def pair_mean(cells):
    shaped = cells.reshape(cells.shape[:-2] + (cells.shape[-2] // 2, 2, cells.shape[-1])).astype(
        jnp.float32
    )
    return ((shaped[..., 0, :] + shaped[..., 1, :]) * 0.5).astype(jnp.bfloat16)


def merge_level(own_pair, other_pair, flag):
    merged = []
    for own_part, other_part in zip(own_pair, other_pair):
        own_small = pair_mean(own_part)
        other_small = pair_mean(other_part)
        merged.append(
            jnp.where(
                flag == 1,
                jnp.concatenate([other_small, own_small], axis=1),
                jnp.concatenate([own_small, other_small], axis=1),
            )
        )
    return tuple(merged)


def to_heads(rows, heads):
    seqs, count, width = rows.shape
    return jnp.transpose(rows.reshape(seqs, count, heads, width // heads), (0, 2, 1, 3))


def from_heads(split):
    seqs, heads, count, head = split.shape
    return jnp.transpose(split, (0, 2, 1, 3)).reshape(seqs, count, heads * head)


def product(form, left, right):
    return jnp.einsum(form, left, right, preferred_element_type=jnp.float32)


def attend(query_four, key_four, value_four, grad_four, level_slope, block):
    head = query_four.shape[3]
    key_count = key_four.shape[2]
    scale = 1.0 / math.sqrt(head)
    column = jnp.arange(key_count, dtype=jnp.int32)
    level_of = column // block - 1
    sibling = jnp.maximum(level_of, 0)
    multiple = jnp.where(level_of < 0, 1.0, jnp.exp2(sibling.astype(jnp.float32)))
    bias = level_slope[:, None] * sibling.astype(jnp.float32)[None, :]
    raw = product("shqd,shkd->shqk", query_four, key_four)
    scores = raw * scale + bias[None, :, None, :]
    top = jnp.max(scores, axis=-1, keepdims=True)
    weights = multiple[None, None, None, :] * jnp.exp(scores - top)
    probs = weights / jnp.sum(weights, axis=-1, keepdims=True)
    probs_low = probs.astype(jnp.bfloat16)
    output = product("shqk,shkd->shqd", probs_low, value_four)
    delta = jnp.sum(grad_four.astype(jnp.float32) * output, axis=-1)
    upstream = product("shqd,shkd->shqk", grad_four, value_four)
    dscore = probs * (upstream - delta[..., None])
    slope_part = jnp.sum(dscore * sibling.astype(jnp.float32)[None, None, None, :], axis=(0, 2, 3))
    dscore_low = dscore.astype(jnp.bfloat16)
    query_part = product("shqk,shkd->shqd", dscore_low, key_four) * scale
    key_part = product("shqk,shqd->shkd", dscore_low, query_four) * scale
    value_part = product("shqk,shqd->shkd", probs_low, grad_four)
    return (query_part, key_part, value_part, slope_part)


def split_level(grad_now, direct, flag, level, block):
    half = block // 2
    lower_src = grad_now[:, :, :half]
    upper_src = grad_now[:, :, half:]
    own_src = jnp.where(flag == 1, upper_src, lower_src)
    other_src = jnp.where(flag == 1, lower_src, upper_src)
    own_half = jnp.repeat(own_src, 2, axis=2) * 0.5
    other_half = jnp.repeat(other_src, 2, axis=2) * 0.5
    sent = (other_half + direct[:, :, (level + 1) * block : (level + 2) * block]).astype(
        jnp.bfloat16
    )
    return (own_half, sent)


def by_blocks(queries, key_rows, value_rows, out_grad, level_slope):
    seqs, block, width = queries.shape
    heads = level_slope.shape[0]
    ctx_count = lax.axis_size("ctx")
    levels = ctx_count.bit_length() - 1
    position = lax.axis_index("ctx")
    bit_list = [position // 2**level % 2 for level in range(levels)]
    own_pair = (key_rows, value_rows)
    partners = []
    for level in range(levels - 2):
        other_pair = jax.tree.map(
            lambda part, own: part.astype(own.dtype),
            from_partner(as_sent(own_pair), "ctx", level),
            own_pair,
        )
        partners.append(other_pair)
        own_pair = merge_level(own_pair, other_pair, bit_list[level])
    for level in range(levels - 2, levels):
        other_pair = jax.tree.map(
            lambda part, own: part.astype(own.dtype),
            from_partner(as_sent(own_pair), "ctx", level),
            own_pair,
        )
        partners.append(other_pair)
        if level + 1 < levels:
            own_pair = merge_level(own_pair, other_pair, bit_list[level])
    key_set = jnp.concatenate(
        [to_heads(key_rows, heads)] + [to_heads(pair[0], heads) for pair in partners], axis=2
    )
    value_set = jnp.concatenate(
        [to_heads(value_rows, heads)] + [to_heads(pair[1], heads) for pair in partners], axis=2
    )
    query_four = to_heads(queries, heads)
    grad_four = to_heads(out_grad, heads)
    query_part, key_part, value_part, slope_part = attend(
        query_four, key_set, value_set, grad_four, level_slope, block
    )
    slope_grad = lax.psum(slope_part, ("dp", "ctx"))
    head = width // heads
    grad_keys = jnp.zeros((seqs, heads, block, head), jnp.float32)
    grad_values = jnp.zeros((seqs, heads, block, head), jnp.float32)
    for level in reversed(range(levels)):
        own_keys, sent_keys = split_level(grad_keys, key_part, bit_list[level], level, block)
        own_values, sent_values = split_level(
            grad_values, value_part, bit_list[level], level, block
        )
        back_keys, back_values = from_partner((sent_keys, sent_values), "ctx", level)
        grad_keys = own_keys + back_keys.astype(jnp.float32)
        grad_values = own_values + back_values.astype(jnp.float32)
    key_grad = from_heads((grad_keys + key_part[:, :, :block]).astype(jnp.bfloat16))
    value_grad = from_heads((grad_values + value_part[:, :, :block]).astype(jnp.bfloat16))
    return (from_heads(query_part.astype(jnp.bfloat16)), key_grad, value_grad, slope_grad)


def shards(queries, key_rows, value_rows, out_grad, level_slope):
    heads, width = level_slope.shape[0], queries.shape[2]
    tiles = queries.shape[1] % 64 == 0 and heads % 16 == 0 and width // heads % 128 == 0
    few = lax.axis_size("ctx") == 16 and tiles
    form = paired if few else by_blocks
    return form(queries, key_rows, value_rows, out_grad, level_slope)


def solution(mesh):
    placed = (
        P("dp", "ctx", None),
        P("dp", "ctx", None),
        P("dp", "ctx", None),
        P("dp", "ctx", None),
        P(),
    )
    return jax.shard_map(
        shards,
        mesh=mesh,
        in_specs=placed,
        out_specs=(P("dp", "ctx", None), P("dp", "ctx", None), P("dp", "ctx", None), P()),
        check_vma=False,
    )
```

```python
import functools
import math

import jax
import jax.numpy as jnp
from jax import lax
from jax.experimental import pallas as pl
from jax.experimental.pallas import tpu as pltpu
from jax.sharding import PartitionSpec as P

F32, BF16 = jnp.float32, jnp.bfloat16
LOG2E = math.log2(math.e)
VMEM = pl.BlockSpec(memory_space=pltpu.VMEM)
SMEM = pl.BlockSpec(memory_space=pltpu.SMEM)
HBM = pl.BlockSpec(memory_space=pltpu.HBM)


def swap(value, apart, dp_apart=0):
    count = lax.axis_size("ctx")
    if not dp_apart:
        return lax.ppermute(value, "ctx", [(source, source ^ apart) for source in range(count)])
    mask = dp_apart * count + apart
    pairs = [(source, source ^ mask) for source in range(lax.axis_size("dp") * count)]
    return lax.ppermute(value, ("dp", "ctx"), pairs)


def like(*shape, dtype=BF16):
    return jax.ShapeDtypeStruct(shape, dtype)


def call(body, out_shape, operands, name, scalars=0, hbm_in=0, hbm_out=0, copies=0, flops=0, limit=32, scratch=(), aliases={}):
    moved = sum(a.size * a.dtype.itemsize for a in jax.tree.leaves((operands, out_shape)))
    count = len(operands) - scalars - hbm_in
    return pl.pallas_call(
        body,
        out_shape=out_shape,
        in_specs=[SMEM] * scalars + [HBM] * hbm_in + [VMEM] * count,
        out_specs=tuple(HBM if i < hbm_out else VMEM for i in range(len(out_shape)))
        if isinstance(out_shape, tuple)
        else VMEM,
        scratch_shapes=[*scratch, *([pltpu.SemaphoreType.DMA((copies,))] if copies else [])],
        compiler_params=pltpu.CompilerParams(vmem_limit_bytes=int(limit * 2**20)),
        cost_estimate=pl.CostEstimate(flops=flops, bytes_accessed=moved, transcendentals=0),
        input_output_aliases=aliases,
        name=name,
    )(*operands)


def dot(left, right, left_dim=1, right_dim=0):
    dims = (((left_dim,), (right_dim,)), ((), ()))
    return lax.dot_general(left, right, dims, preferred_element_type=F32)


def pair_matrix(rows):
    cell = lax.broadcasted_iota(jnp.int32, (rows, 2 * rows), 0)
    source = lax.broadcasted_iota(jnp.int32, (rows, 2 * rows), 1)
    return jnp.where(source // 2 == cell, 0.5, 0.0).astype(BF16)


def spread_matrix(rows, level):
    row = lax.broadcasted_iota(jnp.int32, (rows, rows >> level), 0)
    cell = lax.broadcasted_iota(jnp.int32, (rows, rows >> level), 1)
    return jnp.where(row >> level == cell, 0.5**level, 0.0).astype(BF16)


def two_parts(x):
    high = x.astype(BF16)
    return jnp.concatenate([high, (x - high.astype(F32)).astype(BF16)], axis=0)


def one_part(x):
    rows = x.shape[0] // 2
    return x[:rows].astype(F32) + x[rows:].astype(F32)


def head_halves(core, half):
    mine = pl.ds(pl.multiple_of(core[0] * half, half), half)
    theirs = pl.ds(pl.multiple_of((1 - core[0]) * half, half), half)
    return mine, theirs


def start_all(moves, sems):
    copies = [pltpu.make_async_copy(src, dst, sems.at[i]) for i, (src, dst) in enumerate(moves)]
    for copy in copies:
        copy.start()
    return copies


def copy_all(moves, sems):
    for copy in start_all(moves, sems):
        copy.wait()


def split_body(core, first, second, own, send, sems):
    mine, theirs = head_halves(core, own.shape[-1])
    moves = []
    for index, whole in enumerate((first, second)):
        moves.append((whole.at[:, :, theirs], send.at[index]))
        moves.append((whole.at[:, :, mine], own.at[index]))
    copy_all(moves, sems)


def keep_body(core, k, v, k_other, v_other, own, other):
    mine, _ = head_halves(core, own.shape[-1])
    for index, (first, second) in enumerate(((k, k_other), (v, v_other))):
        own[index] = first[:, :, mine]
        other[index] = second[:, :, mine]


def halve(rows, wide):
    count = rows.shape[0]
    wide[pl.ds(0, count), :] = rows
    return (wide[pl.ds(0, count // 2, stride=2), :] + wide[pl.ds(1, count // 2, stride=2), :]) * 0.5


def tiles_of(shape, core, wide):
    kinds, seqs, _, half = shape
    for kind in range(kinds):
        for seq in range(seqs):
            for start in range(0, half, 128):
                source = pl.ds(pl.multiple_of(core[0] * half + start, 128), 128)
                yield kind, seq, source, slice(start, start + 128), wide.at[kind, seq, start // 128]


def own_summary_body(core, k, v, *refs):
    *cells, wide = refs
    for kind, seq, source, lanes, scratch in tiles_of(cells[0].shape, core, wide):
        rows = (k, v)[kind][seq, :, source].astype(F32)
        for out in cells:
            rows = halve(rows, scratch)
            out[kind, seq, :, lanes] = jnp.concatenate([rows, jnp.zeros_like(rows)], axis=0).astype(BF16)
            rows = rows.astype(BF16).astype(F32)


def summary_body(core, k_other, v_other, *refs):
    *refs, wide = refs
    own, cells = refs[: len(refs) // 2], refs[len(refs) // 2 :]
    for kind, seq, source, lanes, scratch in tiles_of(cells[0].shape, core, wide):
        rows = (k_other, v_other)[kind][seq, :, source].astype(F32)
        for first, out in zip(own, cells):
            rows = halve(rows, scratch)
            before = first[kind, seq, :, lanes].astype(F32)[: rows.shape[0]]
            out[kind, seq, :, lanes] = jnp.concatenate([before, rows], axis=0).astype(BF16)
            rows = rows.astype(BF16).astype(F32)


def coarser_body(cells, done, out):
    for kind in range(cells.shape[0]):
        for seq in range(cells.shape[1]):
            rows = cells[kind, seq]
            out[kind, seq] = dot(pair_matrix(rows.shape[0] // 2), rows).astype(BF16)


def stacked(parts, kind, seq, lanes):
    return jnp.concatenate([part[kind, seq, :, lanes] for part in parts], axis=0)


def turn_body(head, qg_own, qg_other, turned):
    kinds, seqs, _, width = qg_own.shape
    heads = width // head
    for kind in range(kinds):
        for h in range(heads):
            for seq in range(seqs):
                lanes = slice(h * head, (h + 1) * head)
                turned[kind, seq * heads + h] = stacked((qg_own, qg_other), kind, seq, lanes).T


def score_body(levels_of, head, core, slope, turned, *refs):
    *pieces, weights, upstream, stats = refs
    seqs, width = pieces[0].shape[1], pieces[0].shape[3]
    heads = width // head
    scale = LOG2E / math.sqrt(head)
    for h in range(heads):
        lanes = slice(h * head, (h + 1) * head)
        step = slope[core[0] * heads + h] * LOG2E + 1.0
        for seq in range(seqs):
            at = seq * heads + h
            raw = dot(stacked(pieces, 0, seq, lanes), turned[0, at])
            upstream[at] = dot(stacked(pieces, 1, seq, lanes), turned[1, at])
            scores = with_bias(raw * scale, zip(levels_of, [piece.shape[2] for piece in pieces]), step)
            top = jnp.max(scores, axis=0, keepdims=True)
            spread = jnp.exp2(scores - top)
            weights[at] = spread
            stats[at, 0:1] = top
            stats[at, 1:2] = jnp.sum(spread, axis=0, keepdims=True)


def with_bias(scores, runs, step):
    parts, start = [], 0
    for level, count in runs:
        part = scores[start : start + count]
        parts.append(part + step * float(level) if level else part)
        start += count
    return jnp.concatenate(parts, axis=0)


def by_eights(x):
    return jnp.sum(x.reshape(x.shape[0] // 8, 8, x.shape[1]), axis=0)


def attend_body(runs, head, core, slope, *refs):
    *refs, late_scores, late_up = refs
    early, (turned, qg_own, qg_other, *late), outs = refs[:6], refs[6:-5], refs[-5:]
    slope_out, across, relay, dscore_out, probs_out = outs
    seqs, block, width = qg_own.shape[1:]
    heads = width // head
    scale = 1.0 / math.sqrt(head)
    starts = [sum(rows for _, rows in runs[:i]) for i in range(len(runs) + 1)]
    token_rows = early[0].shape[1]
    early_rows = token_rows + early[3].shape[1]
    bounds = (0, token_rows, early_rows, starts[-1])
    late_runs = [run for run, start in zip(runs, starts) if start >= early_rows]
    sent_rows, far_size = starts[-4], runs[-1][1]
    slab = 2 * seqs * heads * far_size

    def score(h, seq):
        at, lanes = seq * heads + h, slice(h * head, (h + 1) * head)
        step = slope[core[0] * heads + h] * LOG2E + 1.0
        raw = dot(stacked(late, 0, seq, lanes), turned[0, at])
        late_scores[at] = with_bias(raw * (scale * LOG2E), late_runs, step)
        late_up[at] = dot(stacked(late, 1, seq, lanes), turned[1, at])

    def normalise(h, seq):
        at = seq * heads + h
        tops = early[2][at, 0:1], early[5][at, 0:1]
        scores = late_scores[at]
        top = jnp.maximum(jnp.maximum(*tops), jnp.max(scores, axis=0, keepdims=True))
        shares = [jnp.exp2(part - top) for part in tops]
        weights = jnp.exp2(scores - top)
        total = early[2][at, 1:2] * shares[0] + early[5][at, 1:2] * shares[1]
        inverse = 1.0 / (total + jnp.sum(weights, axis=0, keepdims=True))
        probs = [early[0][at] * (shares[0] * inverse), early[3][at] * (shares[1] * inverse), weights * inverse]
        upstream = [early[1][at], early[4][at], late_up[at]]
        probs_low = [part.astype(BF16) for part in probs]
        delta = sum(by_eights(p.astype(F32) * u) for p, u in zip(probs_low, upstream))
        delta = jnp.sum(delta, axis=0, keepdims=True)
        slope_sum = jnp.zeros((8, token_rows), F32)
        for p, u, low, high in zip(probs, upstream, bounds, bounds[1:]):
            dscore = p * (u - delta)
            for (level, rows), start in zip(runs, starts):
                if level and low <= start < high:
                    here = dscore[start - low : start - low + rows]
                    slope_sum = slope_sum + by_eights(here) * float(level)
            dscore_out[at, low:high] = dscore.astype(BF16)
        probs_out[at] = jnp.concatenate(probs_low, axis=0)
        return slope_sum

    def gradients(h, seq):
        at, lanes = seq * heads + h, slice(h * head, (h + 1) * head)
        dk = dot(dscore_out[at, sent_rows:], stacked((qg_own, qg_other), 0, seq, lanes)) * scale
        dv = dot(probs_out[at, sent_rows:], stacked((qg_own, qg_other), 1, seq, lanes))
        for kind, direct in enumerate((dk, dv)):
            group = (kind * seqs + seq) * heads + h
            first, direct = direct[:far_size], direct[far_size:]
            across[kind, seq, :, lanes] = direct[:-far_size].astype(BF16)
            relay[pl.ds(group * far_size, far_size), :] = first.astype(BF16)
            relay[pl.ds(slab + group * far_size, far_size), :] = direct[-far_size:].astype(BF16)

    items = [(h, seq) for h in range(heads) for seq in range(seqs)]
    behind = 4
    sums = {}
    for i in range(len(items) + 2 * behind):
        if i < len(items):
            score(*items[i])
        if 0 <= i - behind < len(items):
            item = items[i - behind]
            sums[item] = normalise(*item)
        if 0 <= i - 2 * behind < len(items):
            gradients(*items[i - 2 * behind])
    for h in range(heads):
        slope_out[h : h + 1, :] = jnp.sum(sum(sums[h, seq] for seq in range(seqs)), axis=0, keepdims=True)
    relay[pl.ds(2 * slab, 2 * heads), :] = two_parts(slope_out[...])


def cell_grads_body(head, far_sizes, dscore, probs, qg_own, qg_other, near, side, far):
    seqs, block, width = qg_own.shape[1:]
    heads = width // head
    scale = 1.0 / math.sqrt(head)
    sizes = (block, block // 2, *far_sizes)
    rows = slice(2 * block, 2 * block + sum(sizes))
    for h in range(heads):
        lanes = slice(h * head, (h + 1) * head)
        for seq in range(seqs):
            at = seq * heads + h
            dk = dot(dscore[at, rows], stacked((qg_own, qg_other), 0, seq, lanes)) * scale
            dv = dot(probs[at, rows], stacked((qg_own, qg_other), 1, seq, lanes))
            for kind, direct in enumerate((dk, dv)):
                group = (kind * seqs + seq) * heads + h
                near[kind, seq, :, lanes] = direct[:block]
                start = block + sizes[1]
                side[pl.ds(group * sizes[1], sizes[1]), :] = direct[block:start].astype(BF16)
                slab = 0
                for size in far_sizes:
                    far[pl.ds(slab + group * size, size), :] = direct[start : start + size]
                    start += size
                    slab += 2 * seqs * heads * size


def own_grads_body(head, dscore, probs, qg_own, qg_other, *refs):
    *pieces, dq_own, dq_send, own, other = refs
    seqs, block, width = qg_own.shape[1:]
    heads = width // head
    scale = 1.0 / math.sqrt(head)
    for h in range(heads):
        lanes = slice(h * head, (h + 1) * head)
        for seq in range(seqs):
            at = seq * heads + h
            dq = (dot(dscore[at], stacked(pieces, 0, seq, lanes), 0, 0) * scale).astype(BF16)
            dq_own[seq, :, lanes] = dq[:block]
            dq_send[seq, :, lanes] = dq[block:]
            dk = dot(dscore[at, : 2 * block], stacked((qg_own, qg_other), 0, seq, lanes)) * scale
            dv = dot(probs[at, : 2 * block], stacked((qg_own, qg_other), 1, seq, lanes))
            for kind, direct in enumerate((dk, dv)):
                own[kind, seq, :, lanes] = direct[:block]
                other[kind, seq, :, lanes] = direct[block:]


def fold_body(direct, coarse, done, out):
    rows = direct.shape[2]
    for kind in range(direct.shape[0]):
        for seq in range(direct.shape[1]):
            spread = dot(spread_matrix(rows, 1), coarse[kind, seq])
            out[kind, seq] = (direct[kind, seq] + spread).astype(BF16)


def relay_body(far, back, slope, *refs):
    *slopes, slope_out, keep, message = refs
    rows = keep.shape[0]
    total = slope[...] + one_part(back[pl.ds(2 * rows, 2 * slope.shape[0]), :])
    for ref in slopes:
        total = total + ref[...]
    slope_out[...] = total
    keep[...] = far[pl.ds(0, rows), :] + back[pl.ds(0, rows), :].astype(F32)
    message[pl.ds(0, rows), :] = (far[pl.ds(rows, rows), :] + back[pl.ds(rows, rows), :].astype(F32)).astype(BF16)
    message[pl.ds(rows, 2 * slope.shape[0]), :] = two_parts(total)


def meet_body(keep, back, slope, slope_out, message):
    rows = keep.shape[0]
    total = slope[...] + one_part(back[pl.ds(rows, 2 * slope.shape[0]), :])
    slope_out[...] = total
    message[pl.ds(0, rows), :] = (keep[...] + back[pl.ds(0, rows), :].astype(F32)).astype(BF16)
    message[pl.ds(rows, 2 * slope.shape[0]), :] = two_parts(total)


def gather_body(kind, levels_of, own, other, near, *refs):
    back, (kept, sent) = refs[:-2], refs[-2:]
    _, seqs, block, width = own.shape
    sizes = [2 * block >> level for level in levels_of[1:]]
    head = back[0].shape[1]
    spread = jnp.concatenate([spread_matrix(2 * block, level) for level in levels_of], axis=1)
    for seq in range(seqs):
        for h in range(width // head):
            lanes = slice(h * head, (h + 1) * head)
            group = (kind * seqs + seq) * (width // head) + h
            cells = [near[kind, seq, :, lanes]]
            cells += [part[pl.ds(group * size, size), :] for part, size in zip(back, sizes)]
            total = dot(spread, jnp.concatenate(cells, axis=0))
            kept[seq, :, lanes] = (own[kind, seq, :, lanes] + total[:block]).astype(BF16)
            sent[seq, :, lanes] = (other[kind, seq, :, lanes] + total[block:]).astype(BF16)


def total_body(slope, far, out):
    rows = 2 * slope.shape[0]
    out[...] = slope[...] + one_part(far[pl.ds(far.shape[0] - rows, rows), :])


def keep_grads_body(core, dq, dk, dv, *refs):
    *outs, sems = refs
    mine, _ = head_halves(core, dk.shape[-1])
    copy_all([(half, out.at[:, :, mine]) for half, out in zip((dq, dk, dv), outs)], sems)


def join_grads_body(core, dq_half, dk_half, dv_half, dq, dk, dv, slope, slope_other, *refs):
    *outs, slope_out, sums, sems = refs
    _, theirs = head_halves(core, dk.shape[-1])
    moves = [(half, out.at[:, :, theirs]) for half, out in zip((dq, dk, dv), outs)]
    copies = start_all(moves, sems)
    ours, rest = slope[...], slope_other[...]
    lower = jnp.where(core[0] == 0, ours, rest)
    upper = jnp.where(core[0] == 0, rest, ours)
    terms = jnp.concatenate([lower, upper], axis=0)
    sums[...] = jnp.sum(terms.T, axis=0, keepdims=True)
    last = pltpu.make_async_copy(sums, slope_out, sems.at[len(moves)])
    last.start()
    for copy in (*copies, last):
        copy.wait()


def paired(queries, key_rows, value_rows, out_grad, level_slope):
    seqs, block, width = queries.shape
    heads = level_slope.shape[0]
    half, head = width // 2, width // heads
    dp_count = lax.axis_size("dp")
    levels = 4
    position = lax.axis_index("ctx")
    core = (position % 2).astype(jnp.int32).reshape(1)

    part = like(2, seqs, block, half)
    k_other, v_other = swap(key_rows, 1), swap(value_rows, 1)
    cell_shapes = tuple(like(2, seqs, 2 * block >> level, half) for level in range(1, levels))
    wide = (pltpu.VMEM((2, seqs, half // 128, block, 128), F32),)
    own_cells = call(own_summary_body, cell_shapes, (core, key_rows, value_rows), "own_summaries", scalars=1, scratch=wide)
    cells = call(summary_body, cell_shapes, (core, k_other, v_other, *own_cells), "summaries", scalars=1, scratch=wide)
    qg_own, qg_send = call(
        split_body, (part, part), (core, queries, out_grad), "split_qg", scalars=1, hbm_in=2, copies=4
    )
    qg_other = swap(qg_send, 1)

    kv_own, kv_other = call(
        keep_body, (part, part), (core, key_rows, value_rows, k_other, v_other), "keep_halves", scalars=1
    )
    groups = seqs * heads
    far_size = block // 4
    token_rows, cell_rows, late_rows = 2 * block, 2 * block + far_size, block - far_size
    rows = token_rows + cell_rows + late_rows

    turned = call(
        functools.partial(turn_body, head), like(2, groups // 2, head, token_rows), (qg_own, qg_other), "turn"
    )

    def score(levels_of, pieces, count):
        product = like(groups // 2, count, token_rows, dtype=F32)
        return call(
            functools.partial(score_body, levels_of, head),
            (product, product, like(groups // 2, 8, token_rows, dtype=F32)),
            (core, level_slope, turned, *pieces),
            "scores",
            scalars=2,
            flops=40 * seqs * token_rows * count * half,
        )

    token_pieces = [kv_own, kv_other]
    token_scores = score((0, 0), token_pieces, token_rows)

    near_cells = swap(cells[0], 2)
    far_cells = swap(cells[2], 8)
    side_cells = swap(cells[1], 4)
    across = call(coarser_body, like(2, seqs, block // 2, half), (near_cells, token_scores[2]), "coarser")
    across_cells = swap(across, 4)
    far_side_cells = swap(far_cells, 4)
    relayed_cells = [swap(far_cells, 2), swap(far_side_cells, 2)]

    cell_pieces = [near_cells, side_cells, far_cells, far_side_cells, relayed_cells[0]]
    late_pieces = [across_cells, relayed_cells[1]]
    early = (*token_scores, *score((1, 2, 3, 3, 3), cell_pieces, cell_rows))
    runs = ((0, token_rows), (1, block), (2, block // 2), (3, far_size), (3, far_size))
    runs += ((3, far_size), (2, block // 2), (3, far_size))
    far_rows, tail = groups * far_size, heads
    slope_part = like(heads // 2, token_rows, dtype=F32)
    wide = like(*part.shape, dtype=F32)
    slope, across, relay, dscore, probs = call(
        functools.partial(attend_body, runs, head),
        (
            slope_part,
            like(2, seqs, block // 2, half),
            like(2 * far_rows + tail, head),
            like(groups // 2, rows, token_rows),
            like(groups // 2, rows, token_rows),
        ),
        (core, level_slope, *early, turned, qg_own, qg_other, *late_pieces),
        "attend",
        scalars=2,
        flops=40 * seqs * token_rows * rows * half,
        scratch=(
            pltpu.VMEM((groups // 2, late_rows, token_rows), F32),
            pltpu.VMEM((groups // 2, late_rows, token_rows), F32),
        ),
    )
    near, side, far_direct = call(
        functools.partial(cell_grads_body, head, (far_size, far_size)),
        (wide, like(groups * (block // 2), head), like(2 * far_rows, head, dtype=F32)),
        (dscore, probs, qg_own, qg_other),
        "cell_grads",
    )
    dq_part = like(seqs, block, half)
    dq_own, dq_send, own, other = call(
        functools.partial(own_grads_body, head),
        (dq_part, dq_part, wide, wide),
        (dscore, probs, qg_own, qg_other, *token_pieces, *cell_pieces, *late_pieces),
        "own_grads",
        flops=40 * seqs * token_rows * rows * half,
    )

    across_back = swap(across, 4)
    relay_back = swap(relay, 2)
    slopes = [swap(slope, 2 * y, dp) for dp in range(1, dp_count) for y in range(2)]
    dq_other = swap(dq_send, 1)
    message = like(far_rows + tail, head)
    slope, keep, far_side = call(
        relay_body,
        (slope_part, like(far_rows, head, dtype=F32), message),
        (far_direct, relay_back, slope, *slopes),
        "relay",
    )
    far_side_back = swap(far_side, 4)
    near_back = swap(call(fold_body, like(*near.shape), (near, across_back, slope), "fold"), 2)
    side_back = swap(side, 4)
    slope, far_total = call(meet_body, (slope_part, message), (keep, far_side_back, slope), "meet", flops=int(4e9))
    far_back = swap(far_total, 8)
    whole = like(seqs, block, width)
    kept, others = [], []
    for kind in range(2):
        mine, sent = call(
            functools.partial(gather_body, kind, (1, 2, 3)),
            (dq_part, dq_part),
            (own, other, near_back, side_back, far_back),
            "gather_cells",
        )
        kept.append(mine)
        others.append(swap(sent, 1))
    slope = call(total_body, slope_part, (slope, far_back), "slope_terms")
    halves = call(
        keep_grads_body, (whole,) * 3, (core, dq_own, *kept), "keep_grads", scalars=1, hbm_out=3, copies=3
    )
    dq, dk, dv, slope_grad = call(
        join_grads_body,
        (whole, whole, whole, like(1, heads, dtype=F32)),
        (core, *halves, dq_other, *others, slope, swap(slope, 1)),
        "join_grads",
        scalars=1,
        hbm_in=3,
        hbm_out=4,
        copies=4,
        scratch=(pltpu.VMEM((1, heads), F32),),
        aliases={1: 0, 2: 1, 3: 2},
    )
    return dq, dk, dv, slope_grad.reshape(heads)


def as_sent(x):
    return jax.tree.map(lambda a: a.astype(jnp.bfloat16) if a.dtype == jnp.float32 else a, x)


def from_partner(value, axis, apart):
    mask = 2**apart
    pairs = [(source, source ^ mask) for source in range(lax.axis_size(axis))]
    return lax.ppermute(value, axis, pairs)


def pair_mean(cells):
    shaped = cells.reshape(cells.shape[:-2] + (cells.shape[-2] // 2, 2, cells.shape[-1])).astype(
        jnp.float32
    )
    return ((shaped[..., 0, :] + shaped[..., 1, :]) * 0.5).astype(jnp.bfloat16)


def merge_level(own_pair, other_pair, flag):
    merged = []
    for own_part, other_part in zip(own_pair, other_pair):
        own_small = pair_mean(own_part)
        other_small = pair_mean(other_part)
        merged.append(
            jnp.where(
                flag == 1,
                jnp.concatenate([other_small, own_small], axis=1),
                jnp.concatenate([own_small, other_small], axis=1),
            )
        )
    return tuple(merged)


def to_heads(rows, heads):
    seqs, count, width = rows.shape
    return jnp.transpose(rows.reshape(seqs, count, heads, width // heads), (0, 2, 1, 3))


def from_heads(split):
    seqs, heads, count, head = split.shape
    return jnp.transpose(split, (0, 2, 1, 3)).reshape(seqs, count, heads * head)


def product(form, left, right):
    return jnp.einsum(form, left, right, preferred_element_type=jnp.float32)


def attend(query_four, key_four, value_four, grad_four, level_slope, block):
    head = query_four.shape[3]
    key_count = key_four.shape[2]
    scale = 1.0 / math.sqrt(head)
    column = jnp.arange(key_count, dtype=jnp.int32)
    level_of = column // block - 1
    sibling = jnp.maximum(level_of, 0)
    multiple = jnp.where(level_of < 0, 1.0, jnp.exp2(sibling.astype(jnp.float32)))
    bias = level_slope[:, None] * sibling.astype(jnp.float32)[None, :]
    raw = product("shqd,shkd->shqk", query_four, key_four)
    scores = raw * scale + bias[None, :, None, :]
    top = jnp.max(scores, axis=-1, keepdims=True)
    weights = multiple[None, None, None, :] * jnp.exp(scores - top)
    probs = weights / jnp.sum(weights, axis=-1, keepdims=True)
    probs_low = probs.astype(jnp.bfloat16)
    output = product("shqk,shkd->shqd", probs_low, value_four)
    delta = jnp.sum(grad_four.astype(jnp.float32) * output, axis=-1)
    upstream = product("shqd,shkd->shqk", grad_four, value_four)
    dscore = probs * (upstream - delta[..., None])
    slope_part = jnp.sum(dscore * sibling.astype(jnp.float32)[None, None, None, :], axis=(0, 2, 3))
    dscore_low = dscore.astype(jnp.bfloat16)
    query_part = product("shqk,shkd->shqd", dscore_low, key_four) * scale
    key_part = product("shqk,shqd->shkd", dscore_low, query_four) * scale
    value_part = product("shqk,shqd->shkd", probs_low, grad_four)
    return (query_part, key_part, value_part, slope_part)


def split_level(grad_now, direct, flag, level, block):
    half = block // 2
    lower_src = grad_now[:, :, :half]
    upper_src = grad_now[:, :, half:]
    own_src = jnp.where(flag == 1, upper_src, lower_src)
    other_src = jnp.where(flag == 1, lower_src, upper_src)
    own_half = jnp.repeat(own_src, 2, axis=2) * 0.5
    other_half = jnp.repeat(other_src, 2, axis=2) * 0.5
    sent = (other_half + direct[:, :, (level + 1) * block : (level + 2) * block]).astype(
        jnp.bfloat16
    )
    return (own_half, sent)


def by_blocks(queries, key_rows, value_rows, out_grad, level_slope):
    seqs, block, width = queries.shape
    heads = level_slope.shape[0]
    ctx_count = lax.axis_size("ctx")
    levels = ctx_count.bit_length() - 1
    position = lax.axis_index("ctx")
    bit_list = [position // 2**level % 2 for level in range(levels)]
    own_pair = (key_rows, value_rows)
    partners = []
    for level in range(levels - 2):
        other_pair = jax.tree.map(
            lambda part, own: part.astype(own.dtype),
            from_partner(as_sent(own_pair), "ctx", level),
            own_pair,
        )
        partners.append(other_pair)
        own_pair = merge_level(own_pair, other_pair, bit_list[level])
    for level in range(levels - 2, levels):
        other_pair = jax.tree.map(
            lambda part, own: part.astype(own.dtype),
            from_partner(as_sent(own_pair), "ctx", level),
            own_pair,
        )
        partners.append(other_pair)
        if level + 1 < levels:
            own_pair = merge_level(own_pair, other_pair, bit_list[level])
    key_set = jnp.concatenate(
        [to_heads(key_rows, heads)] + [to_heads(pair[0], heads) for pair in partners], axis=2
    )
    value_set = jnp.concatenate(
        [to_heads(value_rows, heads)] + [to_heads(pair[1], heads) for pair in partners], axis=2
    )
    query_four = to_heads(queries, heads)
    grad_four = to_heads(out_grad, heads)
    query_part, key_part, value_part, slope_part = attend(
        query_four, key_set, value_set, grad_four, level_slope, block
    )
    slope_grad = lax.psum(slope_part, ("dp", "ctx"))
    head = width // heads
    grad_keys = jnp.zeros((seqs, heads, block, head), jnp.float32)
    grad_values = jnp.zeros((seqs, heads, block, head), jnp.float32)
    for level in reversed(range(levels)):
        own_keys, sent_keys = split_level(grad_keys, key_part, bit_list[level], level, block)
        own_values, sent_values = split_level(
            grad_values, value_part, bit_list[level], level, block
        )
        back_keys, back_values = from_partner((sent_keys, sent_values), "ctx", level)
        grad_keys = own_keys + back_keys.astype(jnp.float32)
        grad_values = own_values + back_values.astype(jnp.float32)
    key_grad = from_heads((grad_keys + key_part[:, :, :block]).astype(jnp.bfloat16))
    value_grad = from_heads((grad_values + value_part[:, :, :block]).astype(jnp.bfloat16))
    return (from_heads(query_part.astype(jnp.bfloat16)), key_grad, value_grad, slope_grad)


def shards(queries, key_rows, value_rows, out_grad, level_slope):
    heads, width = level_slope.shape[0], queries.shape[2]
    tiles = queries.shape[1] % 64 == 0 and heads % 16 == 0 and width // heads % 128 == 0
    few = lax.axis_size("ctx") == 16 and tiles
    form = paired if few else by_blocks
    return form(queries, key_rows, value_rows, out_grad, level_slope)


def solution(mesh):
    placed = (
        P("dp", "ctx", None),
        P("dp", "ctx", None),
        P("dp", "ctx", None),
        P("dp", "ctx", None),
        P(),
    )
    return jax.shard_map(
        shards,
        mesh=mesh,
        in_specs=placed,
        out_specs=(P("dp", "ctx", None), P("dp", "ctx", None), P("dp", "ctx", None), P()),
        check_vma=False,
    )
```

```python
import functools
import math

import jax
import jax.numpy as jnp
from jax import lax
from jax.experimental import pallas as pl
from jax.experimental.pallas import tpu as pltpu
from jax.sharding import PartitionSpec as P

F32, BF16 = jnp.float32, jnp.bfloat16
LOG2E = math.log2(math.e)
VMEM = pl.BlockSpec(memory_space=pltpu.VMEM)
SMEM = pl.BlockSpec(memory_space=pltpu.SMEM)
HBM = pl.BlockSpec(memory_space=pltpu.HBM)


def swap(value, apart, dp_apart=0):
    count = lax.axis_size("ctx")
    if not dp_apart:
        return lax.ppermute(value, "ctx", [(source, source ^ apart) for source in range(count)])
    mask = dp_apart * count + apart
    pairs = [(source, source ^ mask) for source in range(lax.axis_size("dp") * count)]
    return lax.ppermute(value, ("dp", "ctx"), pairs)


def like(*shape, dtype=BF16):
    return jax.ShapeDtypeStruct(shape, dtype)


def call(body, out_shape, operands, name, scalars=0, hbm_in=0, hbm_out=0, copies=0, flops=0, limit=32, scratch=(), aliases={}):
    moved = sum(a.size * a.dtype.itemsize for a in jax.tree.leaves((operands, out_shape)))
    count = len(operands) - scalars - hbm_in
    return pl.pallas_call(
        body,
        out_shape=out_shape,
        in_specs=[SMEM] * scalars + [HBM] * hbm_in + [VMEM] * count,
        out_specs=tuple(HBM if i < hbm_out else VMEM for i in range(len(out_shape)))
        if isinstance(out_shape, tuple)
        else VMEM,
        scratch_shapes=[*scratch, *([pltpu.SemaphoreType.DMA((copies,))] if copies else [])],
        compiler_params=pltpu.CompilerParams(vmem_limit_bytes=int(limit * 2**20)),
        cost_estimate=pl.CostEstimate(flops=flops, bytes_accessed=moved, transcendentals=0),
        input_output_aliases=aliases,
        name=name,
    )(*operands)


def dot(left, right, left_dim=1, right_dim=0):
    dims = (((left_dim,), (right_dim,)), ((), ()))
    return lax.dot_general(left, right, dims, preferred_element_type=F32)


def pair_matrix(rows):
    cell = lax.broadcasted_iota(jnp.int32, (rows, 2 * rows), 0)
    source = lax.broadcasted_iota(jnp.int32, (rows, 2 * rows), 1)
    return jnp.where(source // 2 == cell, 0.5, 0.0).astype(BF16)


def spread_matrix(rows, level):
    row = lax.broadcasted_iota(jnp.int32, (rows, rows >> level), 0)
    cell = lax.broadcasted_iota(jnp.int32, (rows, rows >> level), 1)
    return jnp.where(row >> level == cell, 0.5**level, 0.0).astype(BF16)


def two_parts(x):
    high = x.astype(BF16)
    return jnp.concatenate([high, (x - high.astype(F32)).astype(BF16)], axis=0)


def one_part(x):
    rows = x.shape[0] // 2
    return x[:rows].astype(F32) + x[rows:].astype(F32)


def head_halves(core, half):
    mine = pl.ds(pl.multiple_of(core[0] * half, half), half)
    theirs = pl.ds(pl.multiple_of((1 - core[0]) * half, half), half)
    return mine, theirs


def start_all(moves, sems):
    copies = [pltpu.make_async_copy(src, dst, sems.at[i]) for i, (src, dst) in enumerate(moves)]
    for copy in copies:
        copy.start()
    return copies


def copy_all(moves, sems):
    for copy in start_all(moves, sems):
        copy.wait()


def split_body(core, first, second, own, send, sems):
    mine, theirs = head_halves(core, own.shape[-1])
    moves = []
    for index, whole in enumerate((first, second)):
        moves.append((whole.at[:, :, theirs], send.at[index]))
        moves.append((whole.at[:, :, mine], own.at[index]))
    copy_all(moves, sems)


def keep_body(core, k, v, k_other, v_other, own, other):
    mine, _ = head_halves(core, own.shape[-1])
    for index, (first, second) in enumerate(((k, k_other), (v, v_other))):
        own[index] = first[:, :, mine]
        other[index] = second[:, :, mine]


def halve(rows, wide):
    count = rows.shape[0]
    wide[pl.ds(0, count), :] = rows
    return (wide[pl.ds(0, count // 2, stride=2), :] + wide[pl.ds(1, count // 2, stride=2), :]) * 0.5


def tiles_of(shape, core, wide):
    kinds, seqs, _, half = shape
    for kind in range(kinds):
        for seq in range(seqs):
            for start in range(0, half, 128):
                source = pl.ds(pl.multiple_of(core[0] * half + start, 128), 128)
                yield kind, seq, source, slice(start, start + 128), wide.at[kind, seq, start // 128]


def own_summary_body(core, k, v, *refs):
    *cells, wide = refs
    for kind, seq, source, lanes, scratch in tiles_of(cells[0].shape, core, wide):
        rows = (k, v)[kind][seq, :, source].astype(F32)
        for out in cells:
            rows = halve(rows, scratch)
            out[kind, seq, :, lanes] = jnp.concatenate([rows, jnp.zeros_like(rows)], axis=0).astype(BF16)
            rows = rows.astype(BF16).astype(F32)


def summary_body(core, k_other, v_other, *refs):
    *refs, wide = refs
    own, cells = refs[: len(refs) // 2], refs[len(refs) // 2 :]
    for kind, seq, source, lanes, scratch in tiles_of(cells[0].shape, core, wide):
        rows = (k_other, v_other)[kind][seq, :, source].astype(F32)
        for first, out in zip(own, cells):
            rows = halve(rows, scratch)
            before = first[kind, seq, :, lanes].astype(F32)[: rows.shape[0]]
            out[kind, seq, :, lanes] = jnp.concatenate([before, rows], axis=0).astype(BF16)
            rows = rows.astype(BF16).astype(F32)


def coarser_body(cells, done, out):
    for kind in range(cells.shape[0]):
        for seq in range(cells.shape[1]):
            rows = cells[kind, seq]
            out[kind, seq] = dot(pair_matrix(rows.shape[0] // 2), rows).astype(BF16)


def stacked(parts, kind, seq, lanes):
    return jnp.concatenate([part[kind, seq, :, lanes] for part in parts], axis=0)


def turn_body(head, qg_own, qg_other, turned):
    kinds, seqs, _, width = qg_own.shape
    heads = width // head
    for kind in range(kinds):
        for h in range(heads):
            for seq in range(seqs):
                lanes = slice(h * head, (h + 1) * head)
                turned[kind, seq * heads + h] = stacked((qg_own, qg_other), kind, seq, lanes).T


def score_body(levels_of, head, core, slope, turned, *refs):
    *pieces, weights, upstream, stats = refs
    seqs, width = pieces[0].shape[1], pieces[0].shape[3]
    heads = width // head
    scale = LOG2E / math.sqrt(head)
    for h in range(heads):
        lanes = slice(h * head, (h + 1) * head)
        step = slope[core[0] * heads + h] * LOG2E + 1.0
        for seq in range(seqs):
            at = seq * heads + h
            raw = dot(stacked(pieces, 0, seq, lanes), turned[0, at])
            upstream[at] = dot(stacked(pieces, 1, seq, lanes), turned[1, at])
            scores = with_bias(raw * scale, zip(levels_of, [piece.shape[2] for piece in pieces]), step)
            top = jnp.max(scores, axis=0, keepdims=True)
            spread = jnp.exp2(scores - top)
            weights[at] = spread
            stats[at, 0:1] = top
            stats[at, 1:2] = jnp.sum(spread, axis=0, keepdims=True)


def with_bias(scores, runs, step):
    parts, start = [], 0
    for level, count in runs:
        part = scores[start : start + count]
        parts.append(part + step * float(level) if level else part)
        start += count
    return jnp.concatenate(parts, axis=0)


def by_eights(x):
    return jnp.sum(x.reshape(x.shape[0] // 8, 8, x.shape[1]), axis=0)


def attend_body(runs, head, core, slope, *refs):
    *refs, late_scores, late_up = refs
    early, (turned, qg_own, qg_other, *late), outs = refs[:6], refs[6:-5], refs[-5:]
    slope_out, across, relay, dscore_out, probs_out = outs
    seqs, block, width = qg_own.shape[1:]
    heads = width // head
    scale = 1.0 / math.sqrt(head)
    starts = [sum(rows for _, rows in runs[:i]) for i in range(len(runs) + 1)]
    token_rows = early[0].shape[1]
    early_rows = token_rows + early[3].shape[1]
    bounds = (0, token_rows, early_rows, starts[-1])
    late_runs = [run for run, start in zip(runs, starts) if start >= early_rows]
    sent_rows, far_size = starts[-4], runs[-1][1]
    slab = 2 * seqs * heads * far_size

    def score(h, seq):
        at, lanes = seq * heads + h, slice(h * head, (h + 1) * head)
        step = slope[core[0] * heads + h] * LOG2E + 1.0
        raw = dot(stacked(late, 0, seq, lanes), turned[0, at])
        late_scores[at] = with_bias(raw * (scale * LOG2E), late_runs, step)
        late_up[at] = dot(stacked(late, 1, seq, lanes), turned[1, at])

    def normalise(h, seq):
        at = seq * heads + h
        tops = early[2][at, 0:1], early[5][at, 0:1]
        scores = late_scores[at]
        top = jnp.maximum(jnp.maximum(*tops), jnp.max(scores, axis=0, keepdims=True))
        shares = [jnp.exp2(part - top) for part in tops]
        weights = jnp.exp2(scores - top)
        total = early[2][at, 1:2] * shares[0] + early[5][at, 1:2] * shares[1]
        inverse = 1.0 / (total + jnp.sum(weights, axis=0, keepdims=True))
        probs = [early[0][at] * (shares[0] * inverse), early[3][at] * (shares[1] * inverse), weights * inverse]
        upstream = [early[1][at], early[4][at], late_up[at]]
        probs_low = [part.astype(BF16) for part in probs]
        delta = sum(by_eights(p.astype(F32) * u) for p, u in zip(probs_low, upstream))
        delta = jnp.sum(delta, axis=0, keepdims=True)
        slope_sum = jnp.zeros((8, token_rows), F32)
        for p, u, low, high in zip(probs, upstream, bounds, bounds[1:]):
            dscore = p * (u - delta)
            for (level, rows), start in zip(runs, starts):
                if level and low <= start < high:
                    here = dscore[start - low : start - low + rows]
                    slope_sum = slope_sum + by_eights(here) * float(level)
            dscore_out[at, low:high] = dscore.astype(BF16)
        probs_out[at] = jnp.concatenate(probs_low, axis=0)
        return slope_sum

    def gradients(h, seq):
        at, lanes = seq * heads + h, slice(h * head, (h + 1) * head)
        dk = dot(dscore_out[at, sent_rows:], stacked((qg_own, qg_other), 0, seq, lanes)) * scale
        dv = dot(probs_out[at, sent_rows:], stacked((qg_own, qg_other), 1, seq, lanes))
        for kind, direct in enumerate((dk, dv)):
            group = (kind * seqs + seq) * heads + h
            first, direct = direct[:far_size], direct[far_size:]
            across[kind, seq, :, lanes] = direct[:-far_size].astype(BF16)
            relay[pl.ds(group * far_size, far_size), :] = first.astype(BF16)
            relay[pl.ds(slab + group * far_size, far_size), :] = direct[-far_size:].astype(BF16)

    items = [(h, seq) for h in range(heads) for seq in range(seqs)]
    behind = 4
    sums = {}
    for i in range(len(items) + 2 * behind):
        if i < len(items):
            score(*items[i])
        if 0 <= i - behind < len(items):
            item = items[i - behind]
            sums[item] = normalise(*item)
        if 0 <= i - 2 * behind < len(items):
            gradients(*items[i - 2 * behind])
    for h in range(heads):
        slope_out[h : h + 1, :] = jnp.sum(sum(sums[h, seq] for seq in range(seqs)), axis=0, keepdims=True)
    relay[pl.ds(2 * slab, 2 * heads), :] = two_parts(slope_out[...])


def cell_grads_body(head, far_sizes, dscore, probs, qg_own, qg_other, near, side, far):
    seqs, block, width = qg_own.shape[1:]
    heads = width // head
    scale = 1.0 / math.sqrt(head)
    sizes = (block, block // 2, *far_sizes)
    rows = slice(2 * block, 2 * block + sum(sizes))
    for h in range(heads):
        lanes = slice(h * head, (h + 1) * head)
        for seq in range(seqs):
            at = seq * heads + h
            dk = dot(dscore[at, rows], stacked((qg_own, qg_other), 0, seq, lanes)) * scale
            dv = dot(probs[at, rows], stacked((qg_own, qg_other), 1, seq, lanes))
            for kind, direct in enumerate((dk, dv)):
                group = (kind * seqs + seq) * heads + h
                near[kind, seq, :, lanes] = direct[:block]
                start = block + sizes[1]
                side[pl.ds(group * sizes[1], sizes[1]), :] = direct[block:start].astype(BF16)
                slab = 0
                for size in far_sizes:
                    far[pl.ds(slab + group * size, size), :] = direct[start : start + size]
                    start += size
                    slab += 2 * seqs * heads * size


def own_grads_body(head, dscore, probs, qg_own, qg_other, *refs):
    *pieces, dq_own, dq_send, own, other = refs
    seqs, block, width = qg_own.shape[1:]
    heads = width // head
    scale = 1.0 / math.sqrt(head)
    for h in range(heads):
        lanes = slice(h * head, (h + 1) * head)
        for seq in range(seqs):
            at = seq * heads + h
            dq = (dot(dscore[at], stacked(pieces, 0, seq, lanes), 0, 0) * scale).astype(BF16)
            dq_own[seq, :, lanes] = dq[:block]
            dq_send[seq, :, lanes] = dq[block:]
            dk = dot(dscore[at, : 2 * block], stacked((qg_own, qg_other), 0, seq, lanes)) * scale
            dv = dot(probs[at, : 2 * block], stacked((qg_own, qg_other), 1, seq, lanes))
            for kind, direct in enumerate((dk, dv)):
                own[kind, seq, :, lanes] = direct[:block]
                other[kind, seq, :, lanes] = direct[block:]


def fold_body(direct, coarse, done, out):
    rows = direct.shape[2]
    for kind in range(direct.shape[0]):
        for seq in range(direct.shape[1]):
            spread = dot(spread_matrix(rows, 1), coarse[kind, seq])
            out[kind, seq] = (direct[kind, seq] + spread).astype(BF16)


def relay_body(far, back, slope, *refs):
    *slopes, slope_out, keep, message = refs
    rows = keep.shape[0]
    total = slope[...] + one_part(back[pl.ds(2 * rows, 2 * slope.shape[0]), :])
    for ref in slopes:
        total = total + ref[...]
    slope_out[...] = total
    keep[...] = far[pl.ds(0, rows), :] + back[pl.ds(0, rows), :].astype(F32)
    message[pl.ds(0, rows), :] = (far[pl.ds(rows, rows), :] + back[pl.ds(rows, rows), :].astype(F32)).astype(BF16)
    message[pl.ds(rows, 2 * slope.shape[0]), :] = two_parts(total)


def meet_body(keep, back, slope, slope_out, message):
    rows = keep.shape[0]
    total = slope[...] + one_part(back[pl.ds(rows, 2 * slope.shape[0]), :])
    slope_out[...] = total
    message[pl.ds(0, rows), :] = (keep[...] + back[pl.ds(0, rows), :].astype(F32)).astype(BF16)
    message[pl.ds(rows, 2 * slope.shape[0]), :] = two_parts(total)


def gather_body(kind, levels_of, done, own, other, near, *refs):
    back, (kept, sent) = refs[:-2], refs[-2:]
    _, seqs, block, width = own.shape
    sizes = [2 * block >> level for level in levels_of[1:]]
    head = back[0].shape[1]
    spread = jnp.concatenate([spread_matrix(2 * block, level) for level in levels_of], axis=1)
    for seq in range(seqs):
        for h in range(width // head):
            lanes = slice(h * head, (h + 1) * head)
            group = (kind * seqs + seq) * (width // head) + h
            cells = [near[kind, seq, :, lanes]]
            cells += [part[pl.ds(group * size, size), :] for part, size in zip(back, sizes)]
            total = dot(spread, jnp.concatenate(cells, axis=0))
            kept[seq, :, lanes] = (own[kind, seq, :, lanes] + total[:block]).astype(BF16)
            sent[seq, :, lanes] = (other[kind, seq, :, lanes] + total[block:]).astype(BF16)


def total_body(slope, far, out):
    rows = 2 * slope.shape[0]
    out[...] = slope[...] + one_part(far[pl.ds(far.shape[0] - rows, rows), :])


def keep_grads_body(core, dq, dk, dv, *refs):
    *outs, sems = refs
    mine, _ = head_halves(core, dk.shape[-1])
    copy_all([(half, out.at[:, :, mine]) for half, out in zip((dq, dk, dv), outs)], sems)


def join_grads_body(core, dq_half, dk_half, dv_half, dq, dk, dv, slope, slope_other, *refs):
    *outs, slope_out, sums, sems = refs
    _, theirs = head_halves(core, dk.shape[-1])
    moves = [(half, out.at[:, :, theirs]) for half, out in zip((dq, dk, dv), outs)]
    copies = start_all(moves, sems)
    ours, rest = slope[...], slope_other[...]
    lower = jnp.where(core[0] == 0, ours, rest)
    upper = jnp.where(core[0] == 0, rest, ours)
    terms = jnp.concatenate([lower, upper], axis=0)
    sums[...] = jnp.sum(terms.T, axis=0, keepdims=True)
    last = pltpu.make_async_copy(sums, slope_out, sems.at[len(moves)])
    last.start()
    for copy in (*copies, last):
        copy.wait()


def paired(queries, key_rows, value_rows, out_grad, level_slope):
    seqs, block, width = queries.shape
    heads = level_slope.shape[0]
    half, head = width // 2, width // heads
    dp_count = lax.axis_size("dp")
    levels = 4
    position = lax.axis_index("ctx")
    core = (position % 2).astype(jnp.int32).reshape(1)

    part = like(2, seqs, block, half)
    k_other, v_other = swap(key_rows, 1), swap(value_rows, 1)
    cell_shapes = tuple(like(2, seqs, 2 * block >> level, half) for level in range(1, levels))
    wide = (pltpu.VMEM((2, seqs, half // 128, block, 128), F32),)
    own_cells = call(own_summary_body, cell_shapes, (core, key_rows, value_rows), "own_summaries", scalars=1, scratch=wide)
    cells = call(summary_body, cell_shapes, (core, k_other, v_other, *own_cells), "summaries", scalars=1, scratch=wide)
    qg_own, qg_send = call(
        split_body, (part, part), (core, queries, out_grad), "split_qg", scalars=1, hbm_in=2, copies=4
    )
    qg_other = swap(qg_send, 1)

    kv_own, kv_other = call(
        keep_body, (part, part), (core, key_rows, value_rows, k_other, v_other), "keep_halves", scalars=1
    )
    groups = seqs * heads
    far_size = block // 4
    token_rows, cell_rows, late_rows = 2 * block, 2 * block + far_size, block - far_size
    rows = token_rows + cell_rows + late_rows

    turned = call(
        functools.partial(turn_body, head), like(2, groups // 2, head, token_rows), (qg_own, qg_other), "turn"
    )

    def score(levels_of, pieces, count):
        product = like(groups // 2, count, token_rows, dtype=F32)
        return call(
            functools.partial(score_body, levels_of, head),
            (product, product, like(groups // 2, 8, token_rows, dtype=F32)),
            (core, level_slope, turned, *pieces),
            "scores",
            scalars=2,
            flops=40 * seqs * token_rows * count * half,
        )

    token_pieces = [kv_own, kv_other]
    token_scores = score((0, 0), token_pieces, token_rows)

    near_cells = swap(cells[0], 2)
    far_cells = swap(cells[2], 8)
    side_cells = swap(cells[1], 4)
    across = call(coarser_body, like(2, seqs, block // 2, half), (near_cells, token_scores[2]), "coarser")
    across_cells = swap(across, 4)
    far_side_cells = swap(far_cells, 4)
    relayed_cells = [swap(far_cells, 2), swap(far_side_cells, 2)]

    cell_pieces = [near_cells, side_cells, far_cells, far_side_cells, relayed_cells[0]]
    late_pieces = [across_cells, relayed_cells[1]]
    early = (*token_scores, *score((1, 2, 3, 3, 3), cell_pieces, cell_rows))
    runs = ((0, token_rows), (1, block), (2, block // 2), (3, far_size), (3, far_size))
    runs += ((3, far_size), (2, block // 2), (3, far_size))
    far_rows, tail = groups * far_size, heads
    slope_part = like(heads // 2, token_rows, dtype=F32)
    wide = like(*part.shape, dtype=F32)
    slope, across, relay, dscore, probs = call(
        functools.partial(attend_body, runs, head),
        (
            slope_part,
            like(2, seqs, block // 2, half),
            like(2 * far_rows + tail, head),
            like(groups // 2, rows, token_rows),
            like(groups // 2, rows, token_rows),
        ),
        (core, level_slope, *early, turned, qg_own, qg_other, *late_pieces),
        "attend",
        scalars=2,
        flops=40 * seqs * token_rows * rows * half,
        scratch=(
            pltpu.VMEM((groups // 2, late_rows, token_rows), F32),
            pltpu.VMEM((groups // 2, late_rows, token_rows), F32),
        ),
    )
    near, side, far_direct = call(
        functools.partial(cell_grads_body, head, (far_size, far_size)),
        (wide, like(groups * (block // 2), head), like(2 * far_rows, head, dtype=F32)),
        (dscore, probs, qg_own, qg_other),
        "cell_grads",
    )
    dq_part = like(seqs, block, half)
    dq_own, dq_send, own, other = call(
        functools.partial(own_grads_body, head),
        (dq_part, dq_part, wide, wide),
        (dscore, probs, qg_own, qg_other, *token_pieces, *cell_pieces, *late_pieces),
        "own_grads",
        flops=40 * seqs * token_rows * rows * half,
    )

    across_back = swap(across, 4)
    relay_back = swap(relay, 2)
    slopes = [swap(slope, 2 * y, dp) for dp in range(1, dp_count) for y in range(2)]
    dq_other = swap(dq_send, 1)
    message = like(far_rows + tail, head)
    slope, keep, far_side = call(
        relay_body,
        (slope_part, like(far_rows, head, dtype=F32), message),
        (far_direct, relay_back, slope, *slopes),
        "relay",
    )
    far_side_back = swap(far_side, 4)
    near_back = swap(call(fold_body, like(*near.shape), (near, across_back, slope), "fold"), 2)
    side_back = swap(side, 4)
    slope, far_total = call(meet_body, (slope_part, message), (keep, far_side_back, slope), "meet", flops=int(4e9))
    far_back = swap(far_total, 8)
    whole = like(seqs, block, width)
    kept, others = [], []
    for kind in range(2):
        mine, sent = call(
            functools.partial(gather_body, kind, (1, 2, 3)),
            (dq_part, dq_part),
            (dq_other, own, other, near_back, side_back, far_back),
            "gather_cells",
        )
        kept.append(mine)
        others.append(swap(sent, 1))
    slope = call(total_body, slope_part, (slope, far_back), "slope_terms")
    halves = call(
        keep_grads_body, (whole,) * 3, (core, dq_own, *kept), "keep_grads", scalars=1, hbm_out=3, copies=3
    )
    dq, dk, dv, slope_grad = call(
        join_grads_body,
        (whole, whole, whole, like(1, heads, dtype=F32)),
        (core, *halves, dq_other, *others, slope, swap(slope, 1)),
        "join_grads",
        scalars=1,
        hbm_in=3,
        hbm_out=4,
        copies=4,
        scratch=(pltpu.VMEM((1, heads), F32),),
        aliases={1: 0, 2: 1, 3: 2},
    )
    return dq, dk, dv, slope_grad.reshape(heads)


def as_sent(x):
    return jax.tree.map(lambda a: a.astype(jnp.bfloat16) if a.dtype == jnp.float32 else a, x)


def from_partner(value, axis, apart):
    mask = 2**apart
    pairs = [(source, source ^ mask) for source in range(lax.axis_size(axis))]
    return lax.ppermute(value, axis, pairs)


def pair_mean(cells):
    shaped = cells.reshape(cells.shape[:-2] + (cells.shape[-2] // 2, 2, cells.shape[-1])).astype(
        jnp.float32
    )
    return ((shaped[..., 0, :] + shaped[..., 1, :]) * 0.5).astype(jnp.bfloat16)


def merge_level(own_pair, other_pair, flag):
    merged = []
    for own_part, other_part in zip(own_pair, other_pair):
        own_small = pair_mean(own_part)
        other_small = pair_mean(other_part)
        merged.append(
            jnp.where(
                flag == 1,
                jnp.concatenate([other_small, own_small], axis=1),
                jnp.concatenate([own_small, other_small], axis=1),
            )
        )
    return tuple(merged)


def to_heads(rows, heads):
    seqs, count, width = rows.shape
    return jnp.transpose(rows.reshape(seqs, count, heads, width // heads), (0, 2, 1, 3))


def from_heads(split):
    seqs, heads, count, head = split.shape
    return jnp.transpose(split, (0, 2, 1, 3)).reshape(seqs, count, heads * head)


def product(form, left, right):
    return jnp.einsum(form, left, right, preferred_element_type=jnp.float32)


def attend(query_four, key_four, value_four, grad_four, level_slope, block):
    head = query_four.shape[3]
    key_count = key_four.shape[2]
    scale = 1.0 / math.sqrt(head)
    column = jnp.arange(key_count, dtype=jnp.int32)
    level_of = column // block - 1
    sibling = jnp.maximum(level_of, 0)
    multiple = jnp.where(level_of < 0, 1.0, jnp.exp2(sibling.astype(jnp.float32)))
    bias = level_slope[:, None] * sibling.astype(jnp.float32)[None, :]
    raw = product("shqd,shkd->shqk", query_four, key_four)
    scores = raw * scale + bias[None, :, None, :]
    top = jnp.max(scores, axis=-1, keepdims=True)
    weights = multiple[None, None, None, :] * jnp.exp(scores - top)
    probs = weights / jnp.sum(weights, axis=-1, keepdims=True)
    probs_low = probs.astype(jnp.bfloat16)
    output = product("shqk,shkd->shqd", probs_low, value_four)
    delta = jnp.sum(grad_four.astype(jnp.float32) * output, axis=-1)
    upstream = product("shqd,shkd->shqk", grad_four, value_four)
    dscore = probs * (upstream - delta[..., None])
    slope_part = jnp.sum(dscore * sibling.astype(jnp.float32)[None, None, None, :], axis=(0, 2, 3))
    dscore_low = dscore.astype(jnp.bfloat16)
    query_part = product("shqk,shkd->shqd", dscore_low, key_four) * scale
    key_part = product("shqk,shqd->shkd", dscore_low, query_four) * scale
    value_part = product("shqk,shqd->shkd", probs_low, grad_four)
    return (query_part, key_part, value_part, slope_part)


def split_level(grad_now, direct, flag, level, block):
    half = block // 2
    lower_src = grad_now[:, :, :half]
    upper_src = grad_now[:, :, half:]
    own_src = jnp.where(flag == 1, upper_src, lower_src)
    other_src = jnp.where(flag == 1, lower_src, upper_src)
    own_half = jnp.repeat(own_src, 2, axis=2) * 0.5
    other_half = jnp.repeat(other_src, 2, axis=2) * 0.5
    sent = (other_half + direct[:, :, (level + 1) * block : (level + 2) * block]).astype(
        jnp.bfloat16
    )
    return (own_half, sent)


def by_blocks(queries, key_rows, value_rows, out_grad, level_slope):
    seqs, block, width = queries.shape
    heads = level_slope.shape[0]
    ctx_count = lax.axis_size("ctx")
    levels = ctx_count.bit_length() - 1
    position = lax.axis_index("ctx")
    bit_list = [position // 2**level % 2 for level in range(levels)]
    own_pair = (key_rows, value_rows)
    partners = []
    for level in range(levels - 2):
        other_pair = jax.tree.map(
            lambda part, own: part.astype(own.dtype),
            from_partner(as_sent(own_pair), "ctx", level),
            own_pair,
        )
        partners.append(other_pair)
        own_pair = merge_level(own_pair, other_pair, bit_list[level])
    for level in range(levels - 2, levels):
        other_pair = jax.tree.map(
            lambda part, own: part.astype(own.dtype),
            from_partner(as_sent(own_pair), "ctx", level),
            own_pair,
        )
        partners.append(other_pair)
        if level + 1 < levels:
            own_pair = merge_level(own_pair, other_pair, bit_list[level])
    key_set = jnp.concatenate(
        [to_heads(key_rows, heads)] + [to_heads(pair[0], heads) for pair in partners], axis=2
    )
    value_set = jnp.concatenate(
        [to_heads(value_rows, heads)] + [to_heads(pair[1], heads) for pair in partners], axis=2
    )
    query_four = to_heads(queries, heads)
    grad_four = to_heads(out_grad, heads)
    query_part, key_part, value_part, slope_part = attend(
        query_four, key_set, value_set, grad_four, level_slope, block
    )
    slope_grad = lax.psum(slope_part, ("dp", "ctx"))
    head = width // heads
    grad_keys = jnp.zeros((seqs, heads, block, head), jnp.float32)
    grad_values = jnp.zeros((seqs, heads, block, head), jnp.float32)
    for level in reversed(range(levels)):
        own_keys, sent_keys = split_level(grad_keys, key_part, bit_list[level], level, block)
        own_values, sent_values = split_level(
            grad_values, value_part, bit_list[level], level, block
        )
        back_keys, back_values = from_partner((sent_keys, sent_values), "ctx", level)
        grad_keys = own_keys + back_keys.astype(jnp.float32)
        grad_values = own_values + back_values.astype(jnp.float32)
    key_grad = from_heads((grad_keys + key_part[:, :, :block]).astype(jnp.bfloat16))
    value_grad = from_heads((grad_values + value_part[:, :, :block]).astype(jnp.bfloat16))
    return (from_heads(query_part.astype(jnp.bfloat16)), key_grad, value_grad, slope_grad)


def shards(queries, key_rows, value_rows, out_grad, level_slope):
    heads, width = level_slope.shape[0], queries.shape[2]
    tiles = queries.shape[1] % 64 == 0 and heads % 16 == 0 and width // heads % 128 == 0
    few = lax.axis_size("ctx") == 16 and tiles
    form = paired if few else by_blocks
    return form(queries, key_rows, value_rows, out_grad, level_slope)


def solution(mesh):
    placed = (
        P("dp", "ctx", None),
        P("dp", "ctx", None),
        P("dp", "ctx", None),
        P("dp", "ctx", None),
        P(),
    )
    return jax.shard_map(
        shards,
        mesh=mesh,
        in_specs=placed,
        out_specs=(P("dp", "ctx", None), P("dp", "ctx", None), P("dp", "ctx", None), P()),
        check_vma=False,
    )
```
